32 devices in a mesh: blk: 16 (over z, y, x), rep: 2 (over core).
Axes of the slice: x: 2, y: 2, z: 4, core: 2. Of those that a mesh axis runs over, the one named last changes fastest.
Arguments:
- node_feat: bfloat16 [8192, 256], P(('blk', 'rep')), may hold values from -6 to 6
- edge_feat: bfloat16 [8192, 8, 256], P(('blk', 'rep')), may hold values from -6 to 6
- edge_step: int32 [8192, 8], P(('blk', 'rep')), may hold values from -256 to 256
- degree: int32 [8192], P(('blk', 'rep')), may hold values from 1 to 8
- graph_len: int32 [9], replicated, may hold values from 2 to 8088, as said below
- gine_w1: bfloat16 [256, 256], replicated, may hold values from -0.375 to 0.375
- gine_b1: float32 [256], replicated, may hold values from -6 to 6
- gine_w2: bfloat16 [256, 256], replicated, may hold values from -0.375 to 0.375
- query_w: bfloat16 [256, 256], replicated, may hold values from -0.625 to 0.625
- key_w: bfloat16 [256, 256], replicated, may hold values from -0.625 to 0.625
- value_w: bfloat16 [256, 256], replicated, may hold values from -0.375 to 0.375
- out_w: bfloat16 [256, 256], replicated, may hold values from -1.5 to 1.5
- ffn_w1: bfloat16 [256, 512], replicated, may hold values from -0.375 to 0.375
- ffn_b1: float32 [512], replicated, may hold values from -6 to 6
- ffn_w2: bfloat16 [512, 256], replicated, may hold values from -0.25 to 0.25
- norm1_gain: float32 [256], replicated, may hold values from 0.25 to 1.75
- norm2_gain: float32 [256], replicated, may hold values from 0.25 to 1.75
- norm2_bias: float32 [256], replicated, may hold values from -3 to 3
- norm3_gain: float32 [256], replicated, may hold values from 0.25 to 1.75
- norm3_bias: float32 [256], replicated, may hold values from -3 to 3
- out_grad: bfloat16 [8192, 256], P(('blk', 'rep')), may hold values from -6 to 6
Outputs:
- output: bfloat16 [8192, 256], P(('blk', 'rep'))
- node_grad: float32 [8192, 256], P(('blk', 'rep'))
- gine_w1_grad: float32 [256, 256], replicated
- gine_b1_grad: float32 [256], replicated
- gine_w2_grad: float32 [256, 256], replicated
- query_w_grad: float32 [256, 256], replicated
- key_w_grad: float32 [256, 256], replicated
- value_w_grad: float32 [256, 256], replicated
- out_w_grad: float32 [256, 256], replicated
- ffn_w1_grad: float32 [256, 512], replicated
- ffn_b1_grad: float32 [512], replicated
- ffn_w2_grad: float32 [512, 256], replicated
- norm1_gain_grad: float32 [256], replicated
- norm2_gain_grad: float32 [256], replicated
- norm2_bias_grad: float32 [256], replicated
- norm3_gain_grad: float32 [256], replicated
- norm3_bias_grad: float32 [256], replicated
The draws below stay inside these ranges and needn't reach their ends.
Inputs may be any that keep to these rules, and one draw needn't show every extreme that they name: Slot k of node i takes as source the node i + edge_step[i, k], clipped into the nodes of i's own graph. Slots 0 to degree - 1 of a node are its edges, the other slots are padding. `graph_len`: the graphs lie in node order one after another and their lengths sum to 8192; all but one hold 2 to 24 nodes, one of them exactly 2, and these small ones together hold 104 nodes; the remaining graph holds all other nodes.
All inputs are finite; a program needn't handle non-finite values.
Results may differ from the reference program's by a relative error of at most 0.02125.
The reference program's roundings to bfloat16 on the way count: a program that leaves them out, or rounds other values in their place, can miss the bound.
Values may be sent and summed in bfloat16 or wider, within the bound.
A program may use at most 192 MiB of HBM per device.

```python
import math
import jax
import jax.numpy as jnp
from jax import lax

D = 256
HEADS = 8
HDIM = 32
FF = 512
NODE_DEV = 256
EDGES = 8
MOLS = 8
MOL_MAX = 24
NODES = 8192


def draw_graph_len(key, part):
    key = jax.random.fold_in(key, 5)
    first_key, second_key, third_key = jax.random.split(key, 3)
    halves = jax.random.randint(first_key, (MOLS // 2,), 2, MOL_MAX + 1)
    halves = jnp.where(jnp.arange(MOLS // 2) == 0, 2, halves)
    partners = MOL_MAX + 2 - halves
    molecules = jax.random.permutation(third_key, jnp.concatenate([halves, partners]))
    spot = jax.random.randint(second_key, (), 0, MOLS + 1)
    largest = NODES - MOLS * (MOL_MAX + 2) // 2
    places = jnp.arange(MOLS + 1)
    before_spot = molecules[jnp.clip(places, 0, MOLS - 1)]
    after_spot = molecules[jnp.clip(places - 1, 0, MOLS - 1)]
    lengths = jnp.where(places < spot, before_spot, jnp.where(places == spot, largest, after_spot))
    return lengths.astype(jnp.int32)


def with_ends(values, own_key, smallest, top_value):
    longest = values.shape.index(max(values.shape))
    spots = []
    for shift in (0, 1):
        where = [jax.random.randint(jax.random.fold_in(own_key, axis), (), 0, length) for axis, length in enumerate(values.shape)]
        where[longest] = (where[longest] + shift) % values.shape[longest]
        spots.append(tuple(where))
    return values.at[spots[0]].set(smallest).at[spots[1]].set(top_value)


def block_scale(stream_key, shape, cuts, smallest, top_value):
    def one(dim, blocks):
        heights = jax.random.uniform(jax.random.fold_in(jax.random.fold_in(stream_key, 6), dim), (blocks,), jnp.float32, smallest / len(cuts), top_value / len(cuts))
        return jnp.repeat(jnp.exp(heights), shape[dim] // blocks).reshape((-1,) + (1,) * (len(shape) - dim - 1))

    gain = one(*cuts[0])
    for cut in cuts[1:]:
        gain = gain * one(*cut)
    return gain


def gaussian(stream_key, dims, width, bound, cuts=(), kind=jnp.bfloat16):
    array = jax.random.normal(stream_key, dims, jnp.float32) * width
    if len(cuts) > 0:
        array = block_scale(stream_key, dims, cuts, -0.22, 0.18) * array
    return jnp.clip(array, min=-bound, max=bound).astype(kind)


def setup_inputs(seed: int = 0) -> dict:
    streams_of = jax.random.split(jax.random.key(seed), 22)
    return {
        "node_feat": gaussian(streams_of[0], (NODES, D), 1.0, 6.0, ((0, 32),)),
        "edge_feat": gaussian(streams_of[1], (NODES, EDGES, D), 1.0, 6.0, ((0, 32),)),
        "edge_step": with_ends(jax.random.randint(streams_of[2], (NODES, EDGES), 0 - NODE_DEV, NODE_DEV + 1), jax.random.fold_in(streams_of[2], 1), 0 - NODE_DEV, NODE_DEV).astype(jnp.int32),
        "degree": with_ends(jax.random.randint(streams_of[3], (NODES,), 1, EDGES + 1), jax.random.fold_in(streams_of[3], 1), 1, EDGES).astype(jnp.int32),
        "graph_len": draw_graph_len(jax.random.fold_in(streams_of[21], 71), 0),
        "gine_w1": gaussian(streams_of[5], (D, D), D ** -0.5, 0.375),
        "gine_b1": gaussian(streams_of[6], (D,), 1.0, 6.0, (), jnp.float32),
        "gine_w2": gaussian(streams_of[7], (D, D), D ** -0.5, 0.375),
        "query_w": gaussian(streams_of[8], (D, D), (D * 2 // 5) ** -0.5, 0.625),
        "key_w": gaussian(streams_of[9], (D, D), (D * 2 // 5) ** -0.5, 0.625),
        "value_w": gaussian(streams_of[10], (D, D), D ** -0.5, 0.375),
        "out_w": gaussian(streams_of[11], (D, D), (D // 16) ** -0.5, 1.5),
        "ffn_w1": gaussian(streams_of[12], (D, FF), D ** -0.5, 0.375),
        "ffn_b1": gaussian(streams_of[13], (FF,), 1.0, 6.0, (), jnp.float32),
        "ffn_w2": gaussian(streams_of[14], (FF, D), FF ** -0.5, 0.25),
        "norm1_gain": jnp.clip(1.0 + 0.15 * jax.random.normal(streams_of[15], (D,), jnp.float32), 0.25, 1.75),
        "norm2_gain": jnp.clip(1.0 + 0.15 * jax.random.normal(streams_of[16], (D,), jnp.float32), 0.25, 1.75),
        "norm2_bias": gaussian(streams_of[17], (D,), 0.5, 3.0, (), jnp.float32),
        "norm3_gain": jnp.clip(1.0 + 0.15 * jax.random.normal(streams_of[18], (D,), jnp.float32), 0.25, 1.75),
        "norm3_bias": gaussian(streams_of[19], (D,), 0.5, 3.0, (), jnp.float32),
        "out_grad": gaussian(streams_of[20], (NODES, D), 1.0, 6.0, ((0, 32),)),
    }


norm_eps = 1e-05
masked_score = -1e+30

@jax.custom_vjp
def low(v):
    return lax.optimization_barrier(v.astype(jnp.bfloat16)).astype(jnp.float32)

@jax.custom_vjp
def low_back(v):
    return v

def low_keep(v):
    return (low(v), None)

def low_pass(kept, grad):
    return (grad,)

def back_keep(v):
    return (v, None)

def back_low(kept, grad):
    return (low(grad),)
low.defvjp(low_keep, low_pass)
low_back.defvjp(back_keep, back_low)

def matmul(left, right):
    return jnp.dot(left, right, precision=lax.Precision.HIGHEST)

def batch_norm(residual, gain_vec, bias_vec):
    col_mean = lax.optimization_barrier(jnp.mean(residual, axis=0))
    centered = residual - col_mean
    col_var = lax.optimization_barrier(jnp.mean(centered * centered, axis=0))
    return gain_vec * centered * lax.rsqrt(col_var + norm_eps) + bias_vec

def attention(queries, key_rows, value_rows, graph_ids):
    block_rows = math.gcd(NODES, 512)
    block_count = NODES // block_rows
    key_heads = key_rows.reshape(NODES, HEADS, HDIM)
    value_heads = value_rows.reshape(NODES, HEADS, HDIM)
    query_blocks = queries.reshape(block_count, block_rows, HEADS, HDIM)
    id_blocks = graph_ids.reshape(block_count, block_rows)

    def one_block(block_pair):
        query_part, id_part = block_pair
        raw_scores = low_back(jnp.einsum('qhd,khd->hqk', query_part, key_heads, precision=lax.Precision.HIGHEST))
        allowed = (id_part[:, None] == graph_ids[None, :])[None]
        scores = jnp.where(allowed, raw_scores * HDIM ** (-0.5), masked_score)
        row_top = lax.optimization_barrier(jnp.max(scores, axis=2, keepdims=True))
        weights = jnp.where(allowed, jnp.exp(scores - row_top), 0.0)
        totals = lax.optimization_barrier(jnp.sum(weights, axis=2))
        mixed_rows = jnp.einsum('hqk,khd->qhd', low(weights), value_heads, precision=lax.Precision.HIGHEST)
        return mixed_rows / totals.T[:, :, None]
    result_blocks = lax.map(jax.checkpoint(one_block), (query_blocks, id_blocks))
    return result_blocks.reshape(NODES, D)

def gps_layer(node_rows, gine_w1, gine_b1, gine_w2, query_w, key_w, value_w, out_w, ffn_w1, ffn_b1, ffn_w2, norm1_gain, norm2_gain, norm2_bias, norm3_gain, norm3_bias, edge_rows, sources, present, graph_ids):
    picked = low_back(node_rows[sources])
    message = lax.optimization_barrier(jnp.sum(jnp.where(present[:, :, None], jax.nn.gelu(picked + edge_rows), 0.0), axis=1))
    mixed_in = low(node_rows + message)
    hidden_one = low_back(matmul(mixed_in, gine_w1) + gine_b1)
    local_out = low_back(matmul(low(jax.nn.gelu(hidden_one)), gine_w2))
    first_norm = batch_norm(node_rows + local_out, norm1_gain, 0.0)
    queries = low(low_back(matmul(node_rows, query_w)))
    key_rows = low(low_back(matmul(node_rows, key_w)))
    value_rows = low(low_back(matmul(node_rows, value_w)))
    attended = low(low_back(attention(queries, key_rows, value_rows, graph_ids)))
    global_out = low_back(matmul(attended, out_w))
    second_norm = batch_norm(node_rows + global_out, norm2_gain, norm2_bias)
    summed = first_norm + second_norm
    ffn_hidden = low_back(matmul(low(summed), ffn_w1) + ffn_b1)
    ffn_out = low_back(matmul(low(jax.nn.gelu(ffn_hidden)), ffn_w2))
    return batch_norm(summed + ffn_out, norm3_gain, norm3_bias)

def reference(node_feat, edge_feat, edge_step, degree, graph_len, gine_w1, gine_b1, gine_w2, query_w, key_w, value_w, out_w, ffn_w1, ffn_b1, ffn_w2, norm1_gain, norm2_gain, norm2_bias, norm3_gain, norm3_bias, out_grad):
    positions = jnp.arange(NODES, dtype=jnp.int32)
    graph_ends = jnp.cumsum(graph_len).astype(jnp.int32)
    ended_by = graph_ends[None, :] <= positions[:, None]
    graph_ids = lax.optimization_barrier(jnp.sum(ended_by, axis=1)).astype(jnp.int32)
    starts = lax.optimization_barrier(jnp.max(jnp.where(ended_by, graph_ends[None, :], 0), axis=1)).astype(jnp.int32)
    graph_stop = lax.optimization_barrier(jnp.min(jnp.where(ended_by, NODES, graph_ends[None, :]), axis=1)).astype(jnp.int32)
    sources = jnp.clip(positions[:, None] + edge_step, starts[:, None], graph_stop[:, None] - 1).astype(jnp.int32)
    present = jnp.arange(EDGES, dtype=jnp.int32)[None, :] < degree[:, None]
    edge_rows = edge_feat.astype(jnp.float32)
    floats = (node_feat.astype(jnp.float32), gine_w1.astype(jnp.float32), gine_b1.astype(jnp.float32), gine_w2.astype(jnp.float32), query_w.astype(jnp.float32), key_w.astype(jnp.float32), value_w.astype(jnp.float32), out_w.astype(jnp.float32), ffn_w1.astype(jnp.float32), ffn_b1.astype(jnp.float32), ffn_w2.astype(jnp.float32), norm1_gain.astype(jnp.float32), norm2_gain.astype(jnp.float32), norm2_bias.astype(jnp.float32), norm3_gain.astype(jnp.float32), norm3_bias.astype(jnp.float32))

    def forward(node_rows, w_one, b_one, w_two, w_query, w_key, w_value, w_out, w_ffn1, b_ffn1, w_ffn2, gain_one, gain_two, bias_two, gain_three, bias_three):
        return gps_layer(node_rows, w_one, b_one, w_two, w_query, w_key, w_value, w_out, w_ffn1, b_ffn1, w_ffn2, gain_one, gain_two, bias_two, gain_three, bias_three, edge_rows, sources, present, graph_ids)
    result, pullback = jax.vjp(forward, *floats)
    grads = pullback(out_grad.astype(jnp.float32))
    return (result.astype(jnp.bfloat16), grads[0], grads[1], grads[2], grads[3], grads[4], grads[5], grads[6], grads[7], grads[8], grads[9], grads[10], grads[11], grads[12], grads[13], grads[14], grads[15])
```

```python
import functools
import jax
import jax.numpy as jnp
from jax import lax
from jax.experimental import pallas as pl
from jax.experimental.pallas import tpu as pltpu
from jax.sharding import PartitionSpec as P

HEADS = 8
HDIM = 32
EDGES = 8
GRAPHS = 9
AXES = ("blk", "rep")
MESH = pl.DeviceIdType.MESH
bf16 = jnp.bfloat16
f32 = jnp.float32

norm_eps = 1e-05
far_score = -1e30
log2_e = 1.4426950408889634
score_scale = HDIM ** (-0.5)
gelu_c = 0.7978845608028654
gelu_a = 0.044715


def dot(left, right, left_dim=1, right_dim=0):
    return lax.dot_general(
        left, right, (((left_dim,), (right_dim,)), ((), ())), preferred_element_type=f32
    )


def gelu(v):
    return 0.5 * v * (1.0 + jnp.tanh(gelu_c * (v + gelu_a * (v * v * v))))


def gelu_slope(v):
    squared = v * v
    bend = jnp.tanh(gelu_c * v * (1.0 + gelu_a * squared))
    return 0.5 * (1.0 + bend) + 0.5 * v * (1.0 - bend * bend) * (
        gelu_c * (1.0 + 3.0 * gelu_a * squared)
    )


def three_parts(v):
    first = v.astype(bf16)
    rest = v - first.astype(f32)
    second = rest.astype(bf16)
    third = (rest - second.astype(f32)).astype(bf16)
    return first, second, third


class Place:
    def __init__(self, count, cores):
        self.count = count
        self.cores = cores
        self.planes = count // HEADS
        self.me = lax.axis_index("blk") * cores + lax.axis_index("rep")
        self.z = lax.div(self.me, HEADS)
        self.p = lax.rem(self.me, HEADS)

    def device(self, index):
        return {"blk": lax.div(index, self.cores), "rep": lax.rem(index, self.cores)}

    def in_plane(self, k):
        return self.z * HEADS + lax.rem(self.p + k, HEADS)

    def along(self, k):
        return lax.rem(self.me + HEADS * k, self.count)

    def mirrored(self, k):
        peer, bit = 0, 1
        while bit < self.count:
            mine = lax.rem(lax.div(self.me, bit), 2)
            flip = lax.rem(lax.div(k, bit), 2)
            peer = peer + bit * (mine + flip - 2 * mine * flip)
            bit *= 2
        return peer

    def greet(self, peers):
        barrier = pltpu.get_barrier_semaphore()
        for peer in peers:
            pl.semaphore_signal(barrier, inc=1, device_id=self.device(peer), device_id_type=MESH)
        pl.semaphore_wait(barrier, len(peers))

    def greet_all(self):
        barrier = pltpu.get_barrier_semaphore()

        def hello(k, _):
            pl.semaphore_signal(
                barrier, inc=1, device_id=self.device(self.mirrored(k)), device_id_type=MESH
            )
            return 0

        lax.fori_loop(1, self.count, hello, 0)
        pl.semaphore_wait(barrier, self.count - 1)

    def copy(self, src, dst, send_sem, recv_sem, peer):
        return pltpu.make_async_remote_copy(
            src_ref=src,
            dst_ref=dst,
            send_sem=send_sem,
            recv_sem=recv_sem,
            device_id=self.device(peer),
            device_id_type=MESH,
        )


def graph_bounds(len_ref, positions):
    last = 0
    graph = jnp.zeros(positions.shape, jnp.int32)
    start = jnp.zeros(positions.shape, jnp.int32)
    ends = []
    for g in range(GRAPHS):
        last = last + len_ref[g]
        ends.append(last)
        passed = positions >= last
        graph = graph + passed.astype(jnp.int32)
        start = jnp.where(passed, last, start)
    stop = jnp.full(positions.shape, ends[-1], jnp.int32)
    for end in reversed(ends):
        stop = jnp.where(positions < end, end, stop)
    return graph, start, stop


def own_graph(len_ref, first, width):
    positions = first + lax.broadcasted_iota(jnp.int32, (1, width), 1)
    graph, _, _ = graph_bounds(len_ref, positions)
    rows = lax.broadcasted_iota(jnp.int32, (16, width), 0)
    return rows == graph


def edge_places(place, len_ref, step_ref, rows):
    positions = place.me * rows + lax.broadcasted_iota(jnp.int32, (rows, 1), 0)
    _, start, stop = graph_bounds(len_ref, positions)
    source = jnp.minimum(jnp.maximum(positions + step_ref[...], start), stop - 1)
    return source - place.me * rows + rows


def as_column(row, width):
    return jnp.broadcast_to(row, (128, width)).T


def project_kernel(
    count,
    cores,
    len_ref,
    x_ref,
    wq_ref,
    wk_ref,
    wv_ref,
    step_ref,
    degree_ref,
    edge_ref,
    w1_ref,
    b1_ref,
    w2_ref,
    q_out,
    kv_out,
    mixed_out,
    hidden_out,
    res_out,
    slope_out,
    ext,
    q_send,
    kv_send,
    halo_ss,
    halo_rs,
    a2a_ss,
    a2a_rs,
    z_ss,
    z_rs,
):
    place = Place(count, cores)
    rows = x_ref.shape[0]
    planes = place.planes
    after = lax.rem(place.me + 1, count)
    before = lax.rem(place.me + count - 1, count)
    place.greet(
        [after, before]
        + [place.in_plane(k) for k in range(1, HEADS)]
        + [place.along(k) for k in range(1, planes)]
    )
    x = x_ref[...]
    ext[rows : 2 * rows, :] = x
    up = place.copy(x_ref, ext.at[pl.ds(0, rows)], halo_ss.at[0], halo_rs.at[0], after)
    down = place.copy(x_ref, ext.at[pl.ds(2 * rows, rows)], halo_ss.at[1], halo_rs.at[1], before)
    xt = x.T
    for h in range(HEADS):
        cols = slice(HDIM * h, HDIM * (h + 1))
    kt = dot(wk_ref[...].T, xt).astype(bf16)
    vt = dot(wv_ref[...].T, xt).astype(bf16)
    qt = dot(wq_ref[...].T, xt).astype(bf16)
    for h in range(HEADS):
        cols = slice(HDIM * h, HDIM * (h + 1))
        kv_send[h, 0:HDIM] = kt[cols]
        kv_send[h, HDIM : 2 * HDIM] = vt[cols]
        q_send[h] = qt[cols]
    kv_copies = []
    q_copies = []
    for k in range(1, HEADS):
        peer = place.in_plane(k)
        spot = lax.rem(place.p + k, HEADS)
        c = place.copy(
            kv_send.at[spot], kv_out.at[place.me], a2a_ss.at[0, k], a2a_rs.at[0, k], peer
        )
        c.start()
        kv_copies.append(c)
    for k in range(1, HEADS):
        peer = place.in_plane(k)
        spot = lax.rem(place.p + k, HEADS)
        c = place.copy(q_send.at[spot], q_out.at[place.p], a2a_ss.at[1, k], a2a_rs.at[1, k], peer)
        c.start()
        q_copies.append(c)
    up.start()
    down.start()
    kv_out[place.me] = kv_send[place.p]
    q_out[place.p] = q_send[place.p]
    for c in kv_copies:
        c.wait()
    own = pl.ds(place.z * HEADS, HEADS)
    z_copies = []
    for k in range(1, planes):
        c = place.copy(kv_out.at[own], kv_out.at[own], z_ss.at[k], z_rs.at[k], place.along(k))
        c.start()
        z_copies.append(c)
    for c in q_copies:
        c.wait()
    up.wait()
    down.wait()
    source = edge_places(place, len_ref, step_ref, rows)
    degree = as_column(degree_ref[...], rows)
    cells = lax.broadcasted_iota(jnp.int32, (rows, 3 * rows), 1)
    message = jnp.zeros(x.shape, f32)
    around = ext[...]
    for k in range(EDGES):
        select = (source[:, k : k + 1] == cells).astype(f32).astype(bf16)
        v = dot(select, around) + edge_ref[:, k, :].astype(f32)
        present = degree[:, 0:1] > k
        message = message + jnp.where(present, gelu(v), 0.0)
        slope_out[k] = jnp.where(present, gelu_slope(v), 0.0)
    mixed = (x.astype(f32) + message).astype(bf16)
    mixed_out[...] = mixed
    hidden = dot(mixed, w1_ref[...]) + b1_ref[...]
    hidden_out[...] = hidden
    res_out[...] = x.astype(f32) + dot(gelu(hidden).astype(bf16), w2_ref[...])
    for c in z_copies:
        c.wait()


def build_keys(len_ref, kv_ref, keys, cols, block):
    kt = kv_ref[block, 0:HDIM]
    same = own_graph(len_ref, block * cols, cols).astype(f32).astype(bf16)
    ones = jnp.ones((16, cols), bf16)
    keys[pl.ds(pl.multiple_of(block * cols, cols), cols), :] = jnp.concatenate(
        [kt, kt, kt, same, ones], axis=0
    ).T


def build_queries(len_ref, q_ref, queries, cols, block, first, last_rows):
    parts = three_parts(q_ref[block].astype(f32) * (score_scale * log2_e))
    same = own_graph(len_ref, first + block * cols, cols)
    known = lax.broadcasted_iota(jnp.int32, (16, cols), 0) < GRAPHS
    mask = jnp.where(jnp.logical_or(same, jnp.logical_not(known)), 0.0, far_score).astype(bf16)
    queries[:, pl.ds(pl.multiple_of(block * cols, cols), cols)] = jnp.concatenate(
        list(parts) + [mask, last_rows], axis=0
    )


def attend_kernel(
    count,
    cores,
    key_tile,
    query_tile,
    len_ref,
    q_ref,
    kv_ref,
    att_out,
    log_out,
    keys,
    values,
    queries,
    total,
    top,
):
    place = Place(count, cores)
    cols = q_ref.shape[2]
    width = HEADS * cols
    key_count = count * cols
    first = place.z * width

    def prepare_key(b, _):
        build_keys(len_ref, kv_ref, keys, cols, b)
        values[:, pl.ds(pl.multiple_of(b * cols, cols), cols)] = jnp.concatenate(
            [kv_ref[b, HDIM : 2 * HDIM], jnp.ones((16, cols), bf16)], axis=0
        )
        return 0

    def prepare_query(b, _):
        build_queries(
            len_ref, q_ref, queries, cols, b, first, jnp.zeros((16, cols), bf16)
        )
        return 0

    lax.fori_loop(0, count, prepare_key, 0)
    lax.fori_loop(0, HEADS, prepare_query, 0)
    total[...] = jnp.zeros_like(total)

    def key_step(j, _):
        ks = pl.ds(pl.multiple_of(j * key_tile, key_tile), key_tile)
        key_part = keys[ks, :]
        value_part = values[:, ks]

        def query_step(i, _):
            qs = pl.ds(pl.multiple_of(i * query_tile, query_tile), query_tile)
            weights = jnp.exp2(dot(key_part, queries[:, qs])).astype(bf16)
            total[:, qs] += dot(value_part, weights)
            return 0

        lax.fori_loop(0, width // query_tile, query_step, 0, unroll=True)
        return 0

    lax.fori_loop(0, key_count // key_tile, key_step, 0)
    top[...] = jnp.zeros_like(top)
    sums = total[HDIM : HDIM + 1, :]
    fine = jnp.logical_and(sums > 2.0**-60, sums < 2.0**120)
    faulty = jnp.max(jnp.where(fine, 0.0, 1.0)) > 0.5

    @pl.when(faulty)
    def with_running_top():
        tile = 256

        def query_step(i, _):
            qs = pl.ds(pl.multiple_of(i * tile, tile), tile)
            query_part = queries[:, qs]

            def key_step(j, state):
                top_prev, total_prev = state
                ks = pl.ds(pl.multiple_of(j * tile, tile), tile)
                scores = dot(keys[ks, :], query_part)
                top_next = jnp.maximum(top_prev, jnp.max(scores, axis=0, keepdims=True))
                weights = jnp.exp2(scores - top_next).astype(bf16)
                return top_next, total_prev * jnp.exp2(top_prev - top_next) + dot(
                    values[:, ks], weights
                )

            state = (jnp.full((1, tile), 2.0 * far_score, f32), jnp.zeros((HDIM + 16, tile), f32))
            top_last, total_last = lax.fori_loop(0, key_count // tile, key_step, state)
            top[0:1, qs] = top_last
            total[:, qs] = total_last
            return 0

        lax.fori_loop(0, width // tile, query_step, 0)

    sums = total[HDIM : HDIM + 1, :]
    log_out[...] = jnp.broadcast_to(top[0:1, :] + jnp.log2(sums), log_out.shape)
    att_out[...] = total[0:HDIM, :] / sums


def share_stats(place, stats, buffer, send_sems, recv_sems):
    buffer[place.me] = stats

    def begin(k, _):
        far = place.count - 1 - k
        place.copy(
            buffer.at[place.me],
            buffer.at[place.me],
            send_sems.at[far],
            recv_sems.at[far],
            place.mirrored(far),
        ).start()
        return 0

    def finish(k, _):
        peer = place.mirrored(k)
        c = place.copy(
            buffer.at[place.me], buffer.at[peer], send_sems.at[k], recv_sems.at[k], peer
        )
        c.wait()
        return 0

    lax.fori_loop(0, place.count - 1, begin, 0, unroll=place.count <= 32)
    lax.fori_loop(1, place.count, finish, 0, unroll=place.count <= 32)
    return buffer[...]


def col_sum(v):
    return jnp.sum(v, axis=0, keepdims=True)


def stack_rows(rows, width):
    return jnp.concatenate(rows + [jnp.zeros((8 - len(rows), width), f32)], axis=0)


def norms_kernel(
    count,
    cores,
    x_ref,
    res_ref,
    att_ref,
    up_ref,
    out_w_ref,
    f1_ref,
    fb_ref,
    f2_ref,
    g1_ref,
    g2_ref,
    b2_ref,
    g3_ref,
    b3_ref,
    mixed_ref,
    hidden_ref,
    slope_ref,
    len_ref,
    step_ref,
    w1_ref,
    w2_ref,
    result_out,
    grad_out,
    do_out,
    vec_out,
    f1_out,
    f2_out,
    ow_out,
    gw1_out,
    gw2_out,
    att_send,
    att_got,
    do_send,
    edge_send,
    edge_got,
    stat0,
    stat1,
    stat2,
    att_ss,
    att_rs,
    stat_ss,
    stat_rs,
    do_ss,
    do_rs,
    halo_ss,
    halo_rs,
):
    place = Place(count, cores)
    rows, width = x_ref.shape
    total_rows = rows * count
    place.greet_all()
    x = x_ref[...].astype(f32)

    for b in range(HEADS):
        att_send[b] = att_ref[:, b * rows : (b + 1) * rows].astype(bf16)
    copies = []
    for k in range(1, HEADS):
        spot = lax.rem(place.p + k, HEADS)
        c = place.copy(
            att_send.at[spot], att_got.at[place.p], att_ss.at[k], att_rs.at[k], place.in_plane(k)
        )
        c.start()
        copies.append(c)
    att_got[place.p] = att_send[place.p]
    for c in copies:
        c.wait()
    att_half = jnp.concatenate([att_got[h] for h in range(HEADS)], axis=0)
    global_out = dot(att_half.T, out_w_ref[...])
    res_one = res_ref[...]
    res_two = x + global_out

    def centre(v):
        mean = col_sum(v) / rows
        off = v - mean
        return mean, col_sum(off * off)

    def combine(means, squares):
        mean = jnp.sum(means, axis=0, keepdims=True) / count
        off = means - mean
        var = (
            jnp.sum(squares, axis=0, keepdims=True)
            + rows * jnp.sum(off * off, axis=0, keepdims=True)
        ) / total_rows
        return mean, lax.rsqrt(var + norm_eps)

    stats = share_stats(
        place,
        stack_rows([*centre(res_one), *centre(res_two)], width),
        stat0,
        stat_ss.at[0],
        stat_rs.at[0],
    )
    mean_one, inv_one = combine(stats[:, 0, :], stats[:, 1, :])
    mean_two, inv_two = combine(stats[:, 2, :], stats[:, 3, :])
    normed_one = (res_one - mean_one) * inv_one
    normed_two = (res_two - mean_two) * inv_two
    summed = g1_ref[...] * normed_one + (g2_ref[...] * normed_two + b2_ref[...])
    summed_half = summed.astype(bf16)
    ffn_hidden = dot(summed_half, f1_ref[...]) + fb_ref[...]
    ffn_active = gelu(ffn_hidden).astype(bf16)
    res_three = summed + dot(ffn_active, f2_ref[...])
    upstream = up_ref[...].astype(f32)
    mean_here, squares_here = centre(res_three)
    stats = share_stats(
        place,
        stack_rows(
            [
                mean_here,
                squares_here,
                col_sum(upstream),
                col_sum(upstream * (res_three - mean_here)),
            ],
            width,
        ),
        stat1,
        stat_ss.at[1],
        stat_rs.at[1],
    )
    mean_three, inv_three = combine(stats[:, 0, :], stats[:, 1, :])
    normed_three = (res_three - mean_three) * inv_three
    bias_three = jnp.sum(stats[:, 2, :], axis=0, keepdims=True)
    gain_three = inv_three * jnp.sum(
        stats[:, 3, :] + (stats[:, 0, :] - mean_three) * stats[:, 2, :], axis=0, keepdims=True
    )
    g3 = g3_ref[...]
    result_out[...] = (g3 * normed_three + b3_ref[...]).astype(bf16)

    def norm_back(up, normed, inv, gain, bias_sum, gain_sum):
        return inv * (
            gain * up - gain * bias_sum / total_rows - normed * (gain * gain_sum / total_rows)
        )

    grad_three = norm_back(upstream, normed_three, inv_three, g3, bias_three, gain_three)
    grad_ffn = grad_three.astype(bf16)
    grad_hidden = (gelu_slope(ffn_hidden) * dot(grad_ffn, f2_ref[...], 1, 1)).astype(bf16)
    grad_summed = grad_three + dot(grad_hidden, f1_ref[...], 1, 1)
    fb_part = col_sum(grad_hidden.astype(f32))
    stats = share_stats(
        place,
        stack_rows(
            [
                col_sum(grad_summed),
                col_sum(grad_summed * normed_one),
                col_sum(grad_summed * normed_two),
                fb_part[:, :width],
                fb_part[:, width:],
            ],
            width,
        ),
        stat2,
        stat_ss.at[2],
        stat_rs.at[2],
    )
    sums = jnp.sum(stats, axis=0)
    bias_sum, gain_one, gain_two = sums[0:1], sums[1:2], sums[2:3]
    grad_first = norm_back(grad_summed, normed_one, inv_one, g1_ref[...], bias_sum, gain_one)
    grad_second = norm_back(grad_summed, normed_two, inv_two, g2_ref[...], bias_sum, gain_two)
    grad_global = grad_second.astype(bf16)
    grad_att = dot(out_w_ref[...], grad_global, 1, 1).astype(bf16)
    for h in range(HEADS):
        do_send[h] = grad_att[HDIM * h : HDIM * (h + 1)]
    copies = []
    for k in range(1, HEADS):
        spot = lax.rem(place.p + k, HEADS)
        c = place.copy(
            do_send.at[spot], do_out.at[place.p], do_ss.at[k], do_rs.at[k], place.in_plane(k)
        )
        c.start()
        copies.append(c)
    do_out[place.p] = do_send[place.p]

    grad_local = grad_first.astype(bf16)
    hidden = hidden_ref[...]
    active = gelu(hidden).astype(bf16)
    grad_one = (gelu_slope(hidden) * dot(grad_local, w2_ref[...], 1, 1)).astype(bf16)
    grad_mixed = dot(grad_one, w1_ref[...], 1, 1)
    source = edge_places(place, len_ref, step_ref, rows).astype(f32)
    source = jnp.concatenate([source, jnp.zeros((rows, 128 - EDGES), f32)], axis=1).T
    source = source[0:EDGES].astype(jnp.int32)
    cells = lax.broadcasted_iota(jnp.int32, (3 * rows, rows), 0)
    back = jnp.zeros((3 * rows, width), f32)
    for k in range(EDGES):
        select = (source[k : k + 1, :] == cells).astype(f32).astype(bf16)
        back = back + dot(select, (slope_ref[k] * grad_mixed).astype(bf16))
    edge_send[0] = back[2 * rows :].astype(bf16)
    edge_send[1] = back[:rows].astype(bf16)
    after = lax.rem(place.me + 1, count)
    before = lax.rem(place.me + count - 1, count)
    up = place.copy(edge_send.at[0], edge_got.at[0], halo_ss.at[0], halo_rs.at[0], after)
    down = place.copy(edge_send.at[1], edge_got.at[1], halo_ss.at[1], halo_rs.at[1], before)
    up.start()
    down.start()
    f2_out[...] = dot(ffn_active.T, grad_ffn)
    f1_out[...] = dot(summed_half.T, grad_hidden)
    ow_out[...] = dot(att_half, grad_global)
    gw2_out[...] = dot(active.T, grad_local)
    gw1_out[...] = dot(mixed_ref[...].T, grad_one)
    vec_out[...] = jnp.concatenate(
        [
            gain_one,
            gain_two,
            bias_sum,
            gain_three,
            bias_three,
            sums[3:4],
            sums[4:5],
            col_sum(grad_one.astype(f32)),
        ],
        axis=0,
    )
    node_grad = grad_first + grad_second + grad_mixed + back[rows : 2 * rows]
    up.wait()
    down.wait()
    from_before = jnp.where(place.me > 0, edge_got[0].astype(f32), 0.0)
    from_after = jnp.where(place.me < count - 1, edge_got[1].astype(f32), 0.0)
    grad_out[...] = node_grad + from_before + from_after
    for c in copies:
        c.wait()


def attend_back_kernel(
    count,
    cores,
    key_tile,
    query_tile,
    len_ref,
    q_ref,
    kv_ref,
    att_ref,
    log_ref,
    do_ref,
    dq_out,
    dkv_out,
    keys,
    values,
    queries,
    grads,
    key_rows,
    query_rows,
    grad_rows,
    dq_total,
):
    place = Place(count, cores)
    cols = q_ref.shape[2]
    width = HEADS * cols
    key_count = count * cols
    first = place.z * width

    def prepare_key(b, _):
        build_keys(len_ref, kv_ref, keys, cols, b)
        vt = kv_ref[b, HDIM : 2 * HDIM]
        ks = pl.ds(pl.multiple_of(b * cols, cols), cols)
        values[ks, :] = jnp.concatenate([vt, vt, vt, jnp.ones((HDIM, cols), bf16)], axis=0).T
        key_rows[:, ks] = kv_ref[b, 0:HDIM]
        return 0

    def spread(v):
        parts = [part[0:1].astype(f32) for part in three_parts(v)]
        row = lax.broadcasted_iota(jnp.int32, (16, cols), 0)
        out = jnp.where(row == 0, parts[0], 0.0)
        out = jnp.where(row == 1, parts[1], out)
        return jnp.where(row == 2, parts[2], out).astype(bf16)

    def prepare_query(b, _):
        qs = pl.ds(pl.multiple_of(b * cols, cols), cols)
        build_queries(len_ref, q_ref, queries, cols, b, first, spread(-log_ref[0:1, qs]))
        grad = do_ref[b].astype(f32)
        inner = jnp.sum(grad * att_ref[:, qs], axis=0, keepdims=True) * score_scale
        grads[:, qs] = jnp.concatenate(
            list(three_parts(grad * score_scale)) + [spread(-inner), jnp.zeros((16, cols), bf16)],
            axis=0,
        )
        query_rows[:, qs] = q_ref[b]
        grad_rows[:, qs] = do_ref[b]
        return 0

    lax.fori_loop(0, count, prepare_key, 0)
    lax.fori_loop(0, HEADS, prepare_query, 0)
    dq_total[...] = jnp.zeros_like(dq_total)
    blocks = key_tile // cols

    def key_step(j, _):
        ks = pl.ds(pl.multiple_of(j * key_tile, key_tile), key_tile)
        key_part = keys[ks, :]
        value_part = values[ks, :]
        key_t = key_rows[:, ks]

        def query_step(i, state):
            dk, dv = state
            qs = pl.ds(pl.multiple_of(i * query_tile, query_tile), query_tile)
            probs = jnp.exp2(dot(key_part, queries[:, qs]))
            half = probs.astype(bf16)
            grad_scores = (probs * dot(value_part, grads[:, qs])).astype(bf16)
            dq_total[:, qs] += dot(key_t, grad_scores)
            return (
                dk + dot(query_rows[:, qs], grad_scores, 1, 1),
                dv + dot(grad_rows[:, qs], half, 1, 1),
            )

        state = (jnp.zeros((HDIM, key_tile), f32),) * 2
        dk, dv = lax.fori_loop(0, width // query_tile, query_step, state, unroll=True)
        for b in range(blocks):
            part = slice(b * cols, (b + 1) * cols)
            dkv_out[j * blocks + b] = jnp.concatenate([dk[:, part], dv[:, part]], axis=0).astype(
                bf16
            )
        return 0

    lax.fori_loop(0, key_count // key_tile, key_step, 0)
    for b in range(HEADS):
        dq_out[b] = dq_total[:, b * cols : (b + 1) * cols].astype(bf16)


def return_kernel(
    count,
    cores,
    x_ref,
    wq_ref,
    wk_ref,
    wv_ref,
    dq_ref,
    dkv_ref,
    grad_ref,
    grad_out,
    qw_out,
    kw_out,
    vw_out,
    z_got,
    send,
    got,
    z_ss,
    z_rs,
    a2a_ss,
    a2a_rs,
):
    place = Place(count, cores)
    planes = place.planes
    place.greet(
        [place.in_plane(k) for k in range(1, HEADS)] + [place.along(k) for k in range(1, planes)]
    )
    copies = []
    for k in range(1, planes):
        there = lax.rem(place.z + k, planes)
        c = place.copy(
            dkv_ref.at[pl.ds(there * HEADS, HEADS)],
            z_got.at[k],
            z_ss.at[k],
            z_rs.at[k],
            place.along(k),
        )
        c.start()
        copies.append(c)
    xt = x_ref[...].T
    dkv = dkv_ref[pl.ds(place.z * HEADS, HEADS)].astype(f32)
    for k, c in enumerate(copies):
        c.wait()
        dkv = dkv + z_got[k + 1].astype(f32)
    for b in range(HEADS):
        send[b, 0:HDIM] = dq_ref[b]
        send[b, HDIM : 3 * HDIM] = dkv[b].astype(bf16)
    copies = []
    for k in range(1, HEADS):
        spot = lax.rem(place.p + k, HEADS)
        c = place.copy(
            send.at[spot], got.at[place.p], a2a_ss.at[k], a2a_rs.at[k], place.in_plane(k)
        )
        c.start()
        copies.append(c)
    got[place.p] = send[place.p]
    for c in copies:
        c.wait()
    node_grad = grad_ref[...]
    for s, (w_ref, w_out) in enumerate(((wq_ref, qw_out), (wk_ref, kw_out), (wv_ref, vw_out))):
        part = jnp.concatenate(
            [got[h, HDIM * s : HDIM * (s + 1)] for h in range(HEADS)], axis=0
        )
        part = part.T
        node_grad = node_grad + dot(part, w_ref[...], 1, 1)
        w_out[...] = dot(xt, part)
    grad_out[...] = node_grad


def on_device(
    count,
    cores,
    node_feat,
    edge_feat,
    edge_step,
    degree,
    graph_len,
    gine_w1,
    gine_b1,
    gine_w2,
    query_w,
    key_w,
    value_w,
    out_w,
    ffn_w1,
    ffn_b1,
    ffn_w2,
    norm1_gain,
    norm2_gain,
    norm2_bias,
    norm3_gain,
    norm3_bias,
    out_grad,
):
    rows, width = node_feat.shape
    ffn = ffn_w1.shape[1]
    planes = count // HEADS
    plane_rows = HEADS * rows
    all_rows = count * rows
    vmem = pl.BlockSpec(memory_space=pltpu.VMEM)
    smem = pl.BlockSpec(memory_space=pltpu.SMEM)
    dma = pltpu.SemaphoreType.DMA
    shape = jax.ShapeDtypeStruct

    def row(v):
        return v.reshape(1, -1)

    def params(number=None):
        if number is None:
            return pltpu.CompilerParams(vmem_limit_bytes=60 << 20)
        return pltpu.CompilerParams(
            vmem_limit_bytes=60 << 20, collective_id=number, has_side_effects=True
        )

    q, kv, mixed, hidden, res_one, slopes = pl.pallas_call(
        functools.partial(project_kernel, count, cores),
        out_shape=(
            shape((HEADS, HDIM, rows), bf16),
            shape((count, 2 * HDIM, rows), bf16),
            shape((rows, width), bf16),
            shape((rows, width), f32),
            shape((rows, width), f32),
            shape((EDGES, rows, width), f32),
        ),
        in_specs=[smem] + [vmem] * 10,
        out_specs=(vmem,) * 6,
        scratch_shapes=[
            pltpu.VMEM((3 * rows, width), bf16),
            pltpu.VMEM((HEADS, HDIM, rows), bf16),
            pltpu.VMEM((HEADS, 2 * HDIM, rows), bf16),
            dma((2,)),
            dma((2,)),
            dma((2, HEADS)),
            dma((2, HEADS)),
            dma((planes,)),
            dma((planes,)),
        ],
        compiler_params=params(1),
    )(
        graph_len,
        node_feat,
        query_w,
        key_w,
        value_w,
        edge_step,
        row(degree),
        edge_feat,
        gine_w1,
        row(gine_b1),
        gine_w2,
    )

    att, logs = pl.pallas_call(
        functools.partial(attend_kernel, count, cores, 1024, 512),
        out_shape=(shape((HDIM, plane_rows), f32), shape((8, plane_rows), f32)),
        in_specs=[smem, vmem, vmem],
        out_specs=(vmem, vmem),
        scratch_shapes=[
            pltpu.VMEM((all_rows, 128), bf16),
            pltpu.VMEM((HDIM + 16, all_rows), bf16),
            pltpu.VMEM((128, plane_rows), bf16),
            pltpu.VMEM((HDIM + 16, plane_rows), f32),
            pltpu.VMEM((8, plane_rows), f32),
        ],
        compiler_params=params(),
    )(graph_len, q, kv)

    (result, grad_part, grad_att, vectors, f1_part, f2_part, ow_part, gw1_part, gw2_part) = (
        pl.pallas_call(
            functools.partial(norms_kernel, count, cores),
            out_shape=(
                shape((rows, width), bf16),
                shape((rows, width), f32),
                shape((HEADS, HDIM, rows), bf16),
                shape((8, width), f32),
                shape((width, ffn), f32),
                shape((ffn, width), f32),
                shape((width, width), f32),
                shape((width, width), f32),
                shape((width, width), f32),
            ),
            in_specs=[vmem] * 16 + [smem] + [vmem] * 3,
            out_specs=(vmem,) * 9,
            scratch_shapes=[
                pltpu.VMEM((HEADS, HDIM, rows), bf16),
                pltpu.VMEM((HEADS, HDIM, rows), bf16),
                pltpu.VMEM((HEADS, HDIM, rows), bf16),
                pltpu.VMEM((2, rows, width), bf16),
                pltpu.VMEM((2, rows, width), bf16),
                pltpu.VMEM((count, 8, width), f32),
                pltpu.VMEM((count, 8, width), f32),
                pltpu.VMEM((count, 8, width), f32),
                dma((HEADS,)),
                dma((HEADS,)),
                dma((3, count)),
                dma((3, count)),
                dma((HEADS,)),
                dma((HEADS,)),
                dma((2,)),
                dma((2,)),
            ],
            compiler_params=params(2),
        )(
            node_feat,
            res_one,
            att,
            out_grad,
            out_w,
            ffn_w1,
            row(ffn_b1),
            ffn_w2,
            row(norm1_gain),
            row(norm2_gain),
            row(norm2_bias),
            row(norm3_gain),
            row(norm3_bias),
            mixed,
            hidden,
            slopes,
            graph_len,
            edge_step,
            gine_w1,
            gine_w2,
        )
    )

    dq, dkv = pl.pallas_call(
        functools.partial(attend_back_kernel, count, cores, 1024, 512),
        out_shape=(shape((HEADS, HDIM, rows), bf16), shape((count, 2 * HDIM, rows), bf16)),
        in_specs=[smem] + [vmem] * 5,
        out_specs=(vmem, vmem),
        scratch_shapes=[
            pltpu.VMEM((all_rows, 128), bf16),
            pltpu.VMEM((all_rows, 128), bf16),
            pltpu.VMEM((128, plane_rows), bf16),
            pltpu.VMEM((128, plane_rows), bf16),
            pltpu.VMEM((HDIM, all_rows), bf16),
            pltpu.VMEM((HDIM, plane_rows), bf16),
            pltpu.VMEM((HDIM, plane_rows), bf16),
            pltpu.VMEM((HDIM, plane_rows), f32),
        ],
        compiler_params=params(),
    )(graph_len, q, kv, att, logs, grad_att)

    node_grad, qw_part, kw_part, vw_part = pl.pallas_call(
        functools.partial(return_kernel, count, cores),
        out_shape=(shape((rows, width), f32),) + (shape((width, width), f32),) * 3,
        in_specs=[vmem] * 7,
        out_specs=(vmem,) * 4,
        scratch_shapes=[
            pltpu.VMEM((planes, HEADS, 2 * HDIM, rows), bf16),
            pltpu.VMEM((HEADS, 3 * HDIM, rows), bf16),
            pltpu.VMEM((HEADS, 3 * HDIM, rows), bf16),
            dma((planes,)),
            dma((planes,)),
            dma((HEADS,)),
            dma((HEADS,)),
        ],
        compiler_params=params(3),
    )(node_feat, query_w, key_w, value_w, dq, dkv, grad_part)

    gw1, gb1, gw2, qw, kw, vw, ow, f1, f2 = lax.psum(
        (gw1_part, vectors[7], gw2_part, qw_part, kw_part, vw_part, ow_part, f1_part, f2_part),
        AXES,
    )
    fb = vectors[5:7].reshape(ffn)
    return (
        result,
        node_grad,
        gw1,
        gb1,
        gw2,
        qw,
        kw,
        vw,
        ow,
        f1,
        fb,
        f2,
        vectors[0],
        vectors[1],
        vectors[2],
        vectors[3],
        vectors[4],
    )


def solution(mesh):
    count = mesh.shape["blk"] * mesh.shape["rep"]
    rows = P(AXES, None)
    whole = P()
    return jax.shard_map(
        functools.partial(on_device, count, mesh.shape["rep"]),
        mesh=mesh,
        in_specs=(rows, P(AXES, None, None), rows, P(AXES)) + (whole,) * 16 + (rows,),
        out_specs=(rows, rows) + (whole,) * 15,
        check_vma=False,
    )
```

```python
import functools
import jax
import jax.numpy as jnp
from jax import lax
from jax.experimental import pallas as pl
from jax.experimental.pallas import tpu as pltpu
from jax.sharding import PartitionSpec as P

HEADS = 8
HDIM = 32
EDGES = 8
GRAPHS = 9
AXES = ("blk", "rep")
MESH = pl.DeviceIdType.MESH
bf16 = jnp.bfloat16
f32 = jnp.float32

norm_eps = 1e-05
far_score = -1e30
log2_e = 1.4426950408889634
score_scale = HDIM ** (-0.5)
gelu_c = 0.7978845608028654
gelu_a = 0.044715


def dot(left, right, left_dim=1, right_dim=0):
    return lax.dot_general(
        left, right, (((left_dim,), (right_dim,)), ((), ())), preferred_element_type=f32
    )


def gelu(v):
    return 0.5 * v * (1.0 + jnp.tanh(gelu_c * (v + gelu_a * (v * v * v))))


def gelu_slope(v):
    squared = v * v
    bend = jnp.tanh(gelu_c * v * (1.0 + gelu_a * squared))
    return 0.5 * (1.0 + bend) + 0.5 * v * (1.0 - bend * bend) * (
        gelu_c * (1.0 + 3.0 * gelu_a * squared)
    )


def three_parts(v):
    first = v.astype(bf16)
    rest = v - first.astype(f32)
    second = rest.astype(bf16)
    third = (rest - second.astype(f32)).astype(bf16)
    return first, second, third


class Place:
    def __init__(self, count, cores):
        self.count = count
        self.cores = cores
        self.planes = count // HEADS
        self.me = lax.axis_index("blk") * cores + lax.axis_index("rep")
        self.z = lax.div(self.me, HEADS)
        self.p = lax.rem(self.me, HEADS)

    def device(self, index):
        return {"blk": lax.div(index, self.cores), "rep": lax.rem(index, self.cores)}

    def in_plane(self, k):
        return self.z * HEADS + lax.rem(self.p + k, HEADS)

    def along(self, k):
        return lax.rem(self.me + HEADS * k, self.count)

    def mirrored(self, k):
        peer, bit = 0, 1
        while bit < self.count:
            mine = lax.rem(lax.div(self.me, bit), 2)
            flip = lax.rem(lax.div(k, bit), 2)
            peer = peer + bit * (mine + flip - 2 * mine * flip)
            bit *= 2
        return peer

    def greet(self, peers):
        barrier = pltpu.get_barrier_semaphore()
        for peer in peers:
            pl.semaphore_signal(barrier, inc=1, device_id=self.device(peer), device_id_type=MESH)
        pl.semaphore_wait(barrier, len(peers))

    def greet_all(self):
        barrier = pltpu.get_barrier_semaphore()

        def hello(k, _):
            pl.semaphore_signal(
                barrier, inc=1, device_id=self.device(self.mirrored(k)), device_id_type=MESH
            )
            return 0

        lax.fori_loop(1, self.count, hello, 0)
        pl.semaphore_wait(barrier, self.count - 1)

    def copy(self, src, dst, send_sem, recv_sem, peer):
        return pltpu.make_async_remote_copy(
            src_ref=src,
            dst_ref=dst,
            send_sem=send_sem,
            recv_sem=recv_sem,
            device_id=self.device(peer),
            device_id_type=MESH,
        )


def graph_bounds(len_ref, positions):
    last = 0
    graph = jnp.zeros(positions.shape, jnp.int32)
    start = jnp.zeros(positions.shape, jnp.int32)
    ends = []
    for g in range(GRAPHS):
        last = last + len_ref[g]
        ends.append(last)
        passed = positions >= last
        graph = graph + passed.astype(jnp.int32)
        start = jnp.where(passed, last, start)
    stop = jnp.full(positions.shape, ends[-1], jnp.int32)
    for end in reversed(ends):
        stop = jnp.where(positions < end, end, stop)
    return graph, start, stop


def own_graph(len_ref, first, width):
    positions = first + lax.broadcasted_iota(jnp.int32, (1, width), 1)
    graph, _, _ = graph_bounds(len_ref, positions)
    rows = lax.broadcasted_iota(jnp.int32, (16, width), 0)
    return rows == graph


def edge_places(place, len_ref, step_ref, rows):
    positions = place.me * rows + lax.broadcasted_iota(jnp.int32, (rows, 1), 0)
    _, start, stop = graph_bounds(len_ref, positions)
    source = jnp.minimum(jnp.maximum(positions + step_ref[...], start), stop - 1)
    return source - place.me * rows + rows


def as_column(row, width):
    return jnp.broadcast_to(row, (128, width)).T


def project_kernel(
    count,
    cores,
    len_ref,
    x_ref,
    wq_ref,
    wk_ref,
    wv_ref,
    step_ref,
    degree_ref,
    edge_ref,
    w1_ref,
    b1_ref,
    w2_ref,
    q_out,
    kv_out,
    mixed_out,
    hidden_out,
    res_out,
    slope_out,
    ext,
    q_send,
    kv_send,
    halo_ss,
    halo_rs,
    a2a_ss,
    a2a_rs,
    z_ss,
    z_rs,
):
    place = Place(count, cores)
    rows = x_ref.shape[0]
    planes = place.planes
    after = lax.rem(place.me + 1, count)
    before = lax.rem(place.me + count - 1, count)
    place.greet(
        [after, before]
        + [place.in_plane(k) for k in range(1, HEADS)]
        + [place.along(k) for k in range(1, planes)]
    )
    x = x_ref[...]
    ext[rows : 2 * rows, :] = x
    up = place.copy(x_ref, ext.at[pl.ds(0, rows)], halo_ss.at[0], halo_rs.at[0], after)
    down = place.copy(x_ref, ext.at[pl.ds(2 * rows, rows)], halo_ss.at[1], halo_rs.at[1], before)
    xt = x.T
    for h in range(HEADS):
        cols = slice(HDIM * h, HDIM * (h + 1))
    kt = dot(wk_ref[...].T, xt).astype(bf16)
    vt = dot(wv_ref[...].T, xt).astype(bf16)
    qt = dot(wq_ref[...].T, xt).astype(bf16)
    for h in range(HEADS):
        cols = slice(HDIM * h, HDIM * (h + 1))
        kv_send[h, 0:HDIM] = kt[cols]
        kv_send[h, HDIM : 2 * HDIM] = vt[cols]
        q_send[h] = qt[cols]
    kv_copies = []
    q_copies = []
    for k in range(1, HEADS):
        peer = place.in_plane(k)
        spot = lax.rem(place.p + k, HEADS)
        c = place.copy(
            kv_send.at[spot], kv_out.at[place.me], a2a_ss.at[0, k], a2a_rs.at[0, k], peer
        )
        c.start()
        kv_copies.append(c)
    for k in range(1, HEADS):
        peer = place.in_plane(k)
        spot = lax.rem(place.p + k, HEADS)
        c = place.copy(q_send.at[spot], q_out.at[place.p], a2a_ss.at[1, k], a2a_rs.at[1, k], peer)
        c.start()
        q_copies.append(c)
    up.start()
    down.start()
    kv_out[place.me] = kv_send[place.p]
    q_out[place.p] = q_send[place.p]
    for c in kv_copies:
        c.wait()
    own = pl.ds(place.z * HEADS, HEADS)
    z_copies = []
    for k in range(1, planes):
        c = place.copy(kv_out.at[own], kv_out.at[own], z_ss.at[k], z_rs.at[k], place.along(k))
        c.start()
        z_copies.append(c)
    for c in q_copies:
        c.wait()
    up.wait()
    down.wait()
    source = edge_places(place, len_ref, step_ref, rows)
    degree = as_column(degree_ref[...], rows)
    cells = lax.broadcasted_iota(jnp.int32, (rows, 3 * rows), 1)
    message = jnp.zeros(x.shape, f32)
    around = ext[...]
    for k in range(EDGES):
        select = (source[:, k : k + 1] == cells).astype(f32).astype(bf16)
        v = dot(select, around) + edge_ref[:, k, :].astype(f32)
        present = degree[:, 0:1] > k
        message = message + jnp.where(present, gelu(v), 0.0)
        slope_out[k] = jnp.where(present, gelu_slope(v), 0.0)
    mixed = (x.astype(f32) + message).astype(bf16)
    mixed_out[...] = mixed
    hidden = dot(mixed, w1_ref[...]) + b1_ref[...]
    hidden_out[...] = hidden
    res_out[...] = x.astype(f32) + dot(gelu(hidden).astype(bf16), w2_ref[...])
    for c in z_copies:
        c.wait()


def build_keys(len_ref, kv_ref, keys, cols, block):
    kt = kv_ref[block, 0:HDIM]
    same = own_graph(len_ref, block * cols, cols).astype(f32).astype(bf16)
    ones = jnp.ones((16, cols), bf16)
    keys[pl.ds(pl.multiple_of(block * cols, cols), cols), :] = jnp.concatenate(
        [kt, kt, kt, same, ones], axis=0
    ).T


def build_queries(len_ref, q_ref, queries, cols, block, first, last_rows):
    parts = three_parts(q_ref[block].astype(f32) * (score_scale * log2_e))
    same = own_graph(len_ref, first + block * cols, cols)
    known = lax.broadcasted_iota(jnp.int32, (16, cols), 0) < GRAPHS
    mask = jnp.where(jnp.logical_or(same, jnp.logical_not(known)), 0.0, far_score).astype(bf16)
    queries[:, pl.ds(pl.multiple_of(block * cols, cols), cols)] = jnp.concatenate(
        list(parts) + [mask, last_rows], axis=0
    )


def attend_kernel(
    count,
    cores,
    key_tile,
    query_tile,
    len_ref,
    q_ref,
    kv_ref,
    att_out,
    log_out,
    keys,
    values,
    queries,
    total,
    top,
):
    place = Place(count, cores)
    cols = q_ref.shape[2]
    width = HEADS * cols
    key_count = count * cols
    first = place.z * width

    def prepare_key(b, _):
        build_keys(len_ref, kv_ref, keys, cols, b)
        values[:, pl.ds(pl.multiple_of(b * cols, cols), cols)] = jnp.concatenate(
            [kv_ref[b, HDIM : 2 * HDIM], jnp.ones((16, cols), bf16)], axis=0
        )
        return 0

    def prepare_query(b, _):
        build_queries(
            len_ref, q_ref, queries, cols, b, first, jnp.zeros((16, cols), bf16)
        )
        return 0

    lax.fori_loop(0, count, prepare_key, 0)
    lax.fori_loop(0, HEADS, prepare_query, 0)
    total[...] = jnp.zeros_like(total)

    def key_step(j, _):
        ks = pl.ds(pl.multiple_of(j * key_tile, key_tile), key_tile)
        key_part = keys[ks, :]
        value_part = values[:, ks]

        def query_step(i, _):
            qs = pl.ds(pl.multiple_of(i * query_tile, query_tile), query_tile)
            weights = jnp.exp2(dot(key_part, queries[:, qs])).astype(bf16)
            total[:, qs] += dot(value_part, weights)
            return 0

        lax.fori_loop(0, width // query_tile, query_step, 0, unroll=True)
        return 0

    lax.fori_loop(0, key_count // key_tile, key_step, 0)
    top[...] = jnp.zeros_like(top)
    sums = total[HDIM : HDIM + 1, :]
    fine = jnp.logical_and(sums > 2.0**-60, sums < 2.0**120)
    faulty = jnp.max(jnp.where(fine, 0.0, 1.0)) > 0.5

    @pl.when(faulty)
    def with_running_top():
        tile = 256

        def query_step(i, _):
            qs = pl.ds(pl.multiple_of(i * tile, tile), tile)
            query_part = queries[:, qs]

            def key_step(j, state):
                top_prev, total_prev = state
                ks = pl.ds(pl.multiple_of(j * tile, tile), tile)
                scores = dot(keys[ks, :], query_part)
                top_next = jnp.maximum(top_prev, jnp.max(scores, axis=0, keepdims=True))
                weights = jnp.exp2(scores - top_next).astype(bf16)
                return top_next, total_prev * jnp.exp2(top_prev - top_next) + dot(
                    values[:, ks], weights
                )

            state = (jnp.full((1, tile), 2.0 * far_score, f32), jnp.zeros((HDIM + 16, tile), f32))
            top_last, total_last = lax.fori_loop(0, key_count // tile, key_step, state)
            top[0:1, qs] = top_last
            total[:, qs] = total_last
            return 0

        lax.fori_loop(0, width // tile, query_step, 0)

    sums = total[HDIM : HDIM + 1, :]
    log_out[...] = jnp.broadcast_to(top[0:1, :] + jnp.log2(sums), log_out.shape)
    att_out[...] = total[0:HDIM, :] / sums


def share_stats(place, stats, buffer, send_sems, recv_sems):
    buffer[place.me] = stats

    def begin(k, _):
        far = place.count - 1 - k
        place.copy(
            buffer.at[place.me],
            buffer.at[place.me],
            send_sems.at[far],
            recv_sems.at[far],
            place.mirrored(far),
        ).start()
        return 0

    def finish(k, _):
        peer = place.mirrored(k)
        c = place.copy(
            buffer.at[place.me], buffer.at[peer], send_sems.at[k], recv_sems.at[k], peer
        )
        c.wait()
        return 0

    lax.fori_loop(0, place.count - 1, begin, 0, unroll=place.count <= 32)
    lax.fori_loop(1, place.count, finish, 0, unroll=place.count <= 32)
    return buffer[...]


def col_sum(v):
    return jnp.sum(v, axis=0, keepdims=True)


def stack_rows(rows, width):
    return jnp.concatenate(rows + [jnp.zeros((8 - len(rows), width), f32)], axis=0)


def norms_kernel(
    count,
    cores,
    x_ref,
    res_ref,
    att_ref,
    up_ref,
    out_w_ref,
    f1_ref,
    fb_ref,
    f2_ref,
    g1_ref,
    g2_ref,
    b2_ref,
    g3_ref,
    b3_ref,
    mixed_ref,
    hidden_ref,
    slope_ref,
    len_ref,
    step_ref,
    w1_ref,
    w2_ref,
    result_out,
    grad_out,
    do_out,
    vec_out,
    parts_out,
    att_send,
    att_got,
    do_send,
    edge_send,
    edge_got,
    stat0,
    stat1,
    stat2,
    att_ss,
    att_rs,
    stat_ss,
    stat_rs,
    do_ss,
    do_rs,
    halo_ss,
    halo_rs,
):
    place = Place(count, cores)
    rows, width = x_ref.shape
    total_rows = rows * count
    place.greet_all()
    x = x_ref[...].astype(f32)

    for b in range(HEADS):
        att_send[b] = att_ref[:, b * rows : (b + 1) * rows].astype(bf16)
    copies = []
    for k in range(1, HEADS):
        spot = lax.rem(place.p + k, HEADS)
        c = place.copy(
            att_send.at[spot], att_got.at[place.p], att_ss.at[k], att_rs.at[k], place.in_plane(k)
        )
        c.start()
        copies.append(c)
    att_got[place.p] = att_send[place.p]
    for c in copies:
        c.wait()
    att_half = jnp.concatenate([att_got[h] for h in range(HEADS)], axis=0)
    global_out = dot(att_half.T, out_w_ref[...])
    res_one = res_ref[...]
    res_two = x + global_out

    def centre(v):
        mean = col_sum(v) / rows
        off = v - mean
        return mean, col_sum(off * off)

    def combine(means, squares):
        mean = jnp.sum(means, axis=0, keepdims=True) / count
        off = means - mean
        var = (
            jnp.sum(squares, axis=0, keepdims=True)
            + rows * jnp.sum(off * off, axis=0, keepdims=True)
        ) / total_rows
        return mean, lax.rsqrt(var + norm_eps)

    stats = share_stats(
        place,
        stack_rows([*centre(res_one), *centre(res_two)], width),
        stat0,
        stat_ss.at[0],
        stat_rs.at[0],
    )
    mean_one, inv_one = combine(stats[:, 0, :], stats[:, 1, :])
    mean_two, inv_two = combine(stats[:, 2, :], stats[:, 3, :])
    normed_one = (res_one - mean_one) * inv_one
    normed_two = (res_two - mean_two) * inv_two
    summed = g1_ref[...] * normed_one + (g2_ref[...] * normed_two + b2_ref[...])
    summed_half = summed.astype(bf16)
    ffn_hidden = dot(summed_half, f1_ref[...]) + fb_ref[...]
    ffn_active = gelu(ffn_hidden).astype(bf16)
    res_three = summed + dot(ffn_active, f2_ref[...])
    upstream = up_ref[...].astype(f32)
    mean_here, squares_here = centre(res_three)
    stats = share_stats(
        place,
        stack_rows(
            [
                mean_here,
                squares_here,
                col_sum(upstream),
                col_sum(upstream * (res_three - mean_here)),
            ],
            width,
        ),
        stat1,
        stat_ss.at[1],
        stat_rs.at[1],
    )
    mean_three, inv_three = combine(stats[:, 0, :], stats[:, 1, :])
    normed_three = (res_three - mean_three) * inv_three
    bias_three = jnp.sum(stats[:, 2, :], axis=0, keepdims=True)
    gain_three = inv_three * jnp.sum(
        stats[:, 3, :] + (stats[:, 0, :] - mean_three) * stats[:, 2, :], axis=0, keepdims=True
    )
    g3 = g3_ref[...]
    result_out[...] = (g3 * normed_three + b3_ref[...]).astype(bf16)

    def norm_back(up, normed, inv, gain, bias_sum, gain_sum):
        return inv * (
            gain * up - gain * bias_sum / total_rows - normed * (gain * gain_sum / total_rows)
        )

    grad_three = norm_back(upstream, normed_three, inv_three, g3, bias_three, gain_three)
    grad_ffn = grad_three.astype(bf16)
    grad_hidden = (gelu_slope(ffn_hidden) * dot(grad_ffn, f2_ref[...], 1, 1)).astype(bf16)
    grad_summed = grad_three + dot(grad_hidden, f1_ref[...], 1, 1)
    fb_part = col_sum(grad_hidden.astype(f32))
    stats = share_stats(
        place,
        stack_rows(
            [
                col_sum(grad_summed),
                col_sum(grad_summed * normed_one),
                col_sum(grad_summed * normed_two),
                fb_part[:, :width],
                fb_part[:, width:],
            ],
            width,
        ),
        stat2,
        stat_ss.at[2],
        stat_rs.at[2],
    )
    sums = jnp.sum(stats, axis=0)
    bias_sum, gain_one, gain_two = sums[0:1], sums[1:2], sums[2:3]
    grad_first = norm_back(grad_summed, normed_one, inv_one, g1_ref[...], bias_sum, gain_one)
    grad_second = norm_back(grad_summed, normed_two, inv_two, g2_ref[...], bias_sum, gain_two)
    grad_global = grad_second.astype(bf16)
    grad_att = dot(out_w_ref[...], grad_global, 1, 1).astype(bf16)
    for h in range(HEADS):
        do_send[h] = grad_att[HDIM * h : HDIM * (h + 1)]
    copies = []
    for k in range(1, HEADS):
        spot = lax.rem(place.p + k, HEADS)
        c = place.copy(
            do_send.at[spot], do_out.at[place.p], do_ss.at[k], do_rs.at[k], place.in_plane(k)
        )
        c.start()
        copies.append(c)
    do_out[place.p] = do_send[place.p]

    grad_local = grad_first.astype(bf16)
    hidden = hidden_ref[...]
    active = gelu(hidden).astype(bf16)
    grad_one = (gelu_slope(hidden) * dot(grad_local, w2_ref[...], 1, 1)).astype(bf16)
    grad_mixed = dot(grad_one, w1_ref[...], 1, 1)
    source = edge_places(place, len_ref, step_ref, rows).astype(f32)
    source = jnp.concatenate([source, jnp.zeros((rows, 128 - EDGES), f32)], axis=1).T
    source = source[0:EDGES].astype(jnp.int32)
    cells = lax.broadcasted_iota(jnp.int32, (3 * rows, rows), 0)
    back = jnp.zeros((3 * rows, width), f32)
    for k in range(EDGES):
        select = (source[k : k + 1, :] == cells).astype(f32).astype(bf16)
        back = back + dot(select, (slope_ref[k] * grad_mixed).astype(bf16))
    edge_send[0] = back[2 * rows :].astype(bf16)
    edge_send[1] = back[:rows].astype(bf16)
    after = lax.rem(place.me + 1, count)
    before = lax.rem(place.me + count - 1, count)
    up = place.copy(edge_send.at[0], edge_got.at[0], halo_ss.at[0], halo_rs.at[0], after)
    down = place.copy(edge_send.at[1], edge_got.at[1], halo_ss.at[1], halo_rs.at[1], before)
    up.start()
    down.start()
    f1_part = dot(summed_half.T, grad_hidden).astype(bf16)
    at = 0
    for part in (
        dot(mixed_ref[...].T, grad_one),
        dot(active.T, grad_local),
        dot(att_half, grad_global),
        f1_part[:, :width],
        f1_part[:, width:],
        dot(ffn_active.T, grad_ffn),
        jnp.broadcast_to(col_sum(grad_one.astype(f32)), (16, width)),
    ):
        parts_out[at : at + part.shape[0], :] = part.astype(bf16)
        at += part.shape[0]
    parts_out[at:, :] = jnp.zeros((parts_out.shape[0] - at, width), bf16)
    vec_out[...] = jnp.concatenate(
        [
            gain_one,
            gain_two,
            bias_sum,
            gain_three,
            bias_three,
            sums[3:4],
            sums[4:5],
            jnp.zeros((1, width), f32),
        ],
        axis=0,
    )
    node_grad = grad_first + grad_second + grad_mixed + back[rows : 2 * rows]
    up.wait()
    down.wait()
    from_before = jnp.where(place.me > 0, edge_got[0].astype(f32), 0.0)
    from_after = jnp.where(place.me < count - 1, edge_got[1].astype(f32), 0.0)
    grad_out[...] = node_grad + from_before + from_after
    for c in copies:
        c.wait()


def attend_back_kernel(
    count,
    cores,
    key_tile,
    query_tile,
    len_ref,
    q_ref,
    kv_ref,
    att_ref,
    log_ref,
    do_ref,
    x_ref,
    parts_ref,
    back_out,
    heads_out,
    sums_out,
    keys,
    values,
    queries,
    grads,
    key_rows,
    query_rows,
    grad_rows,
    dq_total,
    dkv_part,
    dkv_got,
    back_send,
    x_all,
    parts_got,
    plane_sum,
    line_got,
    line_sum,
    heads_part,
    heads_got,
    x_ss,
    x_rs,
    parts_ss,
    parts_rs,
    line_ss,
    line_rs,
    whole_ss,
    whole_rs,
    dkv_ss,
    dkv_rs,
    back_ss,
    back_rs,
    heads_ss,
    heads_rs,
):
    place = Place(count, cores)
    planes = place.planes
    cols = q_ref.shape[2]
    width = HEADS * cols
    first = place.z * width
    share = parts_ref.shape[0] // HEADS
    slice_rows = share // planes
    place.greet(
        [place.in_plane(k) for k in range(1, HEADS)] + [place.along(k) for k in range(1, planes)]
    )

    def to_plane(src_of, dst, send_sems, recv_sems):
        copies = []
        for k in range(1, HEADS):
            spot = lax.rem(place.p + k, HEADS)
            c = place.copy(src_of(spot), dst, send_sems.at[k], recv_sems.at[k], place.in_plane(k))
            c.start()
            copies.append(c)
        return copies

    def to_line(src_of, dst_of, send_sems, recv_sems):
        copies = []
        for k in range(1, planes):
            there = lax.rem(place.z + k, planes)
            c = place.copy(
                src_of(there), dst_of(k), send_sems.at[k], recv_sems.at[k], place.along(k)
            )
            c.start()
            copies.append(c)
        return copies

    def wait_all(copies):
        for c in copies:
            c.wait()

    def share_rows(ref, spot, size):
        return ref.at[pl.ds(pl.multiple_of(spot * size, size), size)]

    parts_moves = to_plane(
        lambda spot: share_rows(parts_ref, spot, share),
        parts_got.at[place.p],
        parts_ss,
        parts_rs,
    )
    parts_got[place.p] = parts_ref[pl.ds(pl.multiple_of(place.p * share, share), share)]
    x_moves = to_plane(lambda spot: x_ref, x_all.at[place.p], x_ss, x_rs)
    x_all[place.p] = x_ref[...]

    def prepare_key(b, _):
        build_keys(len_ref, kv_ref, keys, cols, b)
        vt = kv_ref[b, HDIM : 2 * HDIM]
        ks = pl.ds(pl.multiple_of(b * cols, cols), cols)
        values[ks, :] = jnp.concatenate([vt, vt, vt, jnp.ones((HDIM, cols), bf16)], axis=0).T
        key_rows[:, ks] = kv_ref[b, 0:HDIM]
        return 0

    def spread(v):
        parts = [part[0:1].astype(f32) for part in three_parts(v)]
        row = lax.broadcasted_iota(jnp.int32, (16, cols), 0)
        out = jnp.where(row == 0, parts[0], 0.0)
        out = jnp.where(row == 1, parts[1], out)
        return jnp.where(row == 2, parts[2], out).astype(bf16)

    def prepare_query(b, _):
        qs = pl.ds(pl.multiple_of(b * cols, cols), cols)
        build_queries(len_ref, q_ref, queries, cols, b, first, spread(-log_ref[0:1, qs]))
        grad = do_ref[b].astype(f32)
        inner = jnp.sum(grad * att_ref[:, qs], axis=0, keepdims=True) * score_scale
        grads[:, qs] = jnp.concatenate(
            list(three_parts(grad * score_scale)) + [spread(-inner), jnp.zeros((16, cols), bf16)],
            axis=0,
        )
        query_rows[:, qs] = q_ref[b]
        grad_rows[:, qs] = do_ref[b]
        return 0

    lax.fori_loop(0, count, prepare_key, 0)
    lax.fori_loop(0, HEADS, prepare_query, 0)
    dq_total[...] = jnp.zeros_like(dq_total)
    blocks = key_tile // cols
    steps = width // key_tile

    def plane_of_keys(plane):
        def key_step(j, _):
            spot = plane * HEADS + j * blocks
            ks = pl.ds(pl.multiple_of(spot * cols, key_tile), key_tile)
            key_part = keys[ks, :]
            value_part = values[ks, :]
            key_t = key_rows[:, ks]

            def query_step(i, state):
                dk, dv = state
                qs = pl.ds(pl.multiple_of(i * query_tile, query_tile), query_tile)
                probs = jnp.exp2(dot(key_part, queries[:, qs]))
                half = probs.astype(bf16)
                grad_scores = (probs * dot(value_part, grads[:, qs])).astype(bf16)
                dq_total[:, qs] += dot(key_t, grad_scores)
                return (
                    dk + dot(query_rows[:, qs], grad_scores, 1, 1),
                    dv + dot(grad_rows[:, qs], half, 1, 1),
                )

            state = (jnp.zeros((HDIM, key_tile), f32),) * 2
            dk, dv = lax.fori_loop(0, width // query_tile, query_step, state, unroll=True)
            for b in range(blocks):
                part = slice(b * cols, (b + 1) * cols)
                dkv_part[spot + b] = jnp.concatenate([dk[:, part], dv[:, part]], axis=0).astype(
                    bf16
                )
            return 0

        lax.fori_loop(0, steps, key_step, 0)

    line_moves, whole_moves, dkv_moves = [], [], []
    for step in range(planes):
        k = (step + 1) % planes
        there = lax.rem(place.z + k, planes)
        plane_of_keys(there)
        if k > 0:
            c = place.copy(
                share_rows(dkv_part, there, HEADS),
                dkv_got.at[k],
                dkv_ss.at[k],
                dkv_rs.at[k],
                place.along(k),
            )
            c.start()
            dkv_moves.append(c)
        if step == 0:
            wait_all(parts_moves)
            total = parts_got[0].astype(f32)
            for h in range(1, HEADS):
                total = total + parts_got[h].astype(f32)
            plane_sum[...] = total.astype(bf16)
            line_moves = to_line(
                lambda spot: share_rows(plane_sum, spot, slice_rows),
                lambda k: line_got.at[k],
                line_ss.at[0],
                line_rs.at[0],
            )
        if step == 1:
            wait_all(line_moves)
            total = plane_sum[
                pl.ds(pl.multiple_of(place.z * slice_rows, slice_rows), slice_rows)
            ].astype(f32)
            for k in range(1, planes):
                total = total + line_got[k].astype(f32)
            line_sum[place.z] = total.astype(bf16)
            line_moves = to_line(
                lambda spot: line_sum.at[place.z],
                lambda k: line_sum.at[place.z],
                line_ss.at[1],
                line_rs.at[1],
            )
        if step == 2:
            wait_all(line_moves)
            sums_out[place.p] = line_sum[...].reshape(share, cols)
            whole_moves = to_plane(
                lambda spot: sums_out.at[place.p], sums_out.at[place.p], whole_ss, whole_rs
            )
    wait_all(x_moves)
    wait_all(dkv_moves)
    dkv = dkv_part[pl.ds(place.z * HEADS, HEADS)].astype(f32)
    for k in range(1, planes):
        dkv = dkv + dkv_got[k].astype(f32)
    for b in range(HEADS):
        back_send[b, 0:HDIM] = dq_total[:, b * cols : (b + 1) * cols].astype(bf16)
        back_send[b, HDIM : 3 * HDIM] = dkv[b].astype(bf16)
    back_moves = to_plane(
        lambda spot: back_send.at[spot], back_out.at[place.p], back_ss, back_rs
    )
    back_out[place.p] = back_send[place.p]
    total = dot(back_send[0], x_all[0])
    for b in range(1, HEADS):
        total = total + dot(back_send[b], x_all[b])
    heads_part[...] = total.astype(bf16)
    line_moves = to_line(
        lambda spot: heads_part, lambda k: heads_got.at[k], heads_ss.at[0], heads_rs.at[0]
    )
    wait_all(line_moves)
    total = heads_part[...].astype(f32)
    for k in range(1, planes):
        total = total + heads_got[k].astype(f32)
    heads_out[place.p] = total.astype(bf16)
    heads_moves = to_plane(
        lambda spot: heads_out.at[place.p], heads_out.at[place.p], heads_ss.at[1], heads_rs.at[1]
    )
    wait_all(back_moves)
    wait_all(whole_moves)
    wait_all(heads_moves)


def finish_kernel(
    wq_ref,
    wk_ref,
    wv_ref,
    grad_ref,
    back_ref,
    heads_ref,
    sums_ref,
    result_ref,
    result_out,
    grad_out,
    gw1_out,
    gb1_out,
    gw2_out,
    qw_out,
    kw_out,
    vw_out,
    ow_out,
    f1_out,
    f2_out,
):
    rows, width = grad_ref.shape
    result_out[...] = result_ref[...]
    grad = grad_ref[...]
    for s, (w_ref, w_out) in enumerate(((wq_ref, qw_out), (wk_ref, kw_out), (wv_ref, vw_out))):
        cols = slice(HDIM * s, HDIM * (s + 1))
        part = jnp.concatenate([back_ref[h, cols] for h in range(HEADS)], axis=0)
        grad = grad + dot(part.T, w_ref[...], 1, 1)
        total = jnp.concatenate([heads_ref[h, cols] for h in range(HEADS)], axis=0)
        w_out[...] = total.T.astype(f32)
    grad_out[...] = grad
    gw1_out[...] = sums_ref[0:width].astype(f32)
    gw2_out[...] = sums_ref[width : 2 * width].astype(f32)
    ow_out[...] = sums_ref[2 * width : 3 * width].astype(f32)
    f1_out[:, 0:width] = sums_ref[3 * width : 4 * width].astype(f32)
    f1_out[:, width:] = sums_ref[4 * width : 5 * width].astype(f32)
    last = 5 * width + f2_out.shape[0]
    f2_out[...] = sums_ref[5 * width : last].astype(f32)
    gb1_out[...] = sums_ref[last : last + 16].astype(f32)[0:1]


def on_device(
    count,
    cores,
    node_feat,
    edge_feat,
    edge_step,
    degree,
    graph_len,
    gine_w1,
    gine_b1,
    gine_w2,
    query_w,
    key_w,
    value_w,
    out_w,
    ffn_w1,
    ffn_b1,
    ffn_w2,
    norm1_gain,
    norm2_gain,
    norm2_bias,
    norm3_gain,
    norm3_bias,
    out_grad,
):
    rows, width = node_feat.shape
    ffn = ffn_w1.shape[1]
    planes = count // HEADS
    plane_rows = HEADS * rows
    all_rows = count * rows
    vmem = pl.BlockSpec(memory_space=pltpu.VMEM)
    smem = pl.BlockSpec(memory_space=pltpu.SMEM)
    dma = pltpu.SemaphoreType.DMA
    shape = jax.ShapeDtypeStruct

    def row(v):
        return v.reshape(1, -1)

    def params(number=None):
        if number is None:
            return pltpu.CompilerParams(vmem_limit_bytes=60 << 20)
        return pltpu.CompilerParams(
            vmem_limit_bytes=60 << 20, collective_id=number, has_side_effects=True
        )

    q, kv, mixed, hidden, res_one, slopes = pl.pallas_call(
        functools.partial(project_kernel, count, cores),
        out_shape=(
            shape((HEADS, HDIM, rows), bf16),
            shape((count, 2 * HDIM, rows), bf16),
            shape((rows, width), bf16),
            shape((rows, width), f32),
            shape((rows, width), f32),
            shape((EDGES, rows, width), f32),
        ),
        in_specs=[smem] + [vmem] * 10,
        out_specs=(vmem,) * 6,
        scratch_shapes=[
            pltpu.VMEM((3 * rows, width), bf16),
            pltpu.VMEM((HEADS, HDIM, rows), bf16),
            pltpu.VMEM((HEADS, 2 * HDIM, rows), bf16),
            dma((2,)),
            dma((2,)),
            dma((2, HEADS)),
            dma((2, HEADS)),
            dma((planes,)),
            dma((planes,)),
        ],
        compiler_params=params(1),
    )(
        graph_len,
        node_feat,
        query_w,
        key_w,
        value_w,
        edge_step,
        row(degree),
        edge_feat,
        gine_w1,
        row(gine_b1),
        gine_w2,
    )

    att, logs = pl.pallas_call(
        functools.partial(attend_kernel, count, cores, 1024, 512),
        out_shape=(shape((HDIM, plane_rows), f32), shape((8, plane_rows), f32)),
        in_specs=[smem, vmem, vmem],
        out_specs=(vmem, vmem),
        scratch_shapes=[
            pltpu.VMEM((all_rows, 128), bf16),
            pltpu.VMEM((HDIM + 16, all_rows), bf16),
            pltpu.VMEM((128, plane_rows), bf16),
            pltpu.VMEM((HDIM + 16, plane_rows), f32),
            pltpu.VMEM((8, plane_rows), f32),
        ],
        compiler_params=params(),
    )(graph_len, q, kv)

    share_unit = 16 * HEADS * planes
    needed = 3 * width + 2 * ffn * width // width + 16
    part_rows = -(-needed // share_unit) * share_unit
    share = part_rows // HEADS

    (result, grad_part, grad_att, vectors, parts) = (
        pl.pallas_call(
            functools.partial(norms_kernel, count, cores),
            out_shape=(
                shape((rows, width), bf16),
                shape((rows, width), f32),
                shape((HEADS, HDIM, rows), bf16),
                shape((8, width), f32),
                shape((part_rows, width), bf16),
            ),
            in_specs=[vmem] * 16 + [smem] + [vmem] * 3,
            out_specs=(vmem,) * 5,
            scratch_shapes=[
                pltpu.VMEM((HEADS, HDIM, rows), bf16),
                pltpu.VMEM((HEADS, HDIM, rows), bf16),
                pltpu.VMEM((HEADS, HDIM, rows), bf16),
                pltpu.VMEM((2, rows, width), bf16),
                pltpu.VMEM((2, rows, width), bf16),
                pltpu.VMEM((count, 8, width), f32),
                pltpu.VMEM((count, 8, width), f32),
                pltpu.VMEM((count, 8, width), f32),
                dma((HEADS,)),
                dma((HEADS,)),
                dma((3, count)),
                dma((3, count)),
                dma((HEADS,)),
                dma((HEADS,)),
                dma((2,)),
                dma((2,)),
            ],
            compiler_params=params(2),
        )(
            node_feat,
            res_one,
            att,
            out_grad,
            out_w,
            ffn_w1,
            row(ffn_b1),
            ffn_w2,
            row(norm1_gain),
            row(norm2_gain),
            row(norm2_bias),
            row(norm3_gain),
            row(norm3_bias),
            mixed,
            hidden,
            slopes,
            graph_len,
            edge_step,
            gine_w1,
            gine_w2,
        )
    )

    back, heads, sums = pl.pallas_call(
        functools.partial(attend_back_kernel, count, cores, 1024, 512),
        out_shape=(
            shape((HEADS, 3 * HDIM, rows), bf16),
            shape((HEADS, 3 * HDIM, width), bf16),
            shape((HEADS, share, width), bf16),
        ),
        in_specs=[smem] + [vmem] * 7,
        out_specs=(vmem,) * 3,
        scratch_shapes=[
            pltpu.VMEM((all_rows, 128), bf16),
            pltpu.VMEM((all_rows, 128), bf16),
            pltpu.VMEM((128, plane_rows), bf16),
            pltpu.VMEM((128, plane_rows), bf16),
            pltpu.VMEM((HDIM, all_rows), bf16),
            pltpu.VMEM((HDIM, plane_rows), bf16),
            pltpu.VMEM((HDIM, plane_rows), bf16),
            pltpu.VMEM((HDIM, plane_rows), f32),
            pltpu.VMEM((count, 2 * HDIM, rows), bf16),
            pltpu.VMEM((planes, HEADS, 2 * HDIM, rows), bf16),
            pltpu.VMEM((HEADS, 3 * HDIM, rows), bf16),
            pltpu.VMEM((HEADS, rows, width), bf16),
            pltpu.VMEM((HEADS, share, width), bf16),
            pltpu.VMEM((share, width), bf16),
            pltpu.VMEM((planes, share // planes, width), bf16),
            pltpu.VMEM((planes, share // planes, width), bf16),
            pltpu.VMEM((3 * HDIM, width), bf16),
            pltpu.VMEM((planes, 3 * HDIM, width), bf16),
        ]
        + [dma((HEADS,))] * 4
        + [dma((2, planes))] * 2
        + [dma((HEADS,))] * 2
        + [dma((planes,))] * 2
        + [dma((HEADS,))] * 2
        + [dma((2, max(planes, HEADS)))] * 2,
        compiler_params=params(3),
    )(graph_len, q, kv, att, logs, grad_att, node_feat, parts)

    square = shape((width, width), f32)
    result, node_grad, gw1, gb1, gw2, qw, kw, vw, ow, f1, f2 = pl.pallas_call(
        finish_kernel,
        out_shape=(
            shape((rows, width), bf16),
            shape((rows, width), f32),
            square,
            shape((1, width), f32),
            square,
            square,
            square,
            square,
            square,
            shape((width, ffn), f32),
            shape((ffn, width), f32),
        ),
        in_specs=[vmem] * 8,
        out_specs=(vmem,) * 11,
        compiler_params=params(),
    )(query_w, key_w, value_w, grad_part, back, heads, sums.reshape(part_rows, width), result)
    gb1 = gb1.reshape(width)
    fb = vectors[5:7].reshape(ffn)
    return (
        result,
        node_grad,
        gw1,
        gb1,
        gw2,
        qw,
        kw,
        vw,
        ow,
        f1,
        fb,
        f2,
        vectors[0],
        vectors[1],
        vectors[2],
        vectors[3],
        vectors[4],
    )


def solution(mesh):
    count = mesh.shape["blk"] * mesh.shape["rep"]
    rows = P(AXES, None)
    whole = P()
    return jax.shard_map(
        functools.partial(on_device, count, mesh.shape["rep"]),
        mesh=mesh,
        in_specs=(rows, P(AXES, None, None), rows, P(AXES)) + (whole,) * 16 + (rows,),
        out_specs=(rows, rows) + (whole,) * 15,
        check_vma=False,
    )
```

```python
import functools
import jax
import jax.numpy as jnp
from jax import lax
from jax.experimental import pallas as pl
from jax.experimental.pallas import tpu as pltpu
from jax.sharding import PartitionSpec as P

HEADS = 8
HDIM = 32
EDGES = 8
GRAPHS = 9
AXES = ("blk", "rep")
MESH = pl.DeviceIdType.MESH
bf16 = jnp.bfloat16
f32 = jnp.float32

norm_eps = 1e-05
far_score = -1e30
log2_e = 1.4426950408889634
score_scale = HDIM ** (-0.5)
gelu_c = 0.7978845608028654
gelu_a = 0.044715


def dot(left, right, left_dim=1, right_dim=0):
    return lax.dot_general(
        left, right, (((left_dim,), (right_dim,)), ((), ())), preferred_element_type=f32
    )


def gelu(v):
    return 0.5 * v * (1.0 + jnp.tanh(gelu_c * (v + gelu_a * (v * v * v))))


def gelu_slope(v):
    squared = v * v
    bend = jnp.tanh(gelu_c * v * (1.0 + gelu_a * squared))
    return 0.5 * (1.0 + bend) + 0.5 * v * (1.0 - bend * bend) * (
        gelu_c * (1.0 + 3.0 * gelu_a * squared)
    )


def three_parts(v):
    first = v.astype(bf16)
    rest = v - first.astype(f32)
    second = rest.astype(bf16)
    third = (rest - second.astype(f32)).astype(bf16)
    return first, second, third


class Place:
    def __init__(self, count, cores):
        self.count = count
        self.cores = cores
        self.planes = count // HEADS
        self.me = lax.axis_index("blk") * cores + lax.axis_index("rep")
        self.z = lax.div(self.me, HEADS)
        self.p = lax.rem(self.me, HEADS)

    def device(self, index):
        return {"blk": lax.div(index, self.cores), "rep": lax.rem(index, self.cores)}

    def in_plane(self, k):
        return self.z * HEADS + lax.rem(self.p + k, HEADS)

    def plane_at(self, k):
        return flipped(self.z, k, self.planes)

    def along(self, k):
        return self.plane_at(k) * HEADS + self.p

    def mirrored(self, k):
        return flipped(self.me, k, self.count)

    def greet(self):
        def hello(k, _):
            pl.semaphore_signal(
                pltpu.get_barrier_semaphore(),
                inc=1,
                device_id=self.device(self.mirrored(k)),
                device_id_type=MESH,
            )
            return 0

        lax.fori_loop(1, self.count, hello, 0, unroll=self.count <= 32)

    def greeted(self):
        pl.semaphore_wait(pltpu.get_barrier_semaphore(), self.count - 1)

    def copy(self, src, dst, send_sem, recv_sem, peer):
        return pltpu.make_async_remote_copy(
            src_ref=src,
            dst_ref=dst,
            send_sem=send_sem,
            recv_sem=recv_sem,
            device_id=self.device(peer),
            device_id_type=MESH,
        )

    def to_plane(self, src_of, dst, sems):
        copies = []
        for k in range(1, HEADS):
            spot = lax.rem(self.p + k, HEADS)
            c = self.copy(src_of(spot), dst, sems.at[0, k], sems.at[1, k], self.in_plane(k))
            c.start()
            copies.append(c)
        return copies

    def to_line(self, src_of, dst_of, sems):
        copies = []
        for k in range(1, self.planes):
            c = self.copy(
                src_of(self.plane_at(k)), dst_of(k), sems.at[0, k], sems.at[1, k], self.along(k)
            )
            c.start()
            copies.append(c)
        return copies


def flipped(index, k, size):
    out, bit = 0, 1
    while bit < size:
        mine = lax.rem(lax.div(index, bit), 2)
        flip = lax.rem(lax.div(k, bit), 2) if not isinstance(k, int) else (k // bit) % 2
        if isinstance(flip, int):
            out = out + bit * (1 - mine if flip else mine)
        else:
            out = out + bit * (mine + flip - 2 * mine * flip)
        bit *= 2
    return out


def wait_all(copies):
    for c in copies:
        c.wait()


def part_of(ref, spot, size):
    return ref.at[pl.ds(pl.multiple_of(spot * size, size), size)]


def total_of(ref, start=0):
    total = ref[start].astype(f32)
    for k in range(start + 1, ref.shape[0]):
        total = total + ref[k].astype(f32)
    return total


def col_sum(v):
    return jnp.sum(v, axis=0, keepdims=True)


def stack_rows(rows, width):
    return jnp.concatenate(rows + [jnp.zeros((8 - len(rows), width), f32)], axis=0)


def graph_bounds(len_ref, positions):
    last = 0
    graph = jnp.zeros(positions.shape, jnp.int32)
    start = jnp.zeros(positions.shape, jnp.int32)
    ends = []
    for g in range(GRAPHS):
        last = last + len_ref[g]
        ends.append(last)
        passed = positions >= last
        graph = graph + passed.astype(jnp.int32)
        start = jnp.where(passed, last, start)
    stop = jnp.full(positions.shape, ends[-1], jnp.int32)
    for end in reversed(ends):
        stop = jnp.where(positions < end, end, stop)
    return graph, start, stop


def own_graph(len_ref, first, width):
    positions = first + lax.broadcasted_iota(jnp.int32, (1, width), 1)
    graph, _, _ = graph_bounds(len_ref, positions)
    rows = lax.broadcasted_iota(jnp.int32, (16, width), 0)
    return rows == graph


def as_columns(rows, width):
    return jnp.concatenate([rows, jnp.zeros((128 - rows.shape[0], width), f32)], axis=0).T


def gelu_and_slope(v):
    squared = v * v
    bend = jnp.tanh(gelu_c * v * (1.0 + gelu_a * squared))
    half = 0.5 * (1.0 + bend)
    slope = half + 0.5 * v * (1.0 - bend * bend) * (gelu_c * (1.0 + 3.0 * gelu_a * squared))
    return v * half, slope


class Refs:
    def __init__(self, names, refs):
        for name, ref in zip(names, refs, strict=True):
            setattr(self, name, ref)


def share_stats(place, stats, buffer, sems, between):
    buffer[place.me] = stats

    def begin(k, _):
        far = place.count - 1 - k
        place.copy(
            buffer.at[place.me],
            buffer.at[place.me],
            sems.at[0, far],
            sems.at[1, far],
            place.mirrored(far),
        ).start()
        return 0

    def finish(k, _):
        peer = place.mirrored(k)
        place.copy(
            buffer.at[place.me], buffer.at[peer], sems.at[0, k], sems.at[1, k], peer
        ).wait()
        return 0

    lax.fori_loop(0, place.count - 1, begin, 0, unroll=place.count <= 32)
    between()
    lax.fori_loop(1, place.count, finish, 0, unroll=place.count <= 32)
    return buffer[...]


def project(r, place):
    rows, width = r.x.shape
    count = place.count
    x = r.x[...]
    r.ext[0:rows, :] = jnp.zeros_like(x)
    r.ext[rows : 2 * rows, :] = x
    r.ext[2 * rows :, :] = jnp.zeros_like(x)
    r.edge_got[...] = jnp.zeros_like(r.edge_got)
    place.greet()
    xt = x.T
    kt = dot(r.wk[...].T, xt).astype(bf16)
    vt = dot(r.wv[...].T, xt).astype(bf16)
    for h in range(HEADS):
        cols = slice(HDIM * h, HDIM * (h + 1))
        r.kv_send[h, 0:HDIM] = kt[cols]
        r.kv_send[h, HDIM : 2 * HDIM] = vt[cols]
    qt = dot(r.wq[...].T, xt).astype(bf16)
    for h in range(HEADS):
        r.q_send[h] = qt[HDIM * h : HDIM * (h + 1)]
    place.greeted()

    def send_kv(index, _):
        dz = lax.div(index, HEADS)
        dp = lax.rem(index, HEADS)
        spot = lax.rem(place.p + dp, HEADS)
        place.copy(
            r.kv_send.at[spot],
            r.kv.at[place.me],
            r.kv_sems.at[0, index],
            r.kv_sems.at[1, index],
            flipped(place.z, dz, place.planes) * HEADS + spot,
        ).start()
        return 0

    lax.fori_loop(1, HEADS, send_kv, 0, unroll=True)
    q_copies = place.to_plane(lambda spot: r.q_send.at[spot], r.q.at[place.p], r.q_sems)
    up, down = halo(r, place, r.x, r.x, r.ext.at[pl.ds(0, rows)], r.ext.at[pl.ds(2 * rows, rows)])
    start_halo(place, up, down)
    lax.fori_loop(HEADS, count, send_kv, 0, unroll=count <= 32)
    r.kv[place.me] = r.kv_send[place.p]
    r.q[place.p] = r.q_send[place.p]
    return q_copies, (up, down)


def halo(r, place, up_src, down_src, up_dst, down_dst, which=0):
    after = lax.rem(place.me + 1, place.count)
    before = lax.rem(place.me + place.count - 1, place.count)
    up = place.copy(up_src, up_dst, r.halo_sems.at[which, 0], r.halo_sems.at[which, 1], after)
    down = place.copy(
        down_src, down_dst, r.halo_sems.at[which, 2], r.halo_sems.at[which, 3], before
    )
    return up, down


def start_halo(place, up, down):
    @pl.when(place.me < place.count - 1)
    def send_up():
        up.start()

    @pl.when(place.me > 0)
    def send_down():
        down.start()


def wait_halo(place, up, down):
    @pl.when(place.me < place.count - 1)
    def with_after():
        up.wait_send()
        down.wait_recv()

    @pl.when(place.me > 0)
    def with_before():
        down.wait_send()
        up.wait_recv()


def gine_forward(r, place):
    rows, width = r.x.shape
    positions = place.me * rows + lax.broadcasted_iota(jnp.int32, (1, rows), 1)
    _, start, stop = graph_bounds(r.graph_len, positions)
    source = jnp.minimum(jnp.maximum(positions + r.step[...], start), stop - 1)
    source = source - place.me * rows + rows
    r.source[...] = source
    columns = as_columns(
        jnp.concatenate([source.astype(f32), r.degree[...].astype(f32)], axis=0), rows
    )
    cells = lax.broadcasted_iota(jnp.int32, (rows, 3 * rows), 1).astype(f32)
    x = r.x[...].astype(f32)
    message = jnp.zeros_like(x)
    around = r.ext[...]
    for k in range(EDGES):
        select = (columns[:, k : k + 1] == cells).astype(f32).astype(bf16)
        v = dot(select, around) + r.edge[:, k, :].astype(f32)
        present = columns[:, EDGES : EDGES + 1] > k
        value, slope = gelu_and_slope(v)
        message = message + jnp.where(present, value, 0.0)
        r.slopes[k] = jnp.where(present, slope, 0.0)
    mixed = (x + message).astype(bf16)
    r.mixed[...] = mixed
    hidden = dot(mixed, r.w1[...]) + r.b1[...]
    value, slope = gelu_and_slope(hidden)
    active = value.astype(bf16)
    r.active[...] = active
    r.hidden_slope[...] = slope
    r.res_one[...] = x + dot(active, r.w2[...])


def build_keys(r, plane):
    cols = r.q.shape[2]
    for b in range(HEADS):
        block = plane * HEADS + b
        kt = r.kv[block, 0:HDIM]
        same = own_graph(r.graph_len, block * cols, cols).astype(f32).astype(bf16)
        ones = jnp.ones((16, cols), bf16)
        r.keys[b * cols : (b + 1) * cols, :] = jnp.concatenate([kt, kt, kt, same, ones], axis=0).T


def build_queries(r, place, last_rows):
    cols = r.q.shape[2]
    for b in range(HEADS):
        parts = three_parts(r.q[b].astype(f32) * (score_scale * log2_e))
        same = own_graph(r.graph_len, (place.z * HEADS + b) * cols, cols)
        known = lax.broadcasted_iota(jnp.int32, (16, cols), 0) < GRAPHS
        mask = jnp.where(jnp.logical_or(same, jnp.logical_not(known)), 0.0, far_score).astype(bf16)
        r.queries[:, b * cols : (b + 1) * cols] = jnp.concatenate(
            list(parts) + [mask, last_rows(b)], axis=0
        )


def attend(r, place, tile):
    cols = r.q.shape[2]
    width = HEADS * cols
    build_queries(r, place, lambda b: jnp.zeros((16, cols), bf16))
    r.total[...] = jnp.zeros_like(r.total)
    r.top[...] = jnp.full(r.top.shape, 2.0 * far_score, f32)

    def plane_step(dz, _):
        plane = flipped(place.z, dz, place.planes)

        def arrived(dp, _):
            spot = lax.rem(place.p + dp, HEADS)
            c = place.copy(
                r.kv_send.at[spot],
                r.kv.at[plane * HEADS + lax.rem(place.p + HEADS - dp, HEADS)],
                r.kv_sems.at[0, dz * HEADS + dp],
                r.kv_sems.at[1, dz * HEADS + dp],
                plane * HEADS + spot,
            )
            c.wait()
            return 0

        @pl.when(dz > 0)
        def first_of_plane():
            arrived(0, 0)

        lax.fori_loop(1, HEADS, arrived, 0, unroll=True)
        build_keys(r, plane)
        keys = r.keys[...]
        values = jnp.concatenate(
            [
                jnp.concatenate(
                    [r.kv[plane * HEADS + b, HDIM : 2 * HDIM] for b in range(HEADS)], axis=1
                ),
                jnp.ones((16, width), bf16),
            ],
            axis=0,
        )

        def ahead(i):
            return dot(keys, r.queries[:, i * tile : (i + 1) * tile])

        def behind(i, scores):
            qs = slice(i * tile, (i + 1) * tile)
            before = r.top[0:1, qs]
            now = jnp.maximum(before, jnp.max(scores, axis=0, keepdims=True))
            weights = jnp.exp2(scores - now).astype(bf16)
            r.total[:, qs] = r.total[:, qs] * jnp.exp2(before - now) + dot(values, weights)
            r.top[0:1, qs] = now

        tiles = width // tile
        current = ahead(0)
        for i in range(tiles):
            following = ahead(i + 1) if i + 1 < tiles else None
            behind(i, current)
            current = following
        return 0

    lax.fori_loop(0, place.planes, plane_step, 0)
    sums = r.total[HDIM : HDIM + 1, :]
    r.logs[0:1, :] = r.top[0:1, :] + jnp.log2(sums)
    attended = r.total[0:HDIM, :] / sums
    r.attended[...] = attended
    for b in range(HEADS):
        r.att_send[b] = attended[:, b * cols : (b + 1) * cols].astype(bf16)


def norms(r, place):
    rows, width = r.x.shape
    count = place.count
    total_rows = rows * count
    copies = place.to_plane(lambda spot: r.att_send.at[spot], r.att_got.at[place.p], r.att_sems)
    r.att_got[place.p] = r.att_send[place.p]
    source = r.source[...]
    cells = lax.broadcasted_iota(jnp.int32, (3 * rows, rows), 0)
    for k in range(EDGES):
        r.selects[k] = (source[k : k + 1, :] == cells).astype(f32).astype(bf16)
    x = r.x[...].astype(f32)
    res_one = r.res_one[...]

    def centre(v):
        mean = col_sum(v) / rows
        off = v - mean
        return mean, col_sum(off * off)

    def combine(means, squares):
        mean = jnp.sum(means, axis=0, keepdims=True) / count
        off = means - mean
        var = (
            jnp.sum(squares, axis=0, keepdims=True)
            + rows * jnp.sum(off * off, axis=0, keepdims=True)
        ) / total_rows
        return mean, lax.rsqrt(var + norm_eps)

    first_stats = centre(res_one)
    wait_all(copies)
    att_half = jnp.concatenate([r.att_got[h] for h in range(HEADS)], axis=0)
    res_two = x + dot(att_half.T, r.out_w[...])

    def nothing():
        pass

    stats = share_stats(
        place,
        stack_rows([*first_stats, *centre(res_two)], width),
        r.stat0,
        r.stat_sems.at[0],
        nothing,
    )
    mean_one, inv_one = combine(stats[:, 0, :], stats[:, 1, :])
    mean_two, inv_two = combine(stats[:, 2, :], stats[:, 3, :])
    normed_one = (res_one - mean_one) * inv_one
    normed_two = (res_two - mean_two) * inv_two
    summed = r.g1[...] * normed_one + (r.g2[...] * normed_two + r.b2[...])
    summed_half = summed.astype(bf16)
    ffn_hidden = dot(summed_half, r.f1[...]) + r.fb[...]
    value, ffn_slope = gelu_and_slope(ffn_hidden)
    ffn_active = value.astype(bf16)
    res_three = summed + dot(ffn_active, r.f2[...])
    upstream = r.up[...].astype(f32)
    mean_here, squares_here = centre(res_three)
    stats = share_stats(
        place,
        stack_rows(
            [
                mean_here,
                squares_here,
                col_sum(upstream),
                col_sum(upstream * (res_three - mean_here)),
            ],
            width,
        ),
        r.stat1,
        r.stat_sems.at[1],
        nothing,
    )
    mean_three, inv_three = combine(stats[:, 0, :], stats[:, 1, :])
    normed_three = (res_three - mean_three) * inv_three
    bias_three = jnp.sum(stats[:, 2, :], axis=0, keepdims=True)
    gain_three = inv_three * jnp.sum(
        stats[:, 3, :] + (stats[:, 0, :] - mean_three) * stats[:, 2, :], axis=0, keepdims=True
    )
    g3 = r.g3[...]

    def norm_back(up, normed, inv, gain, bias_sum, gain_sum):
        return inv * (
            gain * up - gain * bias_sum / total_rows - normed * (gain * gain_sum / total_rows)
        )

    grad_three = norm_back(upstream, normed_three, inv_three, g3, bias_three, gain_three)
    grad_ffn = grad_three.astype(bf16)
    grad_hidden = (ffn_slope * dot(grad_ffn, r.f2[...], 1, 1)).astype(bf16)
    grad_summed = grad_three + dot(grad_hidden, r.f1[...], 1, 1)
    fb_part = col_sum(grad_hidden.astype(f32))

    def ffn_parts():
        r.result[...] = (g3 * normed_three + r.b3[...]).astype(bf16)
        f1_part = dot(summed_half.T, grad_hidden).astype(bf16)
        r.parts[3 * width : 4 * width, :] = f1_part[:, :width]
        r.parts[4 * width : 5 * width, :] = f1_part[:, width:]
        f2_part = dot(ffn_active.T, grad_ffn).astype(bf16)
        r.parts[5 * width : 5 * width + f2_part.shape[0], :] = f2_part

    stats = share_stats(
        place,
        stack_rows(
            [
                col_sum(grad_summed),
                col_sum(grad_summed * normed_one),
                col_sum(grad_summed * normed_two),
                fb_part[:, :width],
                fb_part[:, width:],
            ],
            width,
        ),
        r.stat2,
        r.stat_sems.at[2],
        ffn_parts,
    )
    sums = jnp.sum(stats, axis=0)
    bias_sum, gain_one, gain_two = sums[0:1], sums[1:2], sums[2:3]
    grad_second = norm_back(grad_summed, normed_two, inv_two, r.g2[...], bias_sum, gain_two)
    grad_global = grad_second.astype(bf16)
    grad_att = dot(r.out_w[...], grad_global, 1, 1).astype(bf16)
    for h in range(HEADS):
        r.do_send[h] = grad_att[HDIM * h : HDIM * (h + 1)]
    do_copies = place.to_plane(lambda spot: r.do_send.at[spot], r.do.at[place.p], r.do_sems)
    r.do[place.p] = r.do_send[place.p]
    x_copies = place.to_plane(lambda spot: r.x, r.x_all.at[place.p], r.x_sems)
    r.x_all[place.p] = r.x[...]

    grad_first = norm_back(grad_summed, normed_one, inv_one, r.g1[...], bias_sum, gain_one)
    grad_local = grad_first.astype(bf16)
    grad_one = (r.hidden_slope[...] * dot(grad_local, r.w2[...], 1, 1)).astype(bf16)
    grad_mixed = dot(grad_one, r.w1[...], 1, 1)
    r.parts[2 * width : 3 * width, :] = dot(att_half, grad_global).astype(bf16)
    r.parts[width : 2 * width, :] = dot(r.active[...].T, grad_local).astype(bf16)
    r.parts[0:width, :] = dot(r.mixed[...].T, grad_one).astype(bf16)
    at = 5 * width + r.f2.shape[0]
    gb_part = col_sum(grad_one.astype(f32))
    r.parts[at : at + 16, :] = jnp.broadcast_to(gb_part, (16, width)).astype(bf16)
    r.parts[at + 16 :, :] = jnp.zeros((r.parts.shape[0] - at - 16, width), bf16)
    share = r.parts.shape[0] // HEADS
    parts_copies = place.to_plane(
        lambda spot: part_of(r.parts, spot, share), r.parts_got.at[place.p], r.parts_sems
    )
    r.parts_got[place.p] = part_of(r.parts, place.p, share)[...]
    r.vectors[...] = jnp.concatenate(
        [gain_one, gain_two, bias_sum, gain_three, bias_three, sums[3:5], gb_part], axis=0
    )
    back = jnp.zeros((3 * rows, width), f32)
    for k in range(EDGES):
        back = back + dot(r.selects[k], (r.slopes[k] * grad_mixed).astype(bf16))
    r.edge_send[0] = back[2 * rows :].astype(bf16)
    r.edge_send[1] = back[:rows].astype(bf16)
    up, down = halo(
        r, place, r.edge_send.at[0], r.edge_send.at[1], r.edge_got.at[0], r.edge_got.at[1], 1
    )
    r.grad[...] = grad_first + grad_second + grad_mixed + back[rows : 2 * rows]
    return do_copies, x_copies, parts_copies, (up, down)


def spread(v):
    cols = v.shape[1]
    parts = [part.astype(f32) for part in three_parts(v)]
    row = lax.broadcasted_iota(jnp.int32, (16, cols), 0)
    out = jnp.where(row == 0, parts[0], 0.0)
    out = jnp.where(row == 1, parts[1], out)
    return jnp.where(row == 2, parts[2], out).astype(bf16)


def attend_back(r, place, tile, do_copies, x_copies, parts_copies, halo_copies):
    planes = place.planes
    cols = r.q.shape[2]
    width = HEADS * cols
    share = r.parts.shape[0] // HEADS
    slice_rows = share // planes
    build_queries(
        r, place, lambda b: spread(-r.logs[0:1, b * cols : (b + 1) * cols])
    )
    wait_all(do_copies)
    for b in range(HEADS):
        qs = slice(b * cols, (b + 1) * cols)
        grad = r.do[b].astype(f32)
        inner = jnp.sum(grad * r.attended[:, qs], axis=0, keepdims=True) * score_scale
        r.grads[:, qs] = jnp.concatenate(
            list(three_parts(grad * score_scale)) + [spread(-inner), jnp.zeros((16, cols), bf16)],
            axis=0,
        )
    query_rows = jnp.concatenate([r.q[b] for b in range(HEADS)], axis=1)
    r.query_rows[...] = query_rows
    r.grad_rows[...] = jnp.concatenate([r.do[b] for b in range(HEADS)], axis=1)
    r.dq_total[...] = jnp.zeros_like(r.dq_total)

    def plane_of_keys(plane):
        build_keys(r, plane)
        for b in range(HEADS):
            vt = r.kv[plane * HEADS + b, HDIM : 2 * HDIM]
            r.values[b * cols : (b + 1) * cols, :] = jnp.concatenate(
                [vt, vt, vt, jnp.ones((HDIM, cols), bf16)], axis=0
            ).T
        keys = r.keys[...]
        values = r.values[...]
        key_t = jnp.concatenate([r.kv[plane * HEADS + b, 0:HDIM] for b in range(HEADS)], axis=1)

        def ahead(i):
            qs = slice(i * tile, (i + 1) * tile)
            return dot(keys, r.queries[:, qs]), dot(values, r.grads[:, qs])

        def behind(i, state, products):
            dk, dv = state
            qs = slice(i * tile, (i + 1) * tile)
            probs = jnp.exp2(products[0])
            half = probs.astype(bf16)
            grad_scores = (probs * products[1]).astype(bf16)
            r.dq_total[:, qs] += dot(key_t, grad_scores)
            return (
                dk + dot(r.query_rows[:, qs], grad_scores, 1, 1),
                dv + dot(r.grad_rows[:, qs], half, 1, 1),
            )

        state = (jnp.zeros((HDIM, width), f32),) * 2
        tiles = width // tile
        current = ahead(0)
        for i in range(tiles):
            following = ahead(i + 1) if i + 1 < tiles else None
            state = behind(i, state, current)
            current = following
        for b in range(HEADS):
            part = slice(b * cols, (b + 1) * cols)
            r.dkv_part[plane * HEADS + b] = jnp.concatenate(
                [state[0][:, part], state[1][:, part]], axis=0
            ).astype(bf16)

    def dkv_copy(k):
        return place.copy(
            part_of(r.dkv_part, place.plane_at(k), HEADS),
            r.dkv_got.at[k],
            r.dkv_sems.at[0, k],
            r.dkv_sems.at[1, k],
            place.along(k),
        )

    def line_start(k, which, src, dst):
        place.copy(
            src, dst, r.line_sems.at[which, 0, k], r.line_sems.at[which, 1, k], place.along(k)
        ).start()

    def slice_copies():
        return [
            place.copy(
                part_of(r.plane_sum, place.plane_at(k), slice_rows),
                r.line_got.at[k],
                r.line_sems.at[0, 0, k],
                r.line_sems.at[0, 1, k],
                place.along(k),
            )
            for k in range(1, planes)
        ]

    def line_copies():
        return [
            place.copy(
                r.line_sum.at[place.z],
                r.line_sum.at[place.z],
                r.line_sems.at[1, 0, k],
                r.line_sems.at[1, 1, k],
                place.along(k),
            )
            for k in range(1, planes)
        ]

    def whole_copies():
        return [
            place.copy(
                r.sums.at[place.p],
                r.sums.at[place.p],
                r.whole_sems.at[0, k],
                r.whole_sems.at[1, k],
                place.in_plane(k),
            )
            for k in range(1, HEADS)
        ]

    def start_all(copies):
        for c in copies:
            c.start()

    def plane_step(step, _):
        k = lax.rem(step + 1, planes)
        plane_of_keys(flipped(place.z, k, planes))

        @pl.when(k > 0)
        def send_part():
            dkv_copy(k).start()

        @pl.when(step == 0)
        def sum_plane():
            wait_all(parts_copies)
            start_halo(place, *halo_copies)
            r.plane_sum[...] = total_of(r.parts_got).astype(bf16)
            start_all(slice_copies())

        @pl.when(step == 1)
        def sum_line():
            wait_all(slice_copies())
            total = part_of(r.plane_sum, place.z, slice_rows)[...].astype(f32) + total_of(
                r.line_got, 1
            )
            r.line_sum[place.z] = total.astype(bf16)
            start_all(line_copies())

        @pl.when(step == 2)
        def spread_line():
            wait_all(line_copies())
            r.sums[place.p] = r.line_sum[...].reshape(share, cols)
            start_all(whole_copies())

        return 0

    lax.fori_loop(0, planes, plane_step, 0)
    wait_all(x_copies)
    for k in range(1, planes):
        dkv_copy(k).wait()
    dkv = part_of(r.dkv_part, place.z, HEADS)[...].astype(f32) + total_of(r.dkv_got, 1)
    for b in range(HEADS):
        r.back_send[b, 0:HDIM] = r.dq_total[:, b * cols : (b + 1) * cols].astype(bf16)
        r.back_send[b, HDIM : 3 * HDIM] = dkv[b].astype(bf16)
    back_copies = place.to_plane(
        lambda spot: r.back_send.at[spot], r.back.at[place.p], r.back_sems
    )
    r.back[place.p] = r.back_send[place.p]
    total = dot(r.back_send[0], r.x_all[0])
    for b in range(1, HEADS):
        total = total + dot(r.back_send[b], r.x_all[b])
    r.heads_part[...] = total.astype(bf16)
    heads_copies = place.to_line(
        lambda spot: r.heads_part, lambda k: r.heads_got.at[k], r.heads_sems
    )
    wait_halo(place, *halo_copies)
    grad = r.grad[...] + r.edge_got[0].astype(f32) + r.edge_got[1].astype(f32)
    wait_all(heads_copies)
    total = r.heads_part[...].astype(f32) + total_of(r.heads_got, 1)
    r.heads[place.p] = total.astype(bf16)
    last_copies = place.to_plane(
        lambda spot: r.heads.at[place.p], r.heads.at[place.p], r.last_sems
    )
    wait_all(back_copies)
    for s, w in enumerate((r.wq, r.wk, r.wv)):
        part = jnp.concatenate(
            [r.back[h, HDIM * s : HDIM * (s + 1)] for h in range(HEADS)], axis=0
        )
        grad = grad + dot(part.T, w[...], 1, 1)
    r.grad[...] = grad
    wait_all(whole_copies())
    wait_all(last_copies)


def layer_kernel(count, cores, names, *refs):
    r = Refs(names, refs)
    place = Place(count, cores)
    q_copies, halo_copies = project(r, place)
    wait_halo(place, *halo_copies)
    gine_forward(r, place)
    wait_all(q_copies)
    attend(r, place, 512)
    attend_back(r, place, 512, *norms(r, place))


def finish_kernel(
    grad_ref,
    heads_ref,
    sums_ref,
    result_ref,
    vectors_ref,
    result_out,
    grad_out,
    gw1_out,
    gb1_out,
    gw2_out,
    qw_out,
    kw_out,
    vw_out,
    ow_out,
    f1_out,
    fb_out,
    f2_out,
    gain1_out,
    gain2_out,
    bias2_out,
    gain3_out,
    bias3_out,
):
    width = grad_ref.shape[1]
    result_out[...] = result_ref[...]
    grad_out[...] = grad_ref[...]
    for s, w_out in enumerate((qw_out, kw_out, vw_out)):
        cols = slice(HDIM * s, HDIM * (s + 1))
        total = jnp.concatenate([heads_ref[h, cols] for h in range(HEADS)], axis=0)
        w_out[...] = total.T.astype(f32)
    gw1_out[...] = sums_ref[0:width].astype(f32)
    gw2_out[...] = sums_ref[width : 2 * width].astype(f32)
    ow_out[...] = sums_ref[2 * width : 3 * width].astype(f32)
    f1_out[:, 0:width] = sums_ref[3 * width : 4 * width].astype(f32)
    f1_out[:, width:] = sums_ref[4 * width : 5 * width].astype(f32)
    last = 5 * width + f2_out.shape[0]
    f2_out[...] = sums_ref[5 * width : last].astype(f32)
    gb1_out[...] = sums_ref[last : last + 16].astype(f32)[0:1]
    fb_out[:, 0:width] = vectors_ref[5:6]
    fb_out[:, width:] = vectors_ref[6:7]
    for k, out in enumerate((gain1_out, gain2_out, bias2_out, gain3_out, bias3_out)):
        out[...] = vectors_ref[k : k + 1]


def on_device(
    count,
    cores,
    node_feat,
    edge_feat,
    edge_step,
    degree,
    graph_len,
    gine_w1,
    gine_b1,
    gine_w2,
    query_w,
    key_w,
    value_w,
    out_w,
    ffn_w1,
    ffn_b1,
    ffn_w2,
    norm1_gain,
    norm2_gain,
    norm2_bias,
    norm3_gain,
    norm3_bias,
    out_grad,
):
    rows, width = node_feat.shape
    ffn = ffn_w1.shape[1]
    planes = count // HEADS
    plane_rows = HEADS * rows
    vmem = pl.BlockSpec(memory_space=pltpu.VMEM)
    smem = pl.BlockSpec(memory_space=pltpu.SMEM)
    dma = pltpu.SemaphoreType.DMA
    shape = jax.ShapeDtypeStruct
    share_unit = 16 * HEADS * planes
    needed = 3 * width + 2 * ffn + 16
    part_rows = -(-needed // share_unit) * share_unit
    share = part_rows // HEADS

    def row(v):
        return v.reshape(1, -1)

    args = dict(
        graph_len=graph_len,
        x=node_feat,
        wq=query_w,
        wk=key_w,
        wv=value_w,
        step=edge_step.T,
        degree=row(degree),
        edge=edge_feat,
        w1=gine_w1,
        b1=row(gine_b1),
        w2=gine_w2,
        up=out_grad,
        out_w=out_w,
        f1=ffn_w1,
        fb=row(ffn_b1),
        f2=ffn_w2,
        g1=row(norm1_gain),
        g2=row(norm2_gain),
        b2=row(norm2_bias),
        g3=row(norm3_gain),
        b3=row(norm3_bias),
    )
    outs = dict(
        result=shape((rows, width), bf16),
        grad=shape((rows, width), f32),
        vectors=shape((8, width), f32),
        heads=shape((HEADS, 3 * HDIM, width), bf16),
        sums=shape((HEADS, share, width), bf16),
    )
    scratch = dict(
        ext=pltpu.VMEM((3 * rows, width), bf16),
        kv_send=pltpu.VMEM((HEADS, 2 * HDIM, rows), bf16),
        q_send=pltpu.VMEM((HEADS, HDIM, rows), bf16),
        kv=pltpu.VMEM((count, 2 * HDIM, rows), bf16),
        q=pltpu.VMEM((HEADS, HDIM, rows), bf16),
        source=pltpu.VMEM((EDGES, rows), jnp.int32),
        slopes=pltpu.VMEM((EDGES, rows, width), f32),
        selects=pltpu.VMEM((EDGES, 3 * rows, rows), bf16),
        mixed=pltpu.VMEM((rows, width), bf16),
        active=pltpu.VMEM((rows, width), bf16),
        hidden_slope=pltpu.VMEM((rows, width), f32),
        res_one=pltpu.VMEM((rows, width), f32),
        keys=pltpu.VMEM((plane_rows, 128), bf16),
        values=pltpu.VMEM((plane_rows, 128), bf16),
        queries=pltpu.VMEM((128, plane_rows), bf16),
        grads=pltpu.VMEM((128, plane_rows), bf16),
        query_rows=pltpu.VMEM((HDIM, plane_rows), bf16),
        grad_rows=pltpu.VMEM((HDIM, plane_rows), bf16),
        total=pltpu.VMEM((HDIM + 16, plane_rows), f32),
        top=pltpu.VMEM((8, plane_rows), f32),
        logs=pltpu.VMEM((8, plane_rows), f32),
        attended=pltpu.VMEM((HDIM, plane_rows), f32),
        att_send=pltpu.VMEM((HEADS, HDIM, rows), bf16),
        att_got=pltpu.VMEM((HEADS, HDIM, rows), bf16),
        do_send=pltpu.VMEM((HEADS, HDIM, rows), bf16),
        do=pltpu.VMEM((HEADS, HDIM, rows), bf16),
        stat0=pltpu.VMEM((count, 8, width), f32),
        stat1=pltpu.VMEM((count, 8, width), f32),
        stat2=pltpu.VMEM((count, 8, width), f32),
        edge_send=pltpu.VMEM((2, rows, width), bf16),
        edge_got=pltpu.VMEM((2, rows, width), bf16),
        x_all=pltpu.VMEM((HEADS, rows, width), bf16),
        parts=pltpu.VMEM((part_rows, width), bf16),
        parts_got=pltpu.VMEM((HEADS, share, width), bf16),
        plane_sum=pltpu.VMEM((share, width), bf16),
        line_got=pltpu.VMEM((planes, share // planes, width), bf16),
        line_sum=pltpu.VMEM((planes, share // planes, width), bf16),
        dq_total=pltpu.VMEM((HDIM, plane_rows), f32),
        dkv_part=pltpu.VMEM((count, 2 * HDIM, rows), bf16),
        dkv_got=pltpu.VMEM((planes, HEADS, 2 * HDIM, rows), bf16),
        back_send=pltpu.VMEM((HEADS, 3 * HDIM, rows), bf16),
        back=pltpu.VMEM((HEADS, 3 * HDIM, rows), bf16),
        heads_part=pltpu.VMEM((3 * HDIM, width), bf16),
        heads_got=pltpu.VMEM((planes, 3 * HDIM, width), bf16),
        kv_sems=dma((2, count)),
        q_sems=dma((2, HEADS)),
        halo_sems=dma((2, 4)),
        att_sems=dma((2, HEADS)),
        do_sems=dma((2, HEADS)),
        stat_sems=dma((3, 2, count)),
        x_sems=dma((2, HEADS)),
        parts_sems=dma((2, HEADS)),
        line_sems=dma((2, 2, planes)),
        whole_sems=dma((2, HEADS)),
        dkv_sems=dma((2, planes)),
        back_sems=dma((2, HEADS)),
        heads_sems=dma((2, planes)),
        last_sems=dma((2, HEADS)),
    )
    result, grad, vectors, heads, sums = pl.pallas_call(
        functools.partial(layer_kernel, count, cores, (*args, *outs, *scratch)),
        out_shape=tuple(outs.values()),
        in_specs=[smem] + [vmem] * (len(args) - 1),
        out_specs=(vmem,) * len(outs),
        scratch_shapes=list(scratch.values()),
        compiler_params=pltpu.CompilerParams(
            vmem_limit_bytes=62 << 20, collective_id=1, has_side_effects=True
        ),
    )(*args.values())

    square = shape((width, width), f32)
    line = shape((1, width), f32)
    done = pl.pallas_call(
        finish_kernel,
        out_shape=(
            shape((rows, width), bf16),
            shape((rows, width), f32),
            square,
            line,
            square,
            square,
            square,
            square,
            square,
            shape((width, ffn), f32),
            shape((1, ffn), f32),
            shape((ffn, width), f32),
        )
        + (line,) * 5,
        in_specs=[vmem] * 5,
        out_specs=(vmem,) * 17,
        compiler_params=pltpu.CompilerParams(vmem_limit_bytes=60 << 20),
    )(grad, heads, sums.reshape(part_rows, width), result, vectors)
    return tuple(v.reshape(-1) if v.shape[0] == 1 else v for v in done)


def solution(mesh):
    count = mesh.shape["blk"] * mesh.shape["rep"]
    rows = P(AXES, None)
    whole = P()
    return jax.shard_map(
        functools.partial(on_device, count, mesh.shape["rep"]),
        mesh=mesh,
        in_specs=(rows, P(AXES, None, None), rows, P(AXES)) + (whole,) * 16 + (rows,),
        out_specs=(rows, rows) + (whole,) * 15,
        check_vma=False,
    )
```

```python
import functools
import jax
import jax.numpy as jnp
from jax import lax
from jax.experimental import pallas as pl
from jax.experimental.pallas import tpu as pltpu
from jax.sharding import PartitionSpec as P

HEADS = 8
HDIM = 32
EDGES = 8
GRAPHS = 9
AXES = ("blk", "rep")
MESH = pl.DeviceIdType.MESH
bf16 = jnp.bfloat16
f32 = jnp.float32

norm_eps = 1e-05
far_score = -1e30
log2_e = 1.4426950408889634
score_scale = HDIM ** (-0.5)
gelu_c = 0.7978845608028654
gelu_a = 0.044715


def dot(left, right, left_dim=1, right_dim=0):
    return lax.dot_general(
        left, right, (((left_dim,), (right_dim,)), ((), ())), preferred_element_type=f32
    )


def gelu(v):
    return 0.5 * v * (1.0 + jnp.tanh(gelu_c * (v + gelu_a * (v * v * v))))


def gelu_slope(v):
    squared = v * v
    bend = jnp.tanh(gelu_c * v * (1.0 + gelu_a * squared))
    return 0.5 * (1.0 + bend) + 0.5 * v * (1.0 - bend * bend) * (
        gelu_c * (1.0 + 3.0 * gelu_a * squared)
    )


def three_parts(v):
    first = v.astype(bf16)
    rest = v - first.astype(f32)
    second = rest.astype(bf16)
    third = (rest - second.astype(f32)).astype(bf16)
    return first, second, third


class Place:
    def __init__(self, count, cores):
        self.count = count
        self.cores = cores
        self.planes = count // HEADS
        self.blk = lax.axis_index("blk")
        self.rep = lax.axis_index("rep")
        self.me = self.blk * cores + self.rep
        self.z = lax.div(self.me, HEADS)
        self.p = self.me - self.z * HEADS
        self.chip = lax.div(self.p, 2)
        self.core = self.p - 2 * self.chip
        self.share = self.core * (HEADS // 2) + self.chip
        self.steps = []
        bit, rest = 1, self.me
        while bit < count:
            half = lax.div(rest, 2)
            self.steps.append(bit * (1 - 2 * (rest - 2 * half)))
            bit, rest = 2 * bit, half

    def move(self, k, first=0, last=None):
        total = 0
        for j, step in enumerate(self.steps[first:last]):
            bit = 1 << (first + j)
            if isinstance(k, int):
                if k & bit:
                    total = total + step
            else:
                total = total + lax.rem(lax.div(k, bit), 2) * step
        return total

    def device(self, k):
        low = self.cores.bit_length() - 1
        return {
            "blk": self.blk + lax.div(self.move(k, low), self.cores),
            "rep": self.rep + self.move(k, 0, low),
        }

    def peer(self, k):
        return self.me + self.move(k)

    def spot(self, k):
        return self.p + self.move(k, 0, 3)

    def plane(self, k):
        return self.z + lax.div(self.move(k * HEADS, 3), HEADS)

    def loop(self, first, last, body):
        if last - first <= 32:
            for k in range(first, last):
                body(k)
        else:

            def step(k, _):
                body(k)
                return 0

            lax.fori_loop(first, last, step, 0)

    def greet(self):
        def hello(k):
            pl.semaphore_signal(
                pltpu.get_barrier_semaphore(),
                inc=1,
                device_id=self.device(self.count - k),
                device_id_type=MESH,
            )

        self.loop(1, self.count, hello)

    def greeted(self):
        pl.semaphore_wait(pltpu.get_barrier_semaphore(), self.count - 1)

    def copy(self, src, dst, sems, k):
        return self.copy_to(src, dst, sems.at[0], sems.at[1], self.device(k))

    def copy_to(self, src, dst, send_sem, recv_sem, device):
        return pltpu.make_async_remote_copy(
            src_ref=src,
            dst_ref=dst,
            send_sem=send_sem,
            recv_sem=recv_sem,
            device_id=device,
            device_id_type=MESH,
        )

    def to_plane(self, src_of, dst, sems):
        for k in reversed(range(1, HEADS)):
            self.copy(src_of(self.spot(k)), dst, sems, k).start()

    def to_line(self, src_of, dst_of, sems):
        for k in range(1, self.planes):
            self.copy(src_of(self.plane(k)), dst_of(k), sems, k * HEADS).start()

    def to_chips(self, src_of, dst_of, sems):
        for k in range(1, HEADS // 2):
            there = self.chip + lax.div(self.move(2 * k, 1, 3), 2)
            self.copy(src_of(there), dst_of(k), sems, 2 * k).start()

    def wait(self, like, sems):
        self.copy(like, like, sems, 1).wait()


def part_of(ref, spot, size):
    return ref.at[pl.ds(pl.multiple_of(spot * size, size), size)]


def total_of(ref, start=0):
    total = ref[start].astype(f32)
    for k in range(start + 1, ref.shape[0]):
        total = total + ref[k].astype(f32)
    return total


def col_sum(v):
    return jnp.sum(v, axis=0, keepdims=True)


def stack_rows(rows, width):
    four = jnp.concatenate(rows + [jnp.zeros((1, width), f32)] * (4 - len(rows)), axis=0)
    return jnp.concatenate([four[:, : width // 2], four[:, width // 2 :]], axis=0)


def graph_bounds(len_ref, positions):
    last = 0
    graph = jnp.zeros(positions.shape, jnp.int32)
    start = jnp.zeros(positions.shape, jnp.int32)
    ends = []
    for g in range(GRAPHS):
        last = last + len_ref[g]
        ends.append(last)
        passed = positions >= last
        graph = graph + passed.astype(jnp.int32)
        start = jnp.where(passed, last, start)
    stop = jnp.full(positions.shape, ends[-1], jnp.int32)
    for end in reversed(ends):
        stop = jnp.where(positions < end, end, stop)
    return graph, start, stop


def own_graph(len_ref, first, width):
    positions = first + lax.broadcasted_iota(jnp.int32, (1, width), 1)
    graph, _, _ = graph_bounds(len_ref, positions)
    rows = lax.broadcasted_iota(jnp.int32, (16, width), 0)
    return rows == graph


def as_columns(rows, width):
    return jnp.concatenate([rows, jnp.zeros((128 - rows.shape[0], width), f32)], axis=0).T


def gelu_and_slope(v):
    squared = v * v
    bend = jnp.tanh(gelu_c * v * (1.0 + gelu_a * squared))
    half = 0.5 * (1.0 + bend)
    slope = half + 0.5 * v * (1.0 - bend * bend) * (gelu_c * (1.0 + 3.0 * gelu_a * squared))
    return v * half, slope


class Refs:
    def __init__(self, names, refs):
        for name, ref in zip(names, refs, strict=True):
            setattr(self, name, ref)

    def need(self, *names):
        for name in names:
            self.loads[name].wait()


def share_stats(place, stats, buffer, sems, between):
    buffer[place.me] = stats

    def begin(k):
        place.copy(buffer.at[place.me], buffer.at[place.me], sems, place.count - k).start()

    place.loop(1, place.count, begin)
    between()
    place.wait(buffer.at[pl.ds(0, place.count - 1)], sems)
    return jnp.concatenate([buffer[:, 0:4, :], buffer[:, 4:8, :]], axis=2)


def project(r, place):
    rows, width = r.x.shape
    count = place.count
    r.edge_got[...] = jnp.zeros_like(r.edge_got)
    r.need("x")
    x = r.x[...]
    r.ext[0:rows, :] = jnp.zeros_like(x)
    r.ext[rows : 2 * rows, :] = x
    r.ext[2 * rows :, :] = jnp.zeros_like(x)
    place.greet()
    xt = x.T
    r.need("wk", "wv", "wq")
    kt = dot(r.wk[...].T, xt).astype(bf16)
    vt = dot(r.wv[...].T, xt).astype(bf16)
    for h in range(HEADS):
        cols = slice(HDIM * h, HDIM * (h + 1))
        r.kv_send[h, 0:HDIM] = kt[cols]
        r.kv_send[h, HDIM : 2 * HDIM] = vt[cols]
    qt = dot(r.wq[...].T, xt).astype(bf16)
    for h in range(HEADS):
        r.q_send[h] = qt[HDIM * h : HDIM * (h + 1)]
    place.greeted()

    place.to_plane(lambda spot: r.kv_send.at[spot], r.kv.at[place.me], r.kv_sems.at[0, 0])
    place.to_plane(lambda spot: r.q_send.at[spot], r.q.at[place.p], r.q_sems)
    up, down = halo(r, place, r.x, r.x, r.ext.at[pl.ds(0, rows)], r.ext.at[pl.ds(2 * rows, rows)])
    r.kv[place.me] = r.kv_send[place.p]
    r.q[place.p] = r.q_send[place.p]
    return up, down


def pass_on(r, place, dz, bit, half):
    rows = part_of(r.kv, 2 * place.plane(dz) + half, HEADS // 2)
    place.copy(rows, rows, r.kv_sems.at[dz + bit, half], bit * HEADS).start()


def pass_down(r, place, dz, half):
    bit = 1
    while bit < place.planes // 2:
        pl.when(lax.rem(dz, 2 * bit) == 0)(functools.partial(pass_on, r, place, dz, bit, half))
        bit *= 2


def kv_arrived(r, place, dz, half):
    place.wait(r.kv.at[pl.ds(0, HEADS // 2)], r.kv_sems.at[dz, half])


def halo(r, place, up_src, down_src, up_dst, down_dst, which=0):
    def neighbour(index):
        blk = lax.div(index, place.cores)
        return {"blk": blk, "rep": index - blk * place.cores}

    sems = r.halo_sems.at[which]
    last = place.count - 1
    after = neighbour(jnp.minimum(place.me + 1, last))
    before = neighbour(jnp.maximum(place.me - 1, 0))
    up = place.copy_to(up_src, up_dst, sems.at[0], sems.at[1], after)
    down = place.copy_to(down_src, down_dst, sems.at[2], sems.at[3], before)
    return up, down


def start_halo(place, up, down):
    @pl.when(place.me < place.count - 1)
    def send_up():
        up.start()

    @pl.when(place.me > 0)
    def send_down():
        down.start()


def wait_halo(place, up, down):
    @pl.when(place.me < place.count - 1)
    def with_after():
        up.wait_send()
        down.wait_recv()

    @pl.when(place.me > 0)
    def with_before():
        down.wait_send()
        up.wait_recv()


def gine_forward(r, place):
    rows, width = r.x.shape
    positions = place.me * rows + lax.broadcasted_iota(jnp.int32, (1, rows), 1)
    _, start, stop = graph_bounds(r.graph_len, positions)
    source = jnp.minimum(jnp.maximum(positions + r.step[...], start), stop - 1)
    source = source - place.me * rows + rows
    r.source[...] = source
    columns = as_columns(
        jnp.concatenate([source.astype(f32), r.degree[...].astype(f32)], axis=0), rows
    )
    cells = lax.broadcasted_iota(jnp.int32, (rows, 3 * rows), 1).astype(f32)
    x = r.x[...].astype(f32)
    message = jnp.zeros_like(x)
    around = r.ext[...]
    for k in range(EDGES):
        select = (columns[:, k : k + 1] == cells).astype(f32).astype(bf16)
        v = dot(select, around) + r.edge[:, k, :].astype(f32)
        present = columns[:, EDGES : EDGES + 1] > k
        value, slope = gelu_and_slope(v)
        message = message + jnp.where(present, value, 0.0)
        r.slopes[k] = jnp.where(present, slope, 0.0)
    mixed = (x + message).astype(bf16)
    r.mixed[...] = mixed
    hidden = dot(mixed, r.w1[...]) + r.b1[...]
    value, slope = gelu_and_slope(hidden)
    active = value.astype(bf16)
    r.active[...] = active
    r.hidden_slope[...] = slope
    r.res_one[...] = x + dot(active, r.w2[...])


def build_keys(r, plane):
    cols = r.q.shape[2]
    for b in range(HEADS):
        block = plane * HEADS + b
        kt = r.kv[block, 0:HDIM]
        same = own_graph(r.graph_len, block * cols, cols).astype(f32).astype(bf16)
        ones = jnp.ones((16, cols), bf16)
        r.keys[b * cols : (b + 1) * cols, :] = jnp.concatenate([kt, kt, kt, same, ones], axis=0).T


def build_queries(r, place, last_rows):
    cols = r.q.shape[2]
    for b in range(HEADS):
        parts = three_parts(r.q[b].astype(f32) * (score_scale * log2_e))
        same = own_graph(r.graph_len, (place.z * HEADS + b) * cols, cols)
        known = lax.broadcasted_iota(jnp.int32, (16, cols), 0) < GRAPHS
        mask = jnp.where(jnp.logical_or(same, jnp.logical_not(known)), 0.0, far_score).astype(bf16)
        r.queries[:, b * cols : (b + 1) * cols] = jnp.concatenate(
            list(parts) + [mask, last_rows(b)], axis=0
        )


def attend(r, place, tile, halo_copies, beside):
    cols = r.q.shape[2]
    width = HEADS * cols
    place.wait(r.q.at[pl.ds(0, HEADS - 1)], r.q_sems)
    place.wait(r.kv.at[pl.ds(0, HEADS - 1)], r.kv_sems.at[0, 0])
    for half in range(2):
        bit = 1
        while bit < place.planes:
            pass_on(r, place, 0, bit, half)
            bit *= 2
    start_halo(place, *halo_copies)
    place.to_plane(lambda spot: r.x, r.x_all.at[place.p], r.x_sems)
    r.x_all[place.p] = r.x[...]
    build_queries(r, place, lambda b: jnp.zeros((16, cols), bf16))
    r.total[...] = jnp.zeros_like(r.total)
    r.top[...] = jnp.full(r.top.shape, 2.0 * far_score, f32)
    farthest = place.planes // 2

    def plane_step(dz, _):
        plane = place.plane(dz)

        @pl.when(jnp.logical_and(dz > 0, dz != farthest))
        def first_half():
            kv_arrived(r, place, dz, 0)
            pass_down(r, place, dz, 0)

        @pl.when(dz > 0)
        def second_half():
            kv_arrived(r, place, dz, 1)
            pass_down(r, place, dz, 1)

        build_keys(r, plane)
        keys = r.keys[...]
        values = jnp.concatenate(
            [
                jnp.concatenate(
                    [r.kv[plane * HEADS + b, HDIM : 2 * HDIM] for b in range(HEADS)], axis=1
                ),
                jnp.ones((16, width), bf16),
            ],
            axis=0,
        )

        def ahead(i):
            return dot(keys, r.queries[:, i * tile : (i + 1) * tile])

        def behind(i, scores):
            qs = slice(i * tile, (i + 1) * tile)
            before = r.top[0:1, qs]
            now = jnp.maximum(before, jnp.max(scores, axis=0, keepdims=True))
            weights = jnp.exp2(scores - now).astype(bf16)
            r.total[:, qs] = r.total[:, qs] * jnp.exp2(before - now) + dot(values, weights)
            r.top[0:1, qs] = now

        tiles = width // tile
        current = ahead(0)
        for i in range(tiles):
            following = ahead(i + 1) if i + 1 < tiles else None
            behind(i, current)
            current = following

        @pl.when(dz == 0)
        def after_own():
            beside()
            kv_arrived(r, place, farthest, 0)
            pass_down(r, place, farthest, 0)

        return 0

    lax.fori_loop(0, place.planes, plane_step, 0)
    sums = r.total[HDIM : HDIM + 1, :]
    r.logs[0:1, :] = r.top[0:1, :] + jnp.log2(sums)
    attended = r.total[0:HDIM, :] / sums
    r.attended[...] = attended
    for b in range(HEADS):
        r.att_send[b] = attended[:, b * cols : (b + 1) * cols].astype(bf16)


def norms(r, place):
    rows, width = r.x.shape
    count = place.count
    total_rows = rows * count
    place.to_plane(lambda spot: r.att_send.at[spot], r.att_got.at[place.p], r.att_sems)
    r.att_got[place.p] = r.att_send[place.p]
    source = r.source[...]
    cells = lax.broadcasted_iota(jnp.int32, (3 * rows, rows), 0)
    for k in range(EDGES):
        r.selects[k] = (source[k : k + 1, :] == cells).astype(f32).astype(bf16)
    x = r.x[...].astype(f32)
    res_one = r.res_one[...]

    def centre(v):
        mean = col_sum(v) / rows
        off = v - mean
        return mean, col_sum(off * off)

    def combine(means, squares):
        mean = jnp.sum(means, axis=0, keepdims=True) / count
        off = means - mean
        var = (
            jnp.sum(squares, axis=0, keepdims=True)
            + rows * jnp.sum(off * off, axis=0, keepdims=True)
        ) / total_rows
        return mean, lax.rsqrt(var + norm_eps)

    first_stats = centre(res_one)
    place.wait(r.att_got.at[pl.ds(0, HEADS - 1)], r.att_sems)
    att_half = jnp.concatenate([r.att_got[h] for h in range(HEADS)], axis=0)
    res_two = x + dot(att_half.T, r.out_w[...])

    def nothing():
        pass

    stats = share_stats(
        place,
        stack_rows([*first_stats, *centre(res_two)], width),
        r.stat0,
        r.stat_sems.at[0],
        nothing,
    )
    mean_one, inv_one = combine(stats[:, 0, :], stats[:, 1, :])
    mean_two, inv_two = combine(stats[:, 2, :], stats[:, 3, :])
    normed_one = (res_one - mean_one) * inv_one
    normed_two = (res_two - mean_two) * inv_two
    summed = r.g1[...] * normed_one + (r.g2[...] * normed_two + r.b2[...])
    summed_half = summed.astype(bf16)
    ffn_hidden = dot(summed_half, r.f1[...]) + r.fb[...]
    value, ffn_slope = gelu_and_slope(ffn_hidden)
    ffn_active = value.astype(bf16)
    res_three = summed + dot(ffn_active, r.f2[...])
    upstream = r.up[...].astype(f32)
    mean_here, squares_here = centre(res_three)
    stats = share_stats(
        place,
        stack_rows(
            [
                mean_here,
                squares_here,
                col_sum(upstream),
                col_sum(upstream * (res_three - mean_here)),
            ],
            width,
        ),
        r.stat1,
        r.stat_sems.at[1],
        nothing,
    )
    mean_three, inv_three = combine(stats[:, 0, :], stats[:, 1, :])
    normed_three = (res_three - mean_three) * inv_three
    bias_three = jnp.sum(stats[:, 2, :], axis=0, keepdims=True)
    gain_three = inv_three * jnp.sum(
        stats[:, 3, :] + (stats[:, 0, :] - mean_three) * stats[:, 2, :], axis=0, keepdims=True
    )
    g3 = r.g3[...]

    def norm_back(up, normed, inv, gain, bias_sum, gain_sum):
        return inv * (
            gain * up - gain * bias_sum / total_rows - normed * (gain * gain_sum / total_rows)
        )

    grad_three = norm_back(upstream, normed_three, inv_three, g3, bias_three, gain_three)
    grad_ffn = grad_three.astype(bf16)
    grad_hidden = (ffn_slope * dot(grad_ffn, r.f2[...], 1, 1)).astype(bf16)
    grad_summed = grad_three + dot(grad_hidden, r.f1[...], 1, 1)
    fb_part = col_sum(grad_hidden.astype(f32))

    def ffn_parts():
        r.result[...] = (g3 * normed_three + r.b3[...]).astype(bf16)
        r.stores["result"].start()
        f1_part = dot(summed_half.T, grad_hidden).astype(bf16)
        r.parts[3 * width : 4 * width, :] = f1_part[:, :width]
        r.parts[4 * width : 5 * width, :] = f1_part[:, width:]
        f2_part = dot(ffn_active.T, grad_ffn).astype(bf16)
        r.parts[5 * width : 5 * width + f2_part.shape[0], :] = f2_part

    stats = share_stats(
        place,
        stack_rows(
            [
                col_sum(grad_summed),
                col_sum(grad_summed * normed_one),
                col_sum(grad_summed * normed_two),
            ],
            width,
        ),
        r.stat2,
        r.stat_sems.at[2],
        ffn_parts,
    )
    sums = jnp.sum(stats, axis=0)
    bias_sum, gain_one, gain_two = sums[0:1], sums[1:2], sums[2:3]
    grad_second = norm_back(grad_summed, normed_two, inv_two, r.g2[...], bias_sum, gain_two)
    grad_global = grad_second.astype(bf16)
    grad_att = dot(r.out_w[...], grad_global, 1, 1).astype(bf16)
    for h in range(HEADS):
        r.do_send[h] = grad_att[HDIM * h : HDIM * (h + 1)]
    place.to_plane(lambda spot: r.do_send.at[spot], r.do.at[place.p], r.do_sems)
    r.do[place.p] = r.do_send[place.p]

    grad_first = norm_back(grad_summed, normed_one, inv_one, r.g1[...], bias_sum, gain_one)
    grad_local = grad_first.astype(bf16)
    grad_one = (r.hidden_slope[...] * dot(grad_local, r.w2[...], 1, 1)).astype(bf16)
    grad_mixed = dot(grad_one, r.w1[...], 1, 1)
    r.parts[2 * width : 3 * width, :] = dot(att_half, grad_global).astype(bf16)
    r.parts[width : 2 * width, :] = dot(r.active[...].T, grad_local).astype(bf16)
    r.parts[0:width, :] = dot(r.mixed[...].T, grad_one).astype(bf16)
    at = 5 * width + r.f2.shape[0]
    rows_left = [col_sum(grad_one.astype(f32)), fb_part[:, :width], fb_part[:, width:]]
    r.parts[at : at + 16, :] = jnp.concatenate(
        rows_left + [jnp.zeros((13, width), f32)], axis=0
    ).astype(bf16)
    r.parts[at + 16 :, :] = jnp.zeros((r.parts.shape[0] - at - 16, width), bf16)
    half = r.parts.shape[0] // 2
    place.copy(
        part_of(r.parts, 1 - place.core, half), r.pair_got, r.pair_sems, 1
    ).start()
    r.vectors[...] = jnp.concatenate(
        [gain_one, gain_two, bias_sum, gain_three, bias_three, jnp.zeros((3, width), f32)], axis=0
    )
    r.stores["vectors"].start()
    back = jnp.zeros((3 * rows, width), f32)
    for k in range(EDGES):
        back = back + dot(r.selects[k], (r.slopes[k] * grad_mixed).astype(bf16))
    r.edge_send[0] = back[2 * rows :].astype(bf16)
    r.edge_send[1] = back[:rows].astype(bf16)
    up, down = halo(
        r, place, r.edge_send.at[0], r.edge_send.at[1], r.edge_got.at[0], r.edge_got.at[1], 1
    )
    r.grad[...] = grad_first + grad_second + grad_mixed + back[rows : 2 * rows]
    return up, down


def spread(v):
    cols = v.shape[1]
    parts = [part.astype(f32) for part in three_parts(v)]
    row = lax.broadcasted_iota(jnp.int32, (16, cols), 0)
    out = jnp.where(row == 0, parts[0], 0.0)
    out = jnp.where(row == 1, parts[1], out)
    return jnp.where(row == 2, parts[2], out).astype(bf16)


def attend_back(r, place, tile, halo_copies):
    planes = place.planes
    cols = r.q.shape[2]
    width = HEADS * cols
    share = r.parts.shape[0] // HEADS
    slice_rows = share // planes
    place.wait(r.pair_got, r.pair_sems)
    pair = part_of(r.parts, place.core, 4 * share)[...].astype(f32) + r.pair_got[...].astype(f32)
    r.pair_sum[...] = pair.astype(bf16)
    place.to_chips(
        lambda spot: part_of(r.pair_sum, spot, share), lambda k: r.chips_got.at[k], r.parts_sems
    )
    build_queries(
        r, place, lambda b: spread(-r.logs[0:1, b * cols : (b + 1) * cols])
    )
    place.wait(r.do.at[pl.ds(0, HEADS - 1)], r.do_sems)
    for b in range(HEADS):
        qs = slice(b * cols, (b + 1) * cols)
        grad = r.do[b].astype(f32)
        inner = jnp.sum(grad * r.attended[:, qs], axis=0, keepdims=True) * score_scale
        r.grads[:, qs] = jnp.concatenate(
            list(three_parts(grad * score_scale)) + [spread(-inner), jnp.zeros((16, cols), bf16)],
            axis=0,
        )
    query_rows = jnp.concatenate([r.q[b] for b in range(HEADS)], axis=1)
    r.query_rows[...] = query_rows
    r.grad_rows[...] = jnp.concatenate([r.do[b] for b in range(HEADS)], axis=1)
    r.dq_total[...] = jnp.zeros_like(r.dq_total)

    def plane_of_keys(plane):
        build_keys(r, plane)
        for b in range(HEADS):
            vt = r.kv[plane * HEADS + b, HDIM : 2 * HDIM]
            r.values[b * cols : (b + 1) * cols, :] = jnp.concatenate(
                [vt, vt, vt, jnp.ones((HDIM, cols), bf16)], axis=0
            ).T
        keys = r.keys[...]
        values = r.values[...]
        key_t = jnp.concatenate([r.kv[plane * HEADS + b, 0:HDIM] for b in range(HEADS)], axis=1)

        def ahead(i):
            qs = slice(i * tile, (i + 1) * tile)
            return dot(keys, r.queries[:, qs]), dot(values, r.grads[:, qs])

        def behind(i, state, products):
            dk, dv = state
            qs = slice(i * tile, (i + 1) * tile)
            probs = jnp.exp2(products[0])
            half = probs.astype(bf16)
            grad_scores = (probs * products[1]).astype(bf16)
            r.dq_total[:, qs] += dot(key_t, grad_scores)
            return (
                dk + dot(r.query_rows[:, qs], grad_scores, 1, 1),
                dv + dot(r.grad_rows[:, qs], half, 1, 1),
            )

        state = (jnp.zeros((HDIM, width), f32),) * 2
        tiles = width // tile
        current = ahead(0)
        for i in range(tiles):
            following = ahead(i + 1) if i + 1 < tiles else None
            state = behind(i, state, current)
            current = following
        for b in range(HEADS):
            part = slice(b * cols, (b + 1) * cols)
            r.dkv_part[plane * HEADS + b] = jnp.concatenate(
                [state[0][:, part], state[1][:, part]], axis=0
            ).astype(bf16)

    def plane_step(step, _):
        k = planes - 1 - step
        plane_of_keys(place.plane(k))

        @pl.when(k > 0)
        def send_part():
            place.copy(
                part_of(r.dkv_part, place.plane(k), HEADS), r.dkv_got.at[k], r.dkv_sems, k * HEADS
            ).start()

        @pl.when(step == 0)
        def sum_plane():
            place.wait(r.chips_got.at[pl.ds(1, HEADS // 2 - 1)], r.parts_sems)
            start_halo(place, *halo_copies)
            total = part_of(r.pair_sum, place.chip, share)[...].astype(f32) + total_of(
                r.chips_got, 1
            )
            r.plane_sum[...] = total.astype(bf16)
            place.to_line(
                lambda spot: part_of(r.plane_sum, spot, slice_rows),
                lambda k: r.line_got.at[k],
                r.line_sems.at[0],
            )

        @pl.when(step == 1)
        def sum_line():
            place.wait(r.line_got.at[pl.ds(1, planes - 1)], r.line_sems.at[0])
            total = part_of(r.plane_sum, place.z, slice_rows)[...].astype(f32) + total_of(
                r.line_got, 1
            )
            r.line_sum[place.z] = total.astype(bf16)
            place.to_line(
                lambda spot: r.line_sum.at[place.z],
                lambda k: r.line_sum.at[place.z],
                r.line_sems.at[1],
            )

        @pl.when(step == 2)
        def spread_line():
            place.wait(r.line_sum.at[pl.ds(1, planes - 1)], r.line_sems.at[1])
            r.sums[place.share] = r.line_sum[...].reshape(share, cols)
            place.to_chips(
                lambda spot: r.sums.at[place.share],
                lambda k: r.sums.at[place.share],
                r.whole_sems.at[0],
            )

        return 0

    lax.fori_loop(0, planes, plane_step, 0)
    place.wait(r.sums.at[pl.ds(0, HEADS // 2 - 1)], r.whole_sems.at[0])
    own_half = part_of(r.sums, place.core, HEADS // 2)
    place.copy(own_half, own_half, r.whole_sems.at[1], 1).start()
    place.wait(r.x_all.at[pl.ds(0, HEADS - 1)], r.x_sems)
    place.wait(r.dkv_got.at[pl.ds(1, planes - 1)], r.dkv_sems)
    dkv = part_of(r.dkv_part, place.z, HEADS)[...].astype(f32) + total_of(r.dkv_got, 1)
    for b in range(HEADS):
        r.back_send[b, 0:HDIM] = r.dq_total[:, b * cols : (b + 1) * cols].astype(bf16)
        r.back_send[b, HDIM : 3 * HDIM] = dkv[b].astype(bf16)
    place.to_plane(
        lambda spot: r.back_send.at[spot], r.back.at[place.p], r.back_sems
    )
    r.back[place.p] = r.back_send[place.p]
    total = dot(r.back_send[0], r.x_all[0])
    for b in range(1, HEADS):
        total = total + dot(r.back_send[b], r.x_all[b])
    r.heads_part[...] = total.astype(bf16)
    place.to_line(lambda spot: r.heads_part, lambda k: r.heads_got.at[k], r.heads_sems)
    wait_halo(place, *halo_copies)
    grad = r.grad[...] + r.edge_got[0].astype(f32) + r.edge_got[1].astype(f32)
    place.wait(r.heads_got.at[pl.ds(1, planes - 1)], r.heads_sems)
    total = r.heads_part[...].astype(f32) + total_of(r.heads_got, 1)
    r.heads[place.share] = total.astype(bf16)
    place.to_chips(
        lambda spot: r.heads.at[place.share],
        lambda k: r.heads.at[place.share],
        r.last_sems.at[0],
    )
    place.wait(r.back.at[pl.ds(0, HEADS - 1)], r.back_sems)
    for s, w in enumerate((r.wq, r.wk, r.wv)):
        part = jnp.concatenate(
            [r.back[h, HDIM * s : HDIM * (s + 1)] for h in range(HEADS)], axis=0
        )
        grad = grad + dot(part.T, w[...], 1, 1)
    r.grad[...] = grad
    r.stores["grad"].start()
    place.wait(r.heads.at[pl.ds(0, HEADS // 2 - 1)], r.last_sems.at[0])
    own_half = part_of(r.heads, place.core, HEADS // 2)
    place.copy(own_half, own_half, r.last_sems.at[1], 1).start()
    place.wait(r.sums.at[pl.ds(0, HEADS // 2)], r.whole_sems.at[1])
    r.stores["sums"].start()
    place.wait(r.heads.at[pl.ds(0, HEADS // 2)], r.last_sems.at[1])
    r.stores["heads"].start()


def layer_kernel(count, cores, names, args, outs, *refs):
    r = Refs(names, refs)
    place = Place(count, cores)
    r.loads = {
        name: pltpu.make_async_copy(
            getattr(r, "from_" + name), getattr(r, name), r.load_sems.at[i]
        )
        for i, name in enumerate(args)
    }
    r.stores = {
        name: pltpu.make_async_copy(getattr(r, name), getattr(r, "to_" + name), r.store_sems.at[i])
        for i, name in enumerate(outs)
    }
    for load in r.loads.values():
        load.start()
    halo_copies = project(r, place)

    def beside():
        r.need("step", "degree", "edge", "w1", "b1", "w2")
        wait_halo(place, *halo_copies)
        gine_forward(r, place)

    attend(r, place, 512, halo_copies, beside)
    r.need("up", "out_w", "f1", "fb", "f2", "g1", "g2", "b2", "g3", "b3")
    attend_back(r, place, 512, norms(r, place))
    for store in r.stores.values():
        store.wait()


def finish_kernel(
    grad_ref,
    heads_ref,
    sums_ref,
    result_ref,
    vectors_ref,
    result_out,
    grad_out,
    gw1_out,
    gb1_out,
    gw2_out,
    qw_out,
    kw_out,
    vw_out,
    ow_out,
    f1_out,
    fb_out,
    f2_out,
    gain1_out,
    gain2_out,
    bias2_out,
    gain3_out,
    bias3_out,
):
    width = grad_ref.shape[1]
    result_out[...] = result_ref[...]
    grad_out[...] = grad_ref[...]
    for s, w_out in enumerate((qw_out, kw_out, vw_out)):
        cols = slice(HDIM * s, HDIM * (s + 1))
        spots = [h % 2 * (HEADS // 2) + h // 2 for h in range(HEADS)]
        total = jnp.concatenate([heads_ref[spot, cols] for spot in spots], axis=0)
        w_out[...] = total.T.astype(f32)
    gw1_out[...] = sums_ref[0:width].astype(f32)
    gw2_out[...] = sums_ref[width : 2 * width].astype(f32)
    ow_out[...] = sums_ref[2 * width : 3 * width].astype(f32)
    f1_out[:, 0:width] = sums_ref[3 * width : 4 * width].astype(f32)
    f1_out[:, width:] = sums_ref[4 * width : 5 * width].astype(f32)
    last = 5 * width + f2_out.shape[0]
    f2_out[...] = sums_ref[5 * width : last].astype(f32)
    rows_left = sums_ref[last : last + 16].astype(f32)
    gb1_out[...] = rows_left[0:1]
    fb_out[:, 0:width] = rows_left[1:2]
    fb_out[:, width:] = rows_left[2:3]
    for k, out in enumerate((gain1_out, gain2_out, bias2_out, gain3_out, bias3_out)):
        out[...] = vectors_ref[k : k + 1]


def on_device(
    count,
    cores,
    node_feat,
    edge_feat,
    edge_step,
    degree,
    graph_len,
    gine_w1,
    gine_b1,
    gine_w2,
    query_w,
    key_w,
    value_w,
    out_w,
    ffn_w1,
    ffn_b1,
    ffn_w2,
    norm1_gain,
    norm2_gain,
    norm2_bias,
    norm3_gain,
    norm3_bias,
    out_grad,
):
    rows, width = node_feat.shape
    ffn = ffn_w1.shape[1]
    planes = count // HEADS
    plane_rows = HEADS * rows
    vmem = pl.BlockSpec(memory_space=pltpu.VMEM)
    dma = pltpu.SemaphoreType.DMA
    shape = jax.ShapeDtypeStruct
    share_unit = 16 * HEADS * planes
    needed = 3 * width + 2 * ffn + 16
    part_rows = -(-needed // share_unit) * share_unit
    share = part_rows // HEADS

    def row(v):
        return v.reshape(1, -1)

    args = dict(
        x=node_feat,
        wk=key_w,
        wv=value_w,
        wq=query_w,
        step=edge_step.T,
        degree=row(degree),
        edge=edge_feat,
        w1=gine_w1,
        b1=row(gine_b1),
        w2=gine_w2,
        up=out_grad,
        out_w=out_w,
        f1=ffn_w1,
        fb=row(ffn_b1),
        f2=ffn_w2,
        g1=row(norm1_gain),
        g2=row(norm2_gain),
        b2=row(norm2_bias),
        g3=row(norm3_gain),
        b3=row(norm3_bias),
    )
    outs = dict(
        result=shape((rows, width), bf16),
        grad=shape((rows, width), f32),
        vectors=shape((8, width), f32),
        heads=shape((HEADS, 3 * HDIM, width), bf16),
        sums=shape((HEADS, share, width), bf16),
    )
    scratch = dict(
        ext=pltpu.VMEM((3 * rows, width), bf16),
        kv_send=pltpu.VMEM((HEADS, 2 * HDIM, rows), bf16),
        q_send=pltpu.VMEM((HEADS, HDIM, rows), bf16),
        kv=pltpu.VMEM((count, 2 * HDIM, rows), bf16),
        q=pltpu.VMEM((HEADS, HDIM, rows), bf16),
        source=pltpu.VMEM((EDGES, rows), jnp.int32),
        slopes=pltpu.VMEM((EDGES, rows, width), f32),
        selects=pltpu.VMEM((EDGES, 3 * rows, rows), bf16),
        mixed=pltpu.VMEM((rows, width), bf16),
        active=pltpu.VMEM((rows, width), bf16),
        hidden_slope=pltpu.VMEM((rows, width), f32),
        res_one=pltpu.VMEM((rows, width), f32),
        keys=pltpu.VMEM((plane_rows, 128), bf16),
        values=pltpu.VMEM((plane_rows, 128), bf16),
        queries=pltpu.VMEM((128, plane_rows), bf16),
        grads=pltpu.VMEM((128, plane_rows), bf16),
        query_rows=pltpu.VMEM((HDIM, plane_rows), bf16),
        grad_rows=pltpu.VMEM((HDIM, plane_rows), bf16),
        total=pltpu.VMEM((HDIM + 16, plane_rows), f32),
        top=pltpu.VMEM((8, plane_rows), f32),
        logs=pltpu.VMEM((8, plane_rows), f32),
        attended=pltpu.VMEM((HDIM, plane_rows), f32),
        att_send=pltpu.VMEM((HEADS, HDIM, rows), bf16),
        att_got=pltpu.VMEM((HEADS, HDIM, rows), bf16),
        do_send=pltpu.VMEM((HEADS, HDIM, rows), bf16),
        do=pltpu.VMEM((HEADS, HDIM, rows), bf16),
        stat0=pltpu.VMEM((count, 8, width // 2), f32),
        stat1=pltpu.VMEM((count, 8, width // 2), f32),
        stat2=pltpu.VMEM((count, 8, width // 2), f32),
        edge_send=pltpu.VMEM((2, rows, width), bf16),
        edge_got=pltpu.VMEM((2, rows, width), bf16),
        x_all=pltpu.VMEM((HEADS, rows, width), bf16),
        parts=pltpu.VMEM((part_rows, width), bf16),
        pair_got=pltpu.VMEM((part_rows // 2, width), bf16),
        pair_sum=pltpu.VMEM((part_rows // 2, width), bf16),
        chips_got=pltpu.VMEM((HEADS // 2, share, width), bf16),
        plane_sum=pltpu.VMEM((share, width), bf16),
        line_got=pltpu.VMEM((planes, share // planes, width), bf16),
        line_sum=pltpu.VMEM((planes, share // planes, width), bf16),
        dq_total=pltpu.VMEM((HDIM, plane_rows), f32),
        dkv_part=pltpu.VMEM((count, 2 * HDIM, rows), bf16),
        dkv_got=pltpu.VMEM((planes, HEADS, 2 * HDIM, rows), bf16),
        back_send=pltpu.VMEM((HEADS, 3 * HDIM, rows), bf16),
        back=pltpu.VMEM((HEADS, 3 * HDIM, rows), bf16),
        heads_part=pltpu.VMEM((3 * HDIM, width), bf16),
        heads_got=pltpu.VMEM((planes, 3 * HDIM, width), bf16),
        kv_sems=dma((planes, 2, 2)),
        halo_sems=dma((2, 4)),
        stat_sems=dma((3, 2)),
        line_sems=dma((2, 2)),
        whole_sems=dma((2, 2)),
        last_sems=dma((2, 2)),
        **{
            name + "_sems": dma((2,))
            for name in ("q", "att", "do", "x", "pair", "parts", "dkv", "back", "heads")
        },
    )
    scratch = dict(
        **{name: pltpu.VMEM(v.shape, v.dtype) for name, v in (args | outs).items()},
        **scratch,
        load_sems=dma((len(args),)),
        store_sems=dma((len(outs),)),
    )
    names = (
        "graph_len",
        *("from_" + name for name in args),
        *("to_" + name for name in outs),
        *scratch,
    )
    anywhere = pl.BlockSpec(memory_space=pl.ANY)
    result, grad, vectors, heads, sums = pl.pallas_call(
        functools.partial(layer_kernel, count, cores, names, tuple(args), tuple(outs)),
        out_shape=tuple(outs.values()),
        in_specs=[pl.BlockSpec(memory_space=pltpu.SMEM)] + [anywhere] * len(args),
        out_specs=(anywhere,) * len(outs),
        scratch_shapes=list(scratch.values()),
        compiler_params=pltpu.CompilerParams(
            vmem_limit_bytes=62 << 20, collective_id=1, has_side_effects=True
        ),
    )(graph_len, *args.values())

    square = shape((width, width), f32)
    line = shape((1, width), f32)
    done = pl.pallas_call(
        finish_kernel,
        out_shape=(
            shape((rows, width), bf16),
            shape((rows, width), f32),
            square,
            line,
            square,
            square,
            square,
            square,
            square,
            shape((width, ffn), f32),
            shape((1, ffn), f32),
            shape((ffn, width), f32),
        )
        + (line,) * 5,
        in_specs=[vmem] * 5,
        out_specs=(vmem,) * 17,
        compiler_params=pltpu.CompilerParams(vmem_limit_bytes=60 << 20),
    )(grad, heads, sums.reshape(part_rows, width), result, vectors)
    return tuple(v.reshape(-1) if v.shape[0] == 1 else v for v in done)


def solution(mesh):
    count = mesh.shape["blk"] * mesh.shape["rep"]
    rows = P(AXES, None)
    whole = P()
    return jax.shard_map(
        functools.partial(on_device, count, mesh.shape["rep"]),
        mesh=mesh,
        in_specs=(rows, P(AXES, None, None), rows, P(AXES)) + (whole,) * 16 + (rows,),
        out_specs=(rows, rows) + (whole,) * 15,
        check_vma=False,
    )
```

```python
import functools
import jax
import jax.numpy as jnp
from jax import lax
from jax.experimental import pallas as pl
from jax.experimental.pallas import tpu as pltpu
from jax.sharding import PartitionSpec as P

HEADS = 8
HDIM = 32
EDGES = 8
GRAPHS = 9
AXES = ("blk", "rep")
MESH = pl.DeviceIdType.MESH
bf16 = jnp.bfloat16
f32 = jnp.float32

norm_eps = 1e-05
far_score = -1e30
log2_e = 1.4426950408889634
score_scale = HDIM ** (-0.5)
gelu_c = 0.7978845608028654
gelu_a = 0.044715


def dot(left, right, left_dim=1, right_dim=0):
    return lax.dot_general(
        left, right, (((left_dim,), (right_dim,)), ((), ())), preferred_element_type=f32
    )


def gelu(v):
    return 0.5 * v * (1.0 + jnp.tanh(gelu_c * (v + gelu_a * (v * v * v))))


def gelu_slope(v):
    squared = v * v
    bend = jnp.tanh(gelu_c * v * (1.0 + gelu_a * squared))
    return 0.5 * (1.0 + bend) + 0.5 * v * (1.0 - bend * bend) * (
        gelu_c * (1.0 + 3.0 * gelu_a * squared)
    )


def three_parts(v):
    first = v.astype(bf16)
    rest = v - first.astype(f32)
    second = rest.astype(bf16)
    third = (rest - second.astype(f32)).astype(bf16)
    return first, second, third


class Place:
    def __init__(self, count, cores):
        self.count = count
        self.cores = cores
        self.planes = count // HEADS
        self.blk = lax.axis_index("blk")
        self.rep = lax.axis_index("rep")
        self.me = self.blk * cores + self.rep
        self.z = lax.div(self.me, HEADS)
        self.p = self.me - self.z * HEADS
        self.chip = lax.div(self.p, 2)
        self.core = self.p - 2 * self.chip
        self.share = self.core * (HEADS // 2) + self.chip
        self.steps = []
        bit, rest = 1, self.me
        while bit < count:
            half = lax.div(rest, 2)
            self.steps.append(bit * (1 - 2 * (rest - 2 * half)))
            bit, rest = 2 * bit, half

    def move(self, k, first=0, last=None):
        total = 0
        for j, step in enumerate(self.steps[first:last]):
            bit = 1 << (first + j)
            if isinstance(k, int):
                if k & bit:
                    total = total + step
            else:
                total = total + lax.rem(lax.div(k, bit), 2) * step
        return total

    def device(self, k):
        low = self.cores.bit_length() - 1
        return {
            "blk": self.blk + lax.div(self.move(k, low), self.cores),
            "rep": self.rep + self.move(k, 0, low),
        }

    def peer(self, k):
        return self.me + self.move(k)

    def spot(self, k):
        return self.p + self.move(k, 0, 3)

    def plane(self, k):
        return self.z + lax.div(self.move(k * HEADS, 3), HEADS)

    def loop(self, first, last, body):
        if last - first <= 32:
            for k in range(first, last):
                body(k)
        else:

            def step(k, _):
                body(k)
                return 0

            lax.fori_loop(first, last, step, 0)

    def greet(self):
        def hello(k):
            pl.semaphore_signal(
                pltpu.get_barrier_semaphore(),
                inc=1,
                device_id=self.device(self.count - k),
                device_id_type=MESH,
            )

        self.loop(1, self.count, hello)

    def greeted(self):
        pl.semaphore_wait(pltpu.get_barrier_semaphore(), self.count - 1)

    def copy(self, src, dst, sems, k):
        return self.copy_to(src, dst, sems.at[0], sems.at[1], self.device(k))

    def copy_to(self, src, dst, send_sem, recv_sem, device):
        return pltpu.make_async_remote_copy(
            src_ref=src,
            dst_ref=dst,
            send_sem=send_sem,
            recv_sem=recv_sem,
            device_id=device,
            device_id_type=MESH,
        )

    def to_plane(self, src_of, dst, sems):
        for k in reversed(range(1, HEADS)):
            self.copy(src_of(self.spot(k)), dst, sems, k).start()

    def to_line(self, src_of, dst_of, sems):
        for k in range(1, self.planes):
            self.copy(src_of(self.plane(k)), dst_of(k), sems, k * HEADS).start()

    def to_chips(self, src_of, dst_of, sems):
        for k in range(1, HEADS // 2):
            there = self.chip + lax.div(self.move(2 * k, 1, 3), 2)
            self.copy(src_of(there), dst_of(k), sems, 2 * k).start()

    def wait(self, like, sems):
        self.copy(like, like, sems, 1).wait()


def part_of(ref, spot, size):
    return ref.at[pl.ds(pl.multiple_of(spot * size, size), size)]


def total_of(ref, start=0):
    total = ref[start].astype(f32)
    for k in range(start + 1, ref.shape[0]):
        total = total + ref[k].astype(f32)
    return total


def col_sum(v):
    return jnp.sum(v, axis=0, keepdims=True)


def stack_rows(rows, width):
    four = jnp.concatenate(rows + [jnp.zeros((1, width), f32)] * (4 - len(rows)), axis=0)
    return jnp.concatenate([four[:, : width // 2], four[:, width // 2 :]], axis=0)


def graph_bounds(len_ref, positions):
    last = 0
    graph = jnp.zeros(positions.shape, jnp.int32)
    start = jnp.zeros(positions.shape, jnp.int32)
    ends = []
    for g in range(GRAPHS):
        last = last + len_ref[g]
        ends.append(last)
        passed = positions >= last
        graph = graph + passed.astype(jnp.int32)
        start = jnp.where(passed, last, start)
    stop = jnp.full(positions.shape, ends[-1], jnp.int32)
    for end in reversed(ends):
        stop = jnp.where(positions < end, end, stop)
    return graph, start, stop


def own_graph(len_ref, first, width):
    positions = first + lax.broadcasted_iota(jnp.int32, (1, width), 1)
    graph, _, _ = graph_bounds(len_ref, positions)
    rows = lax.broadcasted_iota(jnp.int32, (16, width), 0)
    return rows == graph


def as_columns(rows, width):
    return jnp.concatenate([rows, jnp.zeros((128 - rows.shape[0], width), f32)], axis=0).T


def gelu_and_slope(v):
    squared = v * v
    bend = jnp.tanh(gelu_c * v * (1.0 + gelu_a * squared))
    half = 0.5 * (1.0 + bend)
    slope = half + 0.5 * v * (1.0 - bend * bend) * (gelu_c * (1.0 + 3.0 * gelu_a * squared))
    return v * half, slope


class Refs:
    def __init__(self, names, refs):
        for name, ref in zip(names, refs, strict=True):
            setattr(self, name, ref)

    def need(self, *names):
        for name in names:
            self.loads[name].wait()


def share_stats(place, stats, buffer, sems, between):
    buffer[place.me] = stats

    def begin(k):
        place.copy(buffer.at[place.me], buffer.at[place.me], sems, place.count - k).start()

    place.loop(1, place.count, begin)
    between()
    place.wait(buffer.at[pl.ds(0, place.count - 1)], sems)
    return jnp.concatenate([buffer[:, 0:4, :], buffer[:, 4:8, :]], axis=2)


def project(r, place):
    rows, width = r.x.shape
    count = place.count
    r.edge_got[...] = jnp.zeros_like(r.edge_got)
    r.need("x")
    x = r.x[...]
    r.ext[0:rows, :] = jnp.zeros_like(x)
    r.ext[rows : 2 * rows, :] = x
    r.ext[2 * rows :, :] = jnp.zeros_like(x)
    place.greet()
    xt = x.T
    r.need("wk", "wv", "wq")
    kt = dot(r.wk[...].T, xt).astype(bf16)
    vt = dot(r.wv[...].T, xt).astype(bf16)
    for h in range(HEADS):
        cols = slice(HDIM * h, HDIM * (h + 1))
        r.kv_send[h, 0:HDIM] = kt[cols]
        r.kv_send[h, HDIM : 2 * HDIM] = vt[cols]
    qt = dot(r.wq[...].T, xt).astype(bf16)
    for h in range(HEADS):
        r.q_send[h] = qt[HDIM * h : HDIM * (h + 1)]
    place.greeted()

    place.to_plane(lambda spot: r.kv_send.at[spot], r.kv.at[place.me], r.kv_sems.at[0, 0])
    place.to_plane(lambda spot: r.q_send.at[spot], r.q.at[place.p], r.q_sems)
    up, down = halo(r, place, r.x, r.x, r.ext.at[pl.ds(0, rows)], r.ext.at[pl.ds(2 * rows, rows)])
    r.kv[place.me] = r.kv_send[place.p]
    r.q[place.p] = r.q_send[place.p]
    return up, down


def pass_on(r, place, dz, bit, half):
    rows = part_of(r.kv, 2 * place.plane(dz) + half, HEADS // 2)
    place.copy(rows, rows, r.kv_sems.at[dz + bit, half], bit * HEADS).start()


def pass_down(r, place, dz, half):
    bit = 1
    while bit < place.planes // 2:
        pl.when(lax.rem(dz, 2 * bit) == 0)(functools.partial(pass_on, r, place, dz, bit, half))
        bit *= 2


def kv_arrived(r, place, dz, half):
    place.wait(r.kv.at[pl.ds(0, HEADS // 2)], r.kv_sems.at[dz, half])


def halo(r, place, up_src, down_src, up_dst, down_dst, which=0):
    def neighbour(index):
        blk = lax.div(index, place.cores)
        return {"blk": blk, "rep": index - blk * place.cores}

    sems = r.halo_sems.at[which]
    last = place.count - 1
    after = neighbour(jnp.minimum(place.me + 1, last))
    before = neighbour(jnp.maximum(place.me - 1, 0))
    up = place.copy_to(up_src, up_dst, sems.at[0], sems.at[1], after)
    down = place.copy_to(down_src, down_dst, sems.at[2], sems.at[3], before)
    return up, down


def start_halo(place, up, down):
    @pl.when(place.me < place.count - 1)
    def send_up():
        up.start()

    @pl.when(place.me > 0)
    def send_down():
        down.start()


def wait_halo(place, up, down):
    @pl.when(place.me < place.count - 1)
    def with_after():
        up.wait_send()
        down.wait_recv()

    @pl.when(place.me > 0)
    def with_before():
        down.wait_send()
        up.wait_recv()


def gine_forward(r, place):
    rows, width = r.x.shape
    positions = place.me * rows + lax.broadcasted_iota(jnp.int32, (1, rows), 1)
    _, start, stop = graph_bounds(r.graph_len, positions)
    source = jnp.minimum(jnp.maximum(positions + r.step[...], start), stop - 1)
    source = source - place.me * rows + rows
    r.source[...] = source
    columns = as_columns(
        jnp.concatenate([source.astype(f32), r.degree[...].astype(f32)], axis=0), rows
    )
    cells = lax.broadcasted_iota(jnp.int32, (rows, 3 * rows), 1).astype(f32)
    x = r.x[...].astype(f32)
    message = jnp.zeros_like(x)
    around = r.ext[...]
    for k in range(EDGES):
        select = (columns[:, k : k + 1] == cells).astype(f32).astype(bf16)
        v = dot(select, around) + r.edge[:, k, :].astype(f32)
        present = columns[:, EDGES : EDGES + 1] > k
        value, slope = gelu_and_slope(v)
        message = message + jnp.where(present, value, 0.0)
        r.slopes[k] = jnp.where(present, slope, 0.0)
    mixed = (x + message).astype(bf16)
    r.mixed[...] = mixed
    hidden = dot(mixed, r.w1[...]) + r.b1[...]
    value, slope = gelu_and_slope(hidden)
    active = value.astype(bf16)
    r.active[...] = active
    r.hidden_slope[...] = slope
    r.res_one[...] = x + dot(active, r.w2[...])


def build_keys(r, plane):
    cols = r.q.shape[2]
    for b in range(HEADS):
        block = plane * HEADS + b
        kt = r.kv[block, 0:HDIM]
        same = own_graph(r.graph_len, block * cols, cols).astype(f32).astype(bf16)
        ones = jnp.ones((16, cols), bf16)
        r.keys[b * cols : (b + 1) * cols, :] = jnp.concatenate([kt, kt, kt, same, ones], axis=0).T


def build_queries(r, place, last_rows):
    cols = r.q.shape[2]
    for b in range(HEADS):
        parts = three_parts(r.q[b].astype(f32) * (score_scale * log2_e))
        same = own_graph(r.graph_len, (place.z * HEADS + b) * cols, cols)
        known = lax.broadcasted_iota(jnp.int32, (16, cols), 0) < GRAPHS
        mask = jnp.where(jnp.logical_or(same, jnp.logical_not(known)), 0.0, far_score).astype(bf16)
        r.queries[:, b * cols : (b + 1) * cols] = jnp.concatenate(
            list(parts) + [mask, last_rows(b)], axis=0
        )


def store_weights(r, dz):
    slot = lax.rem(dz, 2)
    return pltpu.make_async_copy(r.kept.at[slot], r.far.at[dz], r.far_sems.at[0, slot])


def load_weights(r, dz):
    slot = lax.rem(dz, 2)
    return pltpu.make_async_copy(r.far.at[dz], r.kept.at[slot], r.far_sems.at[1, slot])


def pipelined(ahead, behind, depth):
    pairs = [(a, b) for a in range(HEADS) for b in range(HEADS)]
    waiting = [ahead(*pair) for pair in pairs[:depth]]
    for i, pair in enumerate(pairs):
        if i + depth < len(pairs):
            waiting.append(ahead(*pairs[i + depth]))
        behind(*pair, waiting.pop(0))


def attend(r, place, depth, halo_copies, beside):
    cols = r.q.shape[2]
    width = HEADS * cols
    place.wait(r.q.at[pl.ds(0, HEADS - 1)], r.q_sems)
    place.wait(r.kv.at[pl.ds(0, HEADS - 1)], r.kv_sems.at[0, 0])
    for half in range(2):
        bit = 1
        while bit < place.planes:
            pass_on(r, place, 0, bit, half)
            bit *= 2
    start_halo(place, *halo_copies)
    place.to_plane(lambda spot: r.x, r.x_all.at[place.p], r.x_sems)
    r.x_all[place.p] = r.x[...]
    build_queries(r, place, lambda b: jnp.zeros((16, cols), bf16))
    r.total[...] = jnp.zeros_like(r.total)
    r.value_rows[HDIM:, :] = jnp.ones((16, width), bf16)
    r.top[...] = jnp.full(r.top.shape, 2.0 * far_score, f32)
    farthest = place.planes // 2

    def plane_step(dz, _):
        plane = place.plane(dz)

        @pl.when(jnp.logical_and(dz > 0, dz != farthest))
        def first_half():
            kv_arrived(r, place, dz, 0)
            pass_down(r, place, dz, 0)

        @pl.when(dz > 0)
        def second_half():
            kv_arrived(r, place, dz, 1)
            pass_down(r, place, dz, 1)

        slot = lax.rem(dz, 2)

        @pl.when(dz >= 2)
        def slot_free():
            store_weights(r, dz - 2).wait()

        build_keys(r, plane)
        for b in range(HEADS):
            r.value_rows[0:HDIM, b * cols : (b + 1) * cols] = r.kv[
                plane * HEADS + b, HDIM : 2 * HDIM
            ]

        def ahead(a, b):
            ks, qs = slice(a * cols, (a + 1) * cols), slice(b * cols, (b + 1) * cols)
            return dot(r.keys[ks, :], r.queries[:, qs])

        def behind(a, b, scores):
            ks, qs = slice(a * cols, (a + 1) * cols), slice(b * cols, (b + 1) * cols)
            before = r.top[0:1, qs]
            now = jnp.maximum(before, jnp.max(scores, axis=0, keepdims=True))
            weights = jnp.exp2(scores - now).astype(bf16)
            r.kept[slot, ks, qs] = weights
            r.total[:, qs] = r.total[:, qs] * jnp.exp2(before - now) + dot(
                r.value_rows[:, ks], weights
            )
            r.top[0:1, qs] = now
            r.tops[dz, a : a + 1, qs] = now

        pipelined(ahead, behind, depth)

        @pl.when(dz < place.planes - 2)
        def away():
            store_weights(r, dz).start()

        @pl.when(dz == 0)
        def after_own():
            beside()
            kv_arrived(r, place, farthest, 0)
            pass_down(r, place, farthest, 0)

        return 0

    lax.fori_loop(0, place.planes, plane_step, 0)
    sums = r.total[HDIM : HDIM + 1, :]
    r.logs[0:1, :] = r.top[0:1, :] + jnp.log2(sums)
    attended = r.total[0:HDIM, :] / sums
    r.attended[...] = attended
    for b in range(HEADS):
        r.att_send[b] = attended[:, b * cols : (b + 1) * cols].astype(bf16)


def norms(r, place):
    rows, width = r.x.shape
    count = place.count
    total_rows = rows * count
    place.to_plane(lambda spot: r.att_send.at[spot], r.att_got.at[place.p], r.att_sems)
    r.att_got[place.p] = r.att_send[place.p]
    source = r.source[...]
    cells = lax.broadcasted_iota(jnp.int32, (3 * rows, rows), 0)
    for k in range(EDGES):
        r.selects[k] = (source[k : k + 1, :] == cells).astype(f32).astype(bf16)
    x = r.x[...].astype(f32)
    res_one = r.res_one[...]

    def centre(v):
        mean = col_sum(v) / rows
        off = v - mean
        return mean, col_sum(off * off)

    def combine(means, squares):
        mean = jnp.sum(means, axis=0, keepdims=True) / count
        off = means - mean
        var = (
            jnp.sum(squares, axis=0, keepdims=True)
            + rows * jnp.sum(off * off, axis=0, keepdims=True)
        ) / total_rows
        return mean, lax.rsqrt(var + norm_eps)

    first_stats = centre(res_one)
    place.wait(r.att_got.at[pl.ds(0, HEADS - 1)], r.att_sems)
    att_half = jnp.concatenate([r.att_got[h] for h in range(HEADS)], axis=0)
    res_two = x + dot(att_half.T, r.out_w[...])

    def nothing():
        pass

    stats = share_stats(
        place,
        stack_rows([*first_stats, *centre(res_two)], width),
        r.stat0,
        r.stat_sems.at[0],
        nothing,
    )
    mean_one, inv_one = combine(stats[:, 0, :], stats[:, 1, :])
    mean_two, inv_two = combine(stats[:, 2, :], stats[:, 3, :])
    normed_one = (res_one - mean_one) * inv_one
    normed_two = (res_two - mean_two) * inv_two
    summed = r.g1[...] * normed_one + (r.g2[...] * normed_two + r.b2[...])
    summed_half = summed.astype(bf16)
    ffn_hidden = dot(summed_half, r.f1[...]) + r.fb[...]
    value, ffn_slope = gelu_and_slope(ffn_hidden)
    ffn_active = value.astype(bf16)
    res_three = summed + dot(ffn_active, r.f2[...])
    upstream = r.up[...].astype(f32)
    mean_here, squares_here = centre(res_three)
    stats = share_stats(
        place,
        stack_rows(
            [
                mean_here,
                squares_here,
                col_sum(upstream),
                col_sum(upstream * (res_three - mean_here)),
            ],
            width,
        ),
        r.stat1,
        r.stat_sems.at[1],
        nothing,
    )
    mean_three, inv_three = combine(stats[:, 0, :], stats[:, 1, :])
    normed_three = (res_three - mean_three) * inv_three
    bias_three = jnp.sum(stats[:, 2, :], axis=0, keepdims=True)
    gain_three = inv_three * jnp.sum(
        stats[:, 3, :] + (stats[:, 0, :] - mean_three) * stats[:, 2, :], axis=0, keepdims=True
    )
    g3 = r.g3[...]

    def norm_back(up, normed, inv, gain, bias_sum, gain_sum):
        return inv * (
            gain * up - gain * bias_sum / total_rows - normed * (gain * gain_sum / total_rows)
        )

    grad_three = norm_back(upstream, normed_three, inv_three, g3, bias_three, gain_three)
    grad_ffn = grad_three.astype(bf16)
    grad_hidden = (ffn_slope * dot(grad_ffn, r.f2[...], 1, 1)).astype(bf16)
    grad_summed = grad_three + dot(grad_hidden, r.f1[...], 1, 1)
    fb_part = col_sum(grad_hidden.astype(f32))

    def ffn_parts():
        r.result[...] = (g3 * normed_three + r.b3[...]).astype(bf16)
        r.stores["result"].start()
        f1_part = dot(summed_half.T, grad_hidden).astype(bf16)
        r.parts[3 * width : 4 * width, :] = f1_part[:, :width]
        r.parts[4 * width : 5 * width, :] = f1_part[:, width:]
        f2_part = dot(ffn_active.T, grad_ffn).astype(bf16)
        r.parts[5 * width : 5 * width + f2_part.shape[0], :] = f2_part

    stats = share_stats(
        place,
        stack_rows(
            [
                col_sum(grad_summed),
                col_sum(grad_summed * normed_one),
                col_sum(grad_summed * normed_two),
            ],
            width,
        ),
        r.stat2,
        r.stat_sems.at[2],
        ffn_parts,
    )
    sums = jnp.sum(stats, axis=0)
    bias_sum, gain_one, gain_two = sums[0:1], sums[1:2], sums[2:3]
    grad_second = norm_back(grad_summed, normed_two, inv_two, r.g2[...], bias_sum, gain_two)
    grad_global = grad_second.astype(bf16)
    grad_att = dot(r.out_w[...], grad_global, 1, 1).astype(bf16)
    for h in range(HEADS):
        r.do_send[h] = grad_att[HDIM * h : HDIM * (h + 1)]
    place.to_plane(lambda spot: r.do_send.at[spot], r.do.at[place.p], r.do_sems)
    r.do[place.p] = r.do_send[place.p]

    grad_first = norm_back(grad_summed, normed_one, inv_one, r.g1[...], bias_sum, gain_one)
    grad_local = grad_first.astype(bf16)
    grad_one = (r.hidden_slope[...] * dot(grad_local, r.w2[...], 1, 1)).astype(bf16)
    grad_mixed = dot(grad_one, r.w1[...], 1, 1)
    r.parts[2 * width : 3 * width, :] = dot(att_half, grad_global).astype(bf16)
    r.parts[width : 2 * width, :] = dot(r.active[...].T, grad_local).astype(bf16)
    r.parts[0:width, :] = dot(r.mixed[...].T, grad_one).astype(bf16)
    at = 5 * width + r.f2.shape[0]
    rows_left = [col_sum(grad_one.astype(f32)), fb_part[:, :width], fb_part[:, width:]]
    r.parts[at : at + 16, :] = jnp.concatenate(
        rows_left + [jnp.zeros((13, width), f32)], axis=0
    ).astype(bf16)
    r.parts[at + 16 :, :] = jnp.zeros((r.parts.shape[0] - at - 16, width), bf16)
    half = r.parts.shape[0] // 2
    place.copy(
        part_of(r.parts, 1 - place.core, half), r.pair_got, r.pair_sems, 1
    ).start()
    r.vectors[...] = jnp.concatenate(
        [gain_one, gain_two, bias_sum, gain_three, bias_three, jnp.zeros((3, width), f32)], axis=0
    )
    r.stores["vectors"].start()
    r.grad_mixed[...] = grad_mixed
    r.grad[...] = grad_first + grad_second + grad_mixed


def edges_back(r, place):
    rows, width = r.x.shape
    grad_mixed = r.grad_mixed[...]
    back = jnp.zeros((3 * rows, width), f32)
    for k in range(EDGES):
        back = back + dot(r.selects[k], (r.slopes[k] * grad_mixed).astype(bf16))
    r.edge_send[0] = back[2 * rows :].astype(bf16)
    r.edge_send[1] = back[:rows].astype(bf16)
    up, down = halo(
        r, place, r.edge_send.at[0], r.edge_send.at[1], r.edge_got.at[0], r.edge_got.at[1], 1
    )
    start_halo(place, up, down)
    r.grad[...] += back[rows : 2 * rows]
    return up, down


def spread(v):
    cols = v.shape[1]
    parts = [part.astype(f32) for part in three_parts(v)]
    row = lax.broadcasted_iota(jnp.int32, (16, cols), 0)
    out = jnp.where(row == 0, parts[0], 0.0)
    out = jnp.where(row == 1, parts[1], out)
    return jnp.where(row == 2, parts[2], out).astype(bf16)


def attend_back(r, place, depth):
    planes = place.planes
    cols = r.q.shape[2]
    width = HEADS * cols
    share = r.parts.shape[0] // HEADS
    slice_rows = share // planes
    place.wait(r.do.at[pl.ds(0, HEADS - 1)], r.do_sems)
    for b in range(HEADS):
        qs = slice(b * cols, (b + 1) * cols)
        grad = r.do[b].astype(f32)
        inner = jnp.sum(grad * r.attended[:, qs], axis=0, keepdims=True)
        r.grad_rows[:, qs] = r.do[b]
        r.grads[:, qs] = jnp.concatenate(
            list(three_parts(grad * score_scale))
            + [spread(inner * -score_scale), jnp.zeros((16, cols), bf16)],
            axis=0,
        )
    place.wait(r.pair_got, r.pair_sems)
    pair = part_of(r.parts, place.core, 4 * share)[...].astype(f32) + r.pair_got[...].astype(f32)
    r.pair_sum[...] = pair.astype(bf16)
    place.to_chips(
        lambda spot: part_of(r.pair_sum, spot, share), lambda k: r.chips_got.at[k], r.parts_sems
    )
    query_rows = jnp.concatenate([r.q[b] for b in range(HEADS)], axis=1)
    r.query_rows[...] = query_rows
    r.dq_total[...] = jnp.zeros_like(r.dq_total)

    def plane_of_keys(k):
        plane = place.plane(k)
        slot = lax.rem(k, 2)

        @pl.when(k < planes - 2)
        def weights_back():
            load_weights(r, k).wait()

        for b in range(HEADS):
            vt = r.kv[plane * HEADS + b, HDIM : 2 * HDIM]
            r.values[b * cols : (b + 1) * cols, :] = jnp.concatenate(
                [vt, vt, vt, jnp.ones((HDIM, cols), bf16)], axis=0
            ).T
        r.factors[...] = jnp.exp2(r.tops[k] - r.logs[0:1, :])

        def ahead(a, b):
            ks, qs = slice(a * cols, (a + 1) * cols), slice(b * cols, (b + 1) * cols)
            return dot(r.values[ks, :], r.grads[:, qs])

        sums = [None, None]

        def behind(a, b, product):
            ks, qs = slice(a * cols, (a + 1) * cols), slice(b * cols, (b + 1) * cols)
            probs = r.kept[slot, ks, qs].astype(f32) * r.factors[a : a + 1, qs]
            grad_scores = (probs * product).astype(bf16)
            r.dq_total[:, qs] += dot(r.kv[plane * HEADS + a, 0:HDIM], grad_scores)
            dk = dot(r.query_rows[:, qs], grad_scores, 1, 1)
            dv = dot(r.grad_rows[:, qs], probs.astype(bf16), 1, 1)
            sums[:] = (dk, dv) if b == 0 else (sums[0] + dk, sums[1] + dv)
            if b == HEADS - 1:
                r.dkv_part[plane * HEADS + a] = jnp.concatenate(sums, axis=0).astype(bf16)

        pipelined(ahead, behind, depth)

    def plane_step(step, _):
        k = planes - 1 - step
        plane_of_keys(k)

        @pl.when(k >= 2)
        def next_weights():
            load_weights(r, k - 2).start()

        bit = 1
        while bit < planes:
            if 2 * bit < planes:

                @pl.when(jnp.logical_and(k > 0, lax.rem(k, 2 * bit) == 0))
                def add_part(bit=bit):
                    place.wait(r.dkv_got.at[0], r.dkv_sems.at[k + bit])
                    mine = part_of(r.dkv_part, place.plane(k), HEADS)
                    mine[...] = (
                        mine[...].astype(f32) + r.dkv_got[k + bit].astype(f32)
                    ).astype(bf16)

            @pl.when(lax.rem(k, 2 * bit) == bit)
            def send_part(bit=bit):
                place.copy(
                    part_of(r.dkv_part, place.plane(k), HEADS),
                    r.dkv_got.at[k],
                    r.dkv_sems.at[k],
                    bit * HEADS,
                ).start()

            bit *= 2

        @pl.when(step == 0)
        def sum_plane():
            place.wait(r.chips_got.at[pl.ds(1, HEADS // 2 - 1)], r.parts_sems)
            total = part_of(r.pair_sum, place.chip, share)[...].astype(f32) + total_of(
                r.chips_got, 1
            )
            r.plane_sum[...] = total.astype(bf16)
            place.to_line(
                lambda spot: part_of(r.plane_sum, spot, slice_rows),
                lambda k: r.line_got.at[k],
                r.line_sems.at[0],
            )

        @pl.when(step == 1)
        def sum_line():
            place.wait(r.line_got.at[pl.ds(1, planes - 1)], r.line_sems.at[0])
            total = part_of(r.plane_sum, place.z, slice_rows)[...].astype(f32) + total_of(
                r.line_got, 1
            )
            r.line_sum[place.z] = total.astype(bf16)
            place.to_line(
                lambda spot: r.line_sum.at[place.z],
                lambda k: r.line_sum.at[place.z],
                r.line_sems.at[1],
            )

        @pl.when(step == 2)
        def spread_line():
            place.wait(r.line_sum.at[pl.ds(1, planes - 1)], r.line_sems.at[1])
            r.sums[place.share] = r.line_sum[...].reshape(share, cols)
            place.to_chips(
                lambda spot: r.sums.at[place.share],
                lambda k: r.sums.at[place.share],
                r.whole_sems.at[0],
            )

        return 0

    lax.fori_loop(0, planes, plane_step, 0)
    place.wait(r.sums.at[pl.ds(0, HEADS // 2 - 1)], r.whole_sems.at[0])
    own_half = part_of(r.sums, place.core, HEADS // 2)
    place.copy(own_half, own_half, r.whole_sems.at[1], 1).start()
    place.wait(r.x_all.at[pl.ds(0, HEADS - 1)], r.x_sems)
    dkv = part_of(r.dkv_part, place.z, HEADS)[...].astype(f32)
    bit = 1
    while bit < planes:
        place.wait(r.dkv_got.at[0], r.dkv_sems.at[bit])
        dkv = dkv + r.dkv_got[bit].astype(f32)
        bit *= 2
    for b in range(HEADS):
        r.back_send[b, 0:HDIM] = r.dq_total[:, b * cols : (b + 1) * cols].astype(bf16)
        r.back_send[b, HDIM : 3 * HDIM] = dkv[b].astype(bf16)
    place.to_plane(
        lambda spot: r.back_send.at[spot], r.back.at[place.p], r.back_sems
    )
    r.back[place.p] = r.back_send[place.p]
    total = dot(r.back_send[0], r.x_all[0])
    for b in range(1, HEADS):
        total = total + dot(r.back_send[b], r.x_all[b])
    r.heads_part[...] = total.astype(bf16)
    place.to_line(lambda spot: r.heads_part, lambda k: r.heads_got.at[k], r.heads_sems)
    halo_copies = edges_back(r, place)
    place.wait(r.heads_got.at[pl.ds(1, planes - 1)], r.heads_sems)
    total = r.heads_part[...].astype(f32) + total_of(r.heads_got, 1)
    r.heads[place.share] = total.astype(bf16)
    place.to_chips(
        lambda spot: r.heads.at[place.share],
        lambda k: r.heads.at[place.share],
        r.last_sems.at[0],
    )
    place.wait(r.back.at[pl.ds(0, HEADS - 1)], r.back_sems)
    grad = r.grad[...]
    for s, w in enumerate((r.wq, r.wk, r.wv)):
        part = jnp.concatenate(
            [r.back[h, HDIM * s : HDIM * (s + 1)] for h in range(HEADS)], axis=0
        )
        grad = grad + dot(part.T, w[...], 1, 1)
    place.wait(r.heads.at[pl.ds(0, HEADS // 2 - 1)], r.last_sems.at[0])
    own_half = part_of(r.heads, place.core, HEADS // 2)
    place.copy(own_half, own_half, r.last_sems.at[1], 1).start()
    wait_halo(place, *halo_copies)
    r.grad[...] = grad + r.edge_got[0].astype(f32) + r.edge_got[1].astype(f32)
    r.stores["grad"].start()
    place.wait(r.sums.at[pl.ds(0, HEADS // 2)], r.whole_sems.at[1])
    r.stores["sums"].start()
    place.wait(r.heads.at[pl.ds(0, HEADS // 2)], r.last_sems.at[1])
    r.stores["heads"].start()


def layer_kernel(count, cores, names, args, outs, *refs):
    r = Refs(names, refs)
    place = Place(count, cores)
    r.loads = {
        name: pltpu.make_async_copy(
            getattr(r, "from_" + name), getattr(r, name), r.load_sems.at[i]
        )
        for i, name in enumerate(args)
    }
    r.stores = {
        name: pltpu.make_async_copy(getattr(r, name), getattr(r, "to_" + name), r.store_sems.at[i])
        for i, name in enumerate(outs)
    }
    for load in r.loads.values():
        load.start()
    halo_copies = project(r, place)

    def beside():
        r.need("step", "degree", "edge", "w1", "b1", "w2")
        wait_halo(place, *halo_copies)
        gine_forward(r, place)

    attend(r, place, 6, halo_copies, beside)
    r.need("up", "out_w", "f1", "fb", "f2", "g1", "g2", "b2", "g3", "b3")
    norms(r, place)
    attend_back(r, place, 6)
    for store in r.stores.values():
        store.wait()


def finish_kernel(
    grad_ref,
    heads_ref,
    sums_ref,
    result_ref,
    vectors_ref,
    result_out,
    grad_out,
    gw1_out,
    gb1_out,
    gw2_out,
    qw_out,
    kw_out,
    vw_out,
    ow_out,
    f1_out,
    fb_out,
    f2_out,
    gain1_out,
    gain2_out,
    bias2_out,
    gain3_out,
    bias3_out,
):
    width = grad_ref.shape[1]
    result_out[...] = result_ref[...]
    grad_out[...] = grad_ref[...]
    for s, w_out in enumerate((qw_out, kw_out, vw_out)):
        cols = slice(HDIM * s, HDIM * (s + 1))
        spots = [h % 2 * (HEADS // 2) + h // 2 for h in range(HEADS)]
        total = jnp.concatenate([heads_ref[spot, cols] for spot in spots], axis=0)
        w_out[...] = total.T.astype(f32)
    gw1_out[...] = sums_ref[0:width].astype(f32)
    gw2_out[...] = sums_ref[width : 2 * width].astype(f32)
    ow_out[...] = sums_ref[2 * width : 3 * width].astype(f32)
    f1_out[:, 0:width] = sums_ref[3 * width : 4 * width].astype(f32)
    f1_out[:, width:] = sums_ref[4 * width : 5 * width].astype(f32)
    last = 5 * width + f2_out.shape[0]
    f2_out[...] = sums_ref[5 * width : last].astype(f32)
    rows_left = sums_ref[last : last + 16].astype(f32)
    gb1_out[...] = rows_left[0:1]
    fb_out[:, 0:width] = rows_left[1:2]
    fb_out[:, width:] = rows_left[2:3]
    for k, out in enumerate((gain1_out, gain2_out, bias2_out, gain3_out, bias3_out)):
        out[...] = vectors_ref[k : k + 1]


def on_device(
    count,
    cores,
    node_feat,
    edge_feat,
    edge_step,
    degree,
    graph_len,
    gine_w1,
    gine_b1,
    gine_w2,
    query_w,
    key_w,
    value_w,
    out_w,
    ffn_w1,
    ffn_b1,
    ffn_w2,
    norm1_gain,
    norm2_gain,
    norm2_bias,
    norm3_gain,
    norm3_bias,
    out_grad,
):
    rows, width = node_feat.shape
    ffn = ffn_w1.shape[1]
    planes = count // HEADS
    plane_rows = HEADS * rows
    vmem = pl.BlockSpec(memory_space=pltpu.VMEM)
    dma = pltpu.SemaphoreType.DMA
    shape = jax.ShapeDtypeStruct
    share_unit = 16 * HEADS * planes
    needed = 3 * width + 2 * ffn + 16
    part_rows = -(-needed // share_unit) * share_unit
    share = part_rows // HEADS

    def row(v):
        return v.reshape(1, -1)

    args = dict(
        x=node_feat,
        wk=key_w,
        wv=value_w,
        wq=query_w,
        step=edge_step.T,
        degree=row(degree),
        edge=edge_feat,
        w1=gine_w1,
        b1=row(gine_b1),
        w2=gine_w2,
        up=out_grad,
        out_w=out_w,
        f1=ffn_w1,
        fb=row(ffn_b1),
        f2=ffn_w2,
        g1=row(norm1_gain),
        g2=row(norm2_gain),
        b2=row(norm2_bias),
        g3=row(norm3_gain),
        b3=row(norm3_bias),
    )
    outs = dict(
        result=shape((rows, width), bf16),
        grad=shape((rows, width), f32),
        vectors=shape((8, width), f32),
        heads=shape((HEADS, 3 * HDIM, width), bf16),
        sums=shape((HEADS, share, width), bf16),
    )
    scratch = dict(
        ext=pltpu.VMEM((3 * rows, width), bf16),
        kv_send=pltpu.VMEM((HEADS, 2 * HDIM, rows), bf16),
        q_send=pltpu.VMEM((HEADS, HDIM, rows), bf16),
        kv=pltpu.VMEM((count, 2 * HDIM, rows), bf16),
        q=pltpu.VMEM((HEADS, HDIM, rows), bf16),
        source=pltpu.VMEM((EDGES, rows), jnp.int32),
        slopes=pltpu.VMEM((EDGES, rows, width), f32),
        selects=pltpu.VMEM((EDGES, 3 * rows, rows), bf16),
        mixed=pltpu.VMEM((rows, width), bf16),
        active=pltpu.VMEM((rows, width), bf16),
        hidden_slope=pltpu.VMEM((rows, width), f32),
        res_one=pltpu.VMEM((rows, width), f32),
        grad_mixed=pltpu.VMEM((rows, width), f32),
        keys=pltpu.VMEM((plane_rows, 128), bf16),
        value_rows=pltpu.VMEM((HDIM + 16, plane_rows), bf16),
        values=pltpu.VMEM((plane_rows, 128), bf16),
        queries=pltpu.VMEM((128, plane_rows), bf16),
        grads=pltpu.VMEM((128, plane_rows), bf16),
        query_rows=pltpu.VMEM((HDIM, plane_rows), bf16),
        grad_rows=pltpu.VMEM((HDIM, plane_rows), bf16),
        factors=pltpu.VMEM((8, plane_rows), f32),
        kept=pltpu.VMEM((2, plane_rows, plane_rows), bf16),
        tops=pltpu.VMEM((planes, 8, plane_rows), f32),
        total=pltpu.VMEM((HDIM + 16, plane_rows), f32),
        top=pltpu.VMEM((8, plane_rows), f32),
        logs=pltpu.VMEM((8, plane_rows), f32),
        attended=pltpu.VMEM((HDIM, plane_rows), f32),
        att_send=pltpu.VMEM((HEADS, HDIM, rows), bf16),
        att_got=pltpu.VMEM((HEADS, HDIM, rows), bf16),
        do_send=pltpu.VMEM((HEADS, HDIM, rows), bf16),
        do=pltpu.VMEM((HEADS, HDIM, rows), bf16),
        stat0=pltpu.VMEM((count, 8, width // 2), f32),
        stat1=pltpu.VMEM((count, 8, width // 2), f32),
        stat2=pltpu.VMEM((count, 8, width // 2), f32),
        edge_send=pltpu.VMEM((2, rows, width), bf16),
        edge_got=pltpu.VMEM((2, rows, width), bf16),
        x_all=pltpu.VMEM((HEADS, rows, width), bf16),
        parts=pltpu.VMEM((part_rows, width), bf16),
        pair_got=pltpu.VMEM((part_rows // 2, width), bf16),
        pair_sum=pltpu.VMEM((part_rows // 2, width), bf16),
        chips_got=pltpu.VMEM((HEADS // 2, share, width), bf16),
        plane_sum=pltpu.VMEM((share, width), bf16),
        line_got=pltpu.VMEM((planes, share // planes, width), bf16),
        line_sum=pltpu.VMEM((planes, share // planes, width), bf16),
        dq_total=pltpu.VMEM((HDIM, plane_rows), f32),
        dkv_part=pltpu.VMEM((count, 2 * HDIM, rows), bf16),
        dkv_got=pltpu.VMEM((planes, HEADS, 2 * HDIM, rows), bf16),
        back_send=pltpu.VMEM((HEADS, 3 * HDIM, rows), bf16),
        back=pltpu.VMEM((HEADS, 3 * HDIM, rows), bf16),
        heads_part=pltpu.VMEM((3 * HDIM, width), bf16),
        heads_got=pltpu.VMEM((planes, 3 * HDIM, width), bf16),
        kv_sems=dma((planes, 2, 2)),
        halo_sems=dma((2, 4)),
        stat_sems=dma((3, 2)),
        line_sems=dma((2, 2)),
        dkv_sems=dma((planes, 2)),
        far_sems=dma((2, 2)),
        whole_sems=dma((2, 2)),
        last_sems=dma((2, 2)),
        **{
            name + "_sems": dma((2,))
            for name in ("q", "att", "do", "x", "pair", "parts", "back", "heads")
        },
    )
    scratch = dict(
        **{name: pltpu.VMEM(v.shape, v.dtype) for name, v in (args | outs).items()},
        **scratch,
        load_sems=dma((len(args),)),
        store_sems=dma((len(outs),)),
    )
    names = (
        "graph_len",
        *("from_" + name for name in args),
        *("to_" + name for name in outs),
        "far",
        *scratch,
    )
    anywhere = pl.BlockSpec(memory_space=pl.ANY)
    far = shape((planes - 2, plane_rows, plane_rows), bf16)
    result, grad, vectors, heads, sums, _ = pl.pallas_call(
        functools.partial(layer_kernel, count, cores, names, tuple(args), tuple(outs)),
        out_shape=(*outs.values(), far),
        in_specs=[pl.BlockSpec(memory_space=pltpu.SMEM)] + [anywhere] * len(args),
        out_specs=(anywhere,) * (len(outs) + 1),
        scratch_shapes=list(scratch.values()),
        compiler_params=pltpu.CompilerParams(
            vmem_limit_bytes=62 << 20, collective_id=1, has_side_effects=True
        ),
    )(graph_len, *args.values())

    square = shape((width, width), f32)
    line = shape((1, width), f32)
    done = pl.pallas_call(
        finish_kernel,
        out_shape=(
            shape((rows, width), bf16),
            shape((rows, width), f32),
            square,
            line,
            square,
            square,
            square,
            square,
            square,
            shape((width, ffn), f32),
            shape((1, ffn), f32),
            shape((ffn, width), f32),
        )
        + (line,) * 5,
        in_specs=[vmem] * 5,
        out_specs=(vmem,) * 17,
        compiler_params=pltpu.CompilerParams(vmem_limit_bytes=60 << 20),
    )(grad, heads, sums.reshape(part_rows, width), result, vectors)
    return tuple(v.reshape(-1) if v.shape[0] == 1 else v for v in done)


def solution(mesh):
    count = mesh.shape["blk"] * mesh.shape["rep"]
    rows = P(AXES, None)
    whole = P()
    return jax.shard_map(
        functools.partial(on_device, count, mesh.shape["rep"]),
        mesh=mesh,
        in_specs=(rows, P(AXES, None, None), rows, P(AXES)) + (whole,) * 16 + (rows,),
        out_specs=(rows, rows) + (whole,) * 15,
        check_vma=False,
    )
```

```python
import functools
import jax
import jax.numpy as jnp
from jax import lax
from jax.experimental import pallas as pl
from jax.experimental.pallas import tpu as pltpu
from jax.sharding import PartitionSpec as P

HEADS = 8
HDIM = 32
EDGES = 8
GRAPHS = 9
AXES = ("blk", "rep")
MESH = pl.DeviceIdType.MESH
bf16 = jnp.bfloat16
f32 = jnp.float32

norm_eps = 1e-05
far_score = -1e30
log2_e = 1.4426950408889634
score_scale = HDIM ** (-0.5)
gelu_c = 0.7978845608028654
gelu_a = 0.044715


def dot(left, right, left_dim=1, right_dim=0):
    return lax.dot_general(
        left, right, (((left_dim,), (right_dim,)), ((), ())), preferred_element_type=f32
    )


def gelu(v):
    return 0.5 * v * (1.0 + jnp.tanh(gelu_c * (v + gelu_a * (v * v * v))))


def gelu_slope(v):
    squared = v * v
    bend = jnp.tanh(gelu_c * v * (1.0 + gelu_a * squared))
    return 0.5 * (1.0 + bend) + 0.5 * v * (1.0 - bend * bend) * (
        gelu_c * (1.0 + 3.0 * gelu_a * squared)
    )


def three_parts(v):
    first = v.astype(bf16)
    rest = v - first.astype(f32)
    second = rest.astype(bf16)
    third = (rest - second.astype(f32)).astype(bf16)
    return first, second, third


class Place:
    def __init__(self, count, cores):
        self.count = count
        self.cores = cores
        self.planes = count // HEADS
        self.blk = lax.axis_index("blk")
        self.rep = lax.axis_index("rep")
        self.me = self.blk * cores + self.rep
        self.z = lax.div(self.me, HEADS)
        self.p = self.me - self.z * HEADS
        self.chip = lax.div(self.p, 2)
        self.core = self.p - 2 * self.chip
        self.share = self.core * (HEADS // 2) + self.chip
        self.steps = []
        bit, rest = 1, self.me
        while bit < count:
            half = lax.div(rest, 2)
            self.steps.append(bit * (1 - 2 * (rest - 2 * half)))
            bit, rest = 2 * bit, half

    def move(self, k, first=0, last=None):
        total = 0
        for j, step in enumerate(self.steps[first:last]):
            bit = 1 << (first + j)
            if isinstance(k, int):
                if k & bit:
                    total = total + step
            else:
                total = total + lax.rem(lax.div(k, bit), 2) * step
        return total

    def device(self, k):
        low = self.cores.bit_length() - 1
        return {
            "blk": self.blk + lax.div(self.move(k, low), self.cores),
            "rep": self.rep + self.move(k, 0, low),
        }

    def peer(self, k):
        return self.me + self.move(k)

    def spot(self, k):
        return self.p + self.move(k, 0, 3)

    def plane(self, k):
        return self.z + lax.div(self.move(k * HEADS, 3), HEADS)

    def loop(self, first, last, body):
        if last - first <= 32:
            for k in range(first, last):
                body(k)
        else:

            def step(k, _):
                body(k)
                return 0

            lax.fori_loop(first, last, step, 0)

    def greet(self):
        def hello(k):
            pl.semaphore_signal(
                pltpu.get_barrier_semaphore(),
                inc=1,
                device_id=self.device(self.count - k),
                device_id_type=MESH,
            )

        self.loop(1, self.count, hello)

    def greeted(self):
        pl.semaphore_wait(pltpu.get_barrier_semaphore(), self.count - 1)

    def copy(self, src, dst, sems, k):
        return self.copy_to(src, dst, sems.at[0], sems.at[1], self.device(k))

    def copy_to(self, src, dst, send_sem, recv_sem, device):
        return pltpu.make_async_remote_copy(
            src_ref=src,
            dst_ref=dst,
            send_sem=send_sem,
            recv_sem=recv_sem,
            device_id=device,
            device_id_type=MESH,
        )

    def to_plane(self, src_of, dst, sems):
        for k in reversed(range(1, HEADS)):
            self.copy(src_of(self.spot(k)), dst, sems, k).start()

    def to_line(self, src_of, dst_of, sems):
        for k in range(1, self.planes):
            self.copy(src_of(self.plane(k)), dst_of(k), sems, k * HEADS).start()

    def to_chips(self, src_of, dst_of, sems):
        for k in range(1, HEADS // 2):
            there = self.chip + lax.div(self.move(2 * k, 1, 3), 2)
            self.copy(src_of(there), dst_of(k), sems, 2 * k).start()

    def wait(self, like, sems):
        self.copy(like, like, sems, 1).wait()


def part_of(ref, spot, size):
    return ref.at[pl.ds(pl.multiple_of(spot * size, size), size)]


def total_of(ref, start=0):
    total = ref[start].astype(f32)
    for k in range(start + 1, ref.shape[0]):
        total = total + ref[k].astype(f32)
    return total


def col_sum(v):
    return jnp.sum(v, axis=0, keepdims=True)


def stack_rows(rows, width):
    four = jnp.concatenate(rows + [jnp.zeros((1, width), f32)] * (4 - len(rows)), axis=0)
    return jnp.concatenate([four[:, : width // 2], four[:, width // 2 :]], axis=0)


def graph_bounds(len_ref, positions):
    last = 0
    graph = jnp.zeros(positions.shape, jnp.int32)
    start = jnp.zeros(positions.shape, jnp.int32)
    ends = []
    for g in range(GRAPHS):
        last = last + len_ref[g]
        ends.append(last)
        passed = positions >= last
        graph = graph + passed.astype(jnp.int32)
        start = jnp.where(passed, last, start)
    stop = jnp.full(positions.shape, ends[-1], jnp.int32)
    for end in reversed(ends):
        stop = jnp.where(positions < end, end, stop)
    return graph, start, stop


def own_graph(len_ref, first, width):
    positions = first + lax.broadcasted_iota(jnp.int32, (1, width), 1)
    graph, _, _ = graph_bounds(len_ref, positions)
    rows = lax.broadcasted_iota(jnp.int32, (16, width), 0)
    return rows == graph


def as_columns(rows, width):
    return jnp.concatenate([rows, jnp.zeros((128 - rows.shape[0], width), f32)], axis=0).T


def gelu_and_slope(v):
    squared = v * v
    bend = jnp.tanh(gelu_c * v * (1.0 + gelu_a * squared))
    half = 0.5 * (1.0 + bend)
    slope = half + 0.5 * v * (1.0 - bend * bend) * (gelu_c * (1.0 + 3.0 * gelu_a * squared))
    return v * half, slope


class Refs:
    def __init__(self, names, refs):
        for name, ref in zip(names, refs, strict=True):
            setattr(self, name, ref)

    def need(self, *names):
        for name in names:
            self.loads[name].wait()


def share_stats(place, stats, buffer, sems, between):
    buffer[place.me] = stats

    def begin(k):
        place.copy(buffer.at[place.me], buffer.at[place.me], sems, place.count - k).start()

    place.loop(1, place.count, begin)
    between()
    place.wait(buffer.at[pl.ds(0, place.count - 1)], sems)
    return jnp.concatenate([buffer[:, 0:4, :], buffer[:, 4:8, :]], axis=2)


def project(r, place):
    rows, width = r.x.shape
    count = place.count
    r.edge_got[...] = jnp.zeros_like(r.edge_got)
    r.need("x")
    x = r.x[...]
    r.ext[0:rows, :] = jnp.zeros_like(x)
    r.ext[rows : 2 * rows, :] = x
    r.ext[2 * rows :, :] = jnp.zeros_like(x)
    place.greet()
    xt = x.T
    r.need("wk", "wv", "wq")
    kt = dot(r.wk[...].T, xt).astype(bf16)
    vt = dot(r.wv[...].T, xt).astype(bf16)
    for h in range(HEADS):
        cols = slice(HDIM * h, HDIM * (h + 1))
        r.kv_send[h, 0:HDIM] = kt[cols]
        r.kv_send[h, HDIM : 2 * HDIM] = vt[cols]
    qt = dot(r.wq[...].T, xt).astype(bf16)
    for h in range(HEADS):
        r.q_send[h] = qt[HDIM * h : HDIM * (h + 1)]
    r.need("step", "degree")
    edge_sources(r, place)
    place.greeted()

    place.to_plane(lambda spot: r.kv_send.at[spot], r.kv.at[place.me], r.kv_sems.at[0, 0])
    place.to_plane(lambda spot: r.q_send.at[spot], r.q.at[place.p], r.q_sems)
    half = lax.div(place.p, HEADS // 2)
    for k in reversed(range(HEADS)):
        place.copy_to(
            r.kv_send.at[place.spot(k)],
            r.kv.at[place.me],
            r.kv_sems.at[0, 1, 0],
            r.kv_sems.at[place.planes // 2, half, 1],
            place.device(count // 2 + k),
        ).start()
    up, down = halo(r, place, r.x, r.x, r.ext.at[pl.ds(0, rows)], r.ext.at[pl.ds(2 * rows, rows)])
    r.kv[place.me] = r.kv_send[place.p]
    r.q[place.p] = r.q_send[place.p]
    return up, down


def pass_on(r, place, dz, bit, half):
    rows = part_of(r.kv, 2 * place.plane(dz) + half, HEADS // 2)
    place.copy(rows, rows, r.kv_sems.at[dz + bit, half], bit * HEADS).start()


def pass_down(r, place, dz, half):
    bit = 1
    while bit < place.planes // 2:
        pl.when(lax.rem(dz, 2 * bit) == 0)(functools.partial(pass_on, r, place, dz, bit, half))
        bit *= 2


def kv_arrived(r, place, dz, half):
    like = r.kv.at[pl.ds(0, HEADS // 2)]
    place.copy(like, like, r.kv_sems.at[dz, half], 1).wait_recv()


def kv_sent(r, place):
    like = r.kv.at[pl.ds(0, HEADS // 2)]
    for dz in range(1, place.planes):
        if dz != place.planes // 2:
            for half in range(2):
                place.copy(like, like, r.kv_sems.at[dz, half], 1).wait_send()
    like = r.kv.at[pl.ds(0, HEADS)]
    place.copy(like, like, r.kv_sems.at[0, 1], 1).wait_send()


def halo(r, place, up_src, down_src, up_dst, down_dst, which=0):
    def neighbour(index):
        blk = lax.div(index, place.cores)
        return {"blk": blk, "rep": index - blk * place.cores}

    sems = r.halo_sems.at[which]
    last = place.count - 1
    after = neighbour(jnp.minimum(place.me + 1, last))
    before = neighbour(jnp.maximum(place.me - 1, 0))
    up = place.copy_to(up_src, up_dst, sems.at[0], sems.at[1], after)
    down = place.copy_to(down_src, down_dst, sems.at[2], sems.at[3], before)
    return up, down


def start_halo(place, up, down):
    @pl.when(place.me < place.count - 1)
    def send_up():
        up.start()

    @pl.when(place.me > 0)
    def send_down():
        down.start()


def wait_halo(place, up, down):
    @pl.when(place.me < place.count - 1)
    def with_after():
        up.wait_send()
        down.wait_recv()

    @pl.when(place.me > 0)
    def with_before():
        down.wait_send()
        up.wait_recv()


def edge_sources(r, place):
    rows = r.x.shape[0]
    positions = place.me * rows + lax.broadcasted_iota(jnp.int32, (1, rows), 1)
    _, start, stop = graph_bounds(r.graph_len, positions)
    source = jnp.minimum(jnp.maximum(positions + r.step[...], start), stop - 1)
    source = source - place.me * rows + rows
    r.columns[...] = as_columns(
        jnp.concatenate([source.astype(f32), r.degree[...].astype(f32)], axis=0), rows
    )
    cells = lax.broadcasted_iota(jnp.int32, (3 * rows, rows), 0)
    for k in range(EDGES):
        r.selects[k] = (source[k : k + 1, :] == cells).astype(f32).astype(bf16)


def gine_forward(r, place):
    rows, width = r.x.shape
    columns = r.columns[...]
    cells = lax.broadcasted_iota(jnp.int32, (rows, 3 * rows), 1).astype(f32)
    x = r.x[...].astype(f32)
    message = jnp.zeros_like(x)
    around = r.ext[...]
    for k in range(EDGES):
        select = (columns[:, k : k + 1] == cells).astype(f32).astype(bf16)
        v = dot(select, around) + r.edge[:, k, :].astype(f32)
        present = columns[:, EDGES : EDGES + 1] > k
        value, slope = gelu_and_slope(v)
        message = message + jnp.where(present, value, 0.0)
        r.slopes[k] = jnp.where(present, slope, 0.0)
    mixed = (x + message).astype(bf16)
    r.mixed[...] = mixed
    hidden = dot(mixed, r.w1[...]) + r.b1[...]
    value, slope = gelu_and_slope(hidden)
    active = value.astype(bf16)
    r.active[...] = active
    r.hidden_slope[...] = slope
    r.res_one[...] = x + dot(active, r.w2[...])


def build_keys(r, plane, a):
    cols = r.q.shape[2]
    block = plane * HEADS + a
    kt = r.kv[block, 0:HDIM]
    same = own_graph(r.graph_len, block * cols, cols).astype(f32).astype(bf16)
    ones = jnp.ones((16, cols), bf16)
    r.keys[a * cols : (a + 1) * cols, :] = jnp.concatenate([kt, kt, kt, same, ones], axis=0).T
    r.value_rows[0:HDIM, a * cols : (a + 1) * cols] = r.kv[block, HDIM : 2 * HDIM]


def build_queries(r, place, last_rows):
    cols = r.q.shape[2]
    for b in range(HEADS):
        parts = three_parts(r.q[b].astype(f32) * (score_scale * log2_e))
        same = own_graph(r.graph_len, (place.z * HEADS + b) * cols, cols)
        known = lax.broadcasted_iota(jnp.int32, (16, cols), 0) < GRAPHS
        mask = jnp.where(jnp.logical_or(same, jnp.logical_not(known)), 0.0, far_score).astype(bf16)
        r.queries[:, b * cols : (b + 1) * cols] = jnp.concatenate(
            list(parts) + [mask, last_rows(b)], axis=0
        )


def store_weights(r, dz):
    slot = lax.rem(dz, 2)
    return pltpu.make_async_copy(r.kept.at[slot], r.far.at[dz], r.far_sems.at[0, slot])


def load_weights(r, dz):
    slot = lax.rem(dz, 2)
    return pltpu.make_async_copy(r.far.at[dz], r.kept.at[slot], r.far_sems.at[1, slot])


def pipelined(ahead, behind, depth):
    pairs = [(a, b) for a in range(HEADS) for b in range(HEADS)]
    waiting = [ahead(*pair) for pair in pairs[:depth]]
    for i, pair in enumerate(pairs):
        if i + depth < len(pairs):
            waiting.append(ahead(*pairs[i + depth]))
        behind(*pair, waiting.pop(0))


def attend(r, place, depth, halo_copies):
    cols = r.q.shape[2]
    width = HEADS * cols
    place.wait(r.kv.at[pl.ds(0, HEADS - 1)], r.kv_sems.at[0, 0])
    for half in range(2):
        bit = 1
        while bit < place.planes // 2:
            pass_on(r, place, 0, bit, half)
            bit *= 2
    start_halo(place, *halo_copies)
    place.to_plane(lambda spot: r.x, r.x_all.at[place.p], r.x_sems)
    r.x_all[place.p] = r.x[...]
    place.wait(r.q.at[pl.ds(0, HEADS - 1)], r.q_sems)
    build_queries(r, place, lambda b: jnp.zeros((16, cols), bf16))
    r.total[...] = jnp.zeros_like(r.total)
    r.value_rows[HDIM:, :] = jnp.ones((16, width), bf16)
    r.top[...] = jnp.full(r.top.shape, 2.0 * far_score, f32)
    farthest = place.planes // 2

    def plane_step(dz, _):
        plane = place.plane(dz)

        @pl.when(jnp.logical_and(dz > 0, dz != farthest))
        def arrived():
            for half in range(2):
                kv_arrived(r, place, dz, half)
                pass_down(r, place, dz, half)

        slot = lax.rem(dz, 2)

        @pl.when(dz >= 2)
        def slot_free():
            store_weights(r, dz - 2).wait()

        def ahead(a, b):
            ks, qs = slice(a * cols, (a + 1) * cols), slice(b * cols, (b + 1) * cols)
            if b == 0:
                build_keys(r, plane, a)
            return dot(r.keys[ks, :], r.queries[:, qs])

        def behind(a, b, scores):
            ks, qs = slice(a * cols, (a + 1) * cols), slice(b * cols, (b + 1) * cols)
            before = r.top[0:1, qs]
            now = jnp.maximum(before, jnp.max(scores, axis=0, keepdims=True))
            weights = jnp.exp2(scores - now).astype(bf16)
            r.kept[slot, ks, qs] = weights
            r.total[:, qs] = r.total[:, qs] * jnp.exp2(before - now) + dot(
                r.value_rows[:, ks], weights
            )
            r.top[0:1, qs] = now
            r.tops[dz, a : a + 1, qs] = now

        pipelined(ahead, behind, depth)

        @pl.when(dz < place.planes - 2)
        def away():
            store_weights(r, dz).start()

        @pl.when(dz == 0)
        def after_own():
            for half in range(2):
                kv_arrived(r, place, farthest, half)
                pass_down(r, place, farthest, half)

        return 0

    lax.fori_loop(0, place.planes, plane_step, 0)
    kv_sent(r, place)
    sums = r.total[HDIM : HDIM + 1, :]
    r.logs[0:1, :] = r.top[0:1, :] + jnp.log2(sums)
    attended = r.total[0:HDIM, :] / sums
    r.attended[...] = attended
    for b in range(HEADS):
        r.att_send[b] = attended[:, b * cols : (b + 1) * cols].astype(bf16)


def norms(r, place, halo_copies):
    rows, width = r.x.shape
    count = place.count
    total_rows = rows * count
    place.to_plane(lambda spot: r.att_send.at[spot], r.att_got.at[place.p], r.att_sems)
    r.att_got[place.p] = r.att_send[place.p]
    wait_halo(place, *halo_copies)
    gine_forward(r, place)
    x = r.x[...].astype(f32)
    res_one = r.res_one[...]

    def centre(v):
        mean = col_sum(v) / rows
        off = v - mean
        return mean, col_sum(off * off)

    def combine(means, squares):
        mean = jnp.sum(means, axis=0, keepdims=True) / count
        off = means - mean
        var = (
            jnp.sum(squares, axis=0, keepdims=True)
            + rows * jnp.sum(off * off, axis=0, keepdims=True)
        ) / total_rows
        return mean, lax.rsqrt(var + norm_eps)

    first_stats = centre(res_one)
    place.wait(r.att_got.at[pl.ds(0, HEADS - 1)], r.att_sems)
    att_half = jnp.concatenate([r.att_got[h] for h in range(HEADS)], axis=0)
    res_two = x + dot(att_half.T, r.out_w[...])

    def nothing():
        pass

    stats = share_stats(
        place,
        stack_rows([*first_stats, *centre(res_two)], width),
        r.stat0,
        r.stat_sems.at[0],
        nothing,
    )
    mean_one, inv_one = combine(stats[:, 0, :], stats[:, 1, :])
    mean_two, inv_two = combine(stats[:, 2, :], stats[:, 3, :])
    normed_one = (res_one - mean_one) * inv_one
    normed_two = (res_two - mean_two) * inv_two
    summed = r.g1[...] * normed_one + (r.g2[...] * normed_two + r.b2[...])
    summed_half = summed.astype(bf16)
    ffn_hidden = dot(summed_half, r.f1[...]) + r.fb[...]
    value, ffn_slope = gelu_and_slope(ffn_hidden)
    ffn_active = value.astype(bf16)
    res_three = summed + dot(ffn_active, r.f2[...])
    upstream = r.up[...].astype(f32)
    mean_here, squares_here = centre(res_three)
    stats = share_stats(
        place,
        stack_rows(
            [
                mean_here,
                squares_here,
                col_sum(upstream),
                col_sum(upstream * (res_three - mean_here)),
            ],
            width,
        ),
        r.stat1,
        r.stat_sems.at[1],
        nothing,
    )
    mean_three, inv_three = combine(stats[:, 0, :], stats[:, 1, :])
    normed_three = (res_three - mean_three) * inv_three
    bias_three = jnp.sum(stats[:, 2, :], axis=0, keepdims=True)
    gain_three = inv_three * jnp.sum(
        stats[:, 3, :] + (stats[:, 0, :] - mean_three) * stats[:, 2, :], axis=0, keepdims=True
    )
    g3 = r.g3[...]

    def norm_back(up, normed, inv, gain, bias_sum, gain_sum):
        return inv * (
            gain * up - gain * bias_sum / total_rows - normed * (gain * gain_sum / total_rows)
        )

    grad_three = norm_back(upstream, normed_three, inv_three, g3, bias_three, gain_three)
    grad_ffn = grad_three.astype(bf16)
    grad_hidden = (ffn_slope * dot(grad_ffn, r.f2[...], 1, 1)).astype(bf16)
    grad_summed = grad_three + dot(grad_hidden, r.f1[...], 1, 1)
    fb_part = col_sum(grad_hidden.astype(f32))

    def ffn_parts():
        r.result[...] = (g3 * normed_three + r.b3[...]).astype(bf16)
        r.stores["result"].start()
        f1_part = dot(summed_half.T, grad_hidden).astype(bf16)
        r.parts[3 * width : 4 * width, :] = f1_part[:, :width]
        r.parts[4 * width : 5 * width, :] = f1_part[:, width:]
        f2_part = dot(ffn_active.T, grad_ffn).astype(bf16)
        r.parts[5 * width : 5 * width + f2_part.shape[0], :] = f2_part

    stats = share_stats(
        place,
        stack_rows(
            [
                col_sum(grad_summed),
                col_sum(grad_summed * normed_one),
                col_sum(grad_summed * normed_two),
            ],
            width,
        ),
        r.stat2,
        r.stat_sems.at[2],
        ffn_parts,
    )
    sums = jnp.sum(stats, axis=0)
    bias_sum, gain_one, gain_two = sums[0:1], sums[1:2], sums[2:3]
    grad_second = norm_back(grad_summed, normed_two, inv_two, r.g2[...], bias_sum, gain_two)
    grad_global = grad_second.astype(bf16)
    grad_att = dot(r.out_w[...], grad_global, 1, 1).astype(bf16)
    for h in range(HEADS):
        r.do_send[h] = grad_att[HDIM * h : HDIM * (h + 1)]
    place.to_plane(lambda spot: r.do_send.at[spot], r.do.at[place.p], r.do_sems)
    r.do[place.p] = r.do_send[place.p]

    grad_first = norm_back(grad_summed, normed_one, inv_one, r.g1[...], bias_sum, gain_one)
    grad_local = grad_first.astype(bf16)
    grad_one = (r.hidden_slope[...] * dot(grad_local, r.w2[...], 1, 1)).astype(bf16)
    grad_mixed = dot(grad_one, r.w1[...], 1, 1)
    r.parts[2 * width : 3 * width, :] = dot(att_half, grad_global).astype(bf16)
    r.parts[width : 2 * width, :] = dot(r.active[...].T, grad_local).astype(bf16)
    r.parts[0:width, :] = dot(r.mixed[...].T, grad_one).astype(bf16)
    at = 5 * width + r.f2.shape[0]
    rows_left = [col_sum(grad_one.astype(f32)), fb_part[:, :width], fb_part[:, width:]]
    r.parts[at : at + 16, :] = jnp.concatenate(
        rows_left + [jnp.zeros((13, width), f32)], axis=0
    ).astype(bf16)
    r.parts[at + 16 :, :] = jnp.zeros((r.parts.shape[0] - at - 16, width), bf16)
    half = r.parts.shape[0] // 2
    place.copy(
        part_of(r.parts, 1 - place.core, half), r.pair_got, r.pair_sems, 1
    ).start()
    r.vectors[...] = jnp.concatenate(
        [gain_one, gain_two, bias_sum, gain_three, bias_three, jnp.zeros((3, width), f32)], axis=0
    )
    r.stores["vectors"].start()
    r.grad_mixed[...] = grad_mixed
    r.grad[...] = grad_first + grad_second + grad_mixed


def edges_back(r, place):
    rows, width = r.x.shape
    grad_mixed = r.grad_mixed[...]
    back = jnp.zeros((3 * rows, width), f32)
    for k in range(EDGES):
        back = back + dot(r.selects[k], (r.slopes[k] * grad_mixed).astype(bf16))
    r.edge_send[0] = back[2 * rows :].astype(bf16)
    r.edge_send[1] = back[:rows].astype(bf16)
    up, down = halo(
        r, place, r.edge_send.at[0], r.edge_send.at[1], r.edge_got.at[0], r.edge_got.at[1], 1
    )
    start_halo(place, up, down)
    r.grad[...] += back[rows : 2 * rows]
    return up, down


def spread(v):
    cols = v.shape[1]
    parts = [part.astype(f32) for part in three_parts(v)]
    row = lax.broadcasted_iota(jnp.int32, (16, cols), 0)
    out = jnp.where(row == 0, parts[0], 0.0)
    out = jnp.where(row == 1, parts[1], out)
    return jnp.where(row == 2, parts[2], out).astype(bf16)


def attend_back(r, place, depth):
    planes = place.planes
    cols = r.q.shape[2]
    width = HEADS * cols
    share = r.parts.shape[0] // HEADS
    slice_rows = share // planes
    place.wait(r.do.at[pl.ds(0, HEADS - 1)], r.do_sems)
    for b in range(HEADS):
        qs = slice(b * cols, (b + 1) * cols)
        grad = r.do[b].astype(f32)
        inner = jnp.sum(grad * r.attended[:, qs], axis=0, keepdims=True)
        r.grad_rows[:, qs] = r.do[b]
        r.grads[:, qs] = jnp.concatenate(
            list(three_parts(grad * score_scale))
            + [spread(inner * -score_scale), jnp.zeros((16, cols), bf16)],
            axis=0,
        )
    place.wait(r.pair_got, r.pair_sems)
    pair = part_of(r.parts, place.core, 4 * share)[...].astype(f32) + r.pair_got[...].astype(f32)
    r.pair_sum[...] = pair.astype(bf16)
    place.to_chips(
        lambda spot: part_of(r.pair_sum, spot, share), lambda k: r.chips_got.at[k], r.parts_sems
    )
    query_rows = jnp.concatenate([r.q[b] for b in range(HEADS)], axis=1)
    r.query_rows[...] = query_rows
    r.dq_total[...] = jnp.zeros_like(r.dq_total)

    def plane_of_keys(k):
        plane = place.plane(k)
        slot = lax.rem(k, 2)

        @pl.when(k < planes - 2)
        def weights_back():
            load_weights(r, k).wait()

        r.factors[...] = jnp.exp2(r.tops[k] - r.logs[0:1, :])

        def ahead(a, b):
            ks, qs = slice(a * cols, (a + 1) * cols), slice(b * cols, (b + 1) * cols)
            if b == 0:
                vt = r.kv[plane * HEADS + a, HDIM : 2 * HDIM]
                r.values[ks, :] = jnp.concatenate(
                    [vt, vt, vt, jnp.ones((HDIM, cols), bf16)], axis=0
                ).T
            return dot(r.values[ks, :], r.grads[:, qs])

        sums = [None, None]

        def behind(a, b, product):
            ks, qs = slice(a * cols, (a + 1) * cols), slice(b * cols, (b + 1) * cols)
            probs = r.kept[slot, ks, qs].astype(f32) * r.factors[a : a + 1, qs]
            grad_scores = (probs * product).astype(bf16)
            r.dq_total[:, qs] += dot(r.kv[plane * HEADS + a, 0:HDIM], grad_scores)
            dk = dot(r.query_rows[:, qs], grad_scores, 1, 1)
            dv = dot(r.grad_rows[:, qs], probs.astype(bf16), 1, 1)
            sums[:] = (dk, dv) if b == 0 else (sums[0] + dk, sums[1] + dv)
            if b == HEADS - 1:
                r.dkv_part[plane * HEADS + a] = jnp.concatenate(sums, axis=0).astype(bf16)

        pipelined(ahead, behind, depth)

    def plane_step(step, _):
        k = planes - 1 - step
        plane_of_keys(k)

        @pl.when(k >= 2)
        def next_weights():
            load_weights(r, k - 2).start()

        bit = 1
        while bit < planes:
            if 2 * bit < planes:

                @pl.when(jnp.logical_and(k > 0, lax.rem(k, 2 * bit) == 0))
                def add_part(bit=bit):
                    place.wait(r.dkv_got.at[0], r.dkv_sems.at[k + bit])
                    mine = part_of(r.dkv_part, place.plane(k), HEADS)
                    mine[...] = (
                        mine[...].astype(f32) + r.dkv_got[k + bit].astype(f32)
                    ).astype(bf16)

            @pl.when(lax.rem(k, 2 * bit) == bit)
            def send_part(bit=bit):
                place.copy(
                    part_of(r.dkv_part, place.plane(k), HEADS),
                    r.dkv_got.at[k],
                    r.dkv_sems.at[k],
                    bit * HEADS,
                ).start()

            bit *= 2

        @pl.when(step == 0)
        def sum_plane():
            place.wait(r.chips_got.at[pl.ds(1, HEADS // 2 - 1)], r.parts_sems)
            total = part_of(r.pair_sum, place.chip, share)[...].astype(f32) + total_of(
                r.chips_got, 1
            )
            r.plane_sum[...] = total.astype(bf16)
            place.to_line(
                lambda spot: part_of(r.plane_sum, spot, slice_rows),
                lambda k: r.line_got.at[k],
                r.line_sems.at[0],
            )

        @pl.when(step == 1)
        def sum_line():
            place.wait(r.line_got.at[pl.ds(1, planes - 1)], r.line_sems.at[0])
            total = part_of(r.plane_sum, place.z, slice_rows)[...].astype(f32) + total_of(
                r.line_got, 1
            )
            r.line_sum[place.z] = total.astype(bf16)
            place.to_line(
                lambda spot: r.line_sum.at[place.z],
                lambda k: r.line_sum.at[place.z],
                r.line_sems.at[1],
            )

        @pl.when(step == 2)
        def spread_line():
            place.wait(r.line_sum.at[pl.ds(1, planes - 1)], r.line_sems.at[1])
            r.sums[place.share] = r.line_sum[...].reshape(share, cols)
            place.to_chips(
                lambda spot: r.sums.at[place.share],
                lambda k: r.sums.at[place.share],
                r.whole_sems.at[0],
            )

        return 0

    lax.fori_loop(0, planes, plane_step, 0)
    place.wait(r.sums.at[pl.ds(0, HEADS // 2 - 1)], r.whole_sems.at[0])
    own_half = part_of(r.sums, place.core, HEADS // 2)
    place.copy(own_half, own_half, r.whole_sems.at[1], 1).start()
    place.wait(r.x_all.at[pl.ds(0, HEADS - 1)], r.x_sems)
    dkv = part_of(r.dkv_part, place.z, HEADS)[...].astype(f32)
    bit = 1
    while bit < planes:
        place.wait(r.dkv_got.at[0], r.dkv_sems.at[bit])
        dkv = dkv + r.dkv_got[bit].astype(f32)
        bit *= 2
    for b in range(HEADS):
        r.back_send[b, 0:HDIM] = r.dq_total[:, b * cols : (b + 1) * cols].astype(bf16)
        r.back_send[b, HDIM : 3 * HDIM] = dkv[b].astype(bf16)
    place.to_plane(
        lambda spot: r.back_send.at[spot], r.back.at[place.p], r.back_sems
    )
    r.back[place.p] = r.back_send[place.p]
    total = dot(r.back_send[0], r.x_all[0])
    for b in range(1, HEADS):
        total = total + dot(r.back_send[b], r.x_all[b])
    r.heads_part[...] = total.astype(bf16)
    place.to_line(lambda spot: r.heads_part, lambda k: r.heads_got.at[k], r.heads_sems)
    halo_copies = edges_back(r, place)
    place.wait(r.heads_got.at[pl.ds(1, planes - 1)], r.heads_sems)
    total = r.heads_part[...].astype(f32) + total_of(r.heads_got, 1)
    r.heads[place.share] = total.astype(bf16)
    place.to_chips(
        lambda spot: r.heads.at[place.share],
        lambda k: r.heads.at[place.share],
        r.last_sems.at[0],
    )
    place.wait(r.back.at[pl.ds(0, HEADS - 1)], r.back_sems)
    grad = r.grad[...]
    for s, w in enumerate((r.wq, r.wk, r.wv)):
        part = jnp.concatenate(
            [r.back[h, HDIM * s : HDIM * (s + 1)] for h in range(HEADS)], axis=0
        )
        grad = grad + dot(part.T, w[...], 1, 1)
    place.wait(r.heads.at[pl.ds(0, HEADS // 2 - 1)], r.last_sems.at[0])
    own_half = part_of(r.heads, place.core, HEADS // 2)
    place.copy(own_half, own_half, r.last_sems.at[1], 1).start()
    wait_halo(place, *halo_copies)
    r.grad[...] = grad + r.edge_got[0].astype(f32) + r.edge_got[1].astype(f32)
    r.stores["grad"].start()
    place.wait(r.sums.at[pl.ds(0, HEADS // 2)], r.whole_sems.at[1])
    r.stores["sums"].start()
    place.wait(r.heads.at[pl.ds(0, HEADS // 2)], r.last_sems.at[1])
    r.stores["heads"].start()


def layer_kernel(count, cores, names, args, outs, *refs):
    r = Refs(names, refs)
    place = Place(count, cores)
    r.loads = {
        name: pltpu.make_async_copy(
            getattr(r, "from_" + name), getattr(r, name), r.load_sems.at[i]
        )
        for i, name in enumerate(args)
    }
    r.stores = {
        name: pltpu.make_async_copy(getattr(r, name), getattr(r, "to_" + name), r.store_sems.at[i])
        for i, name in enumerate(outs)
    }
    for load in r.loads.values():
        load.start()
    halo_copies = project(r, place)
    attend(r, place, 6, halo_copies)
    r.need("edge", "w1", "b1", "w2")
    r.need("up", "out_w", "f1", "fb", "f2", "g1", "g2", "b2", "g3", "b3")
    norms(r, place, halo_copies)
    attend_back(r, place, 6)
    for store in r.stores.values():
        store.wait()


def finish_kernel(names, outs, *refs):
    r = Refs(names, refs)
    width = r.grad.shape[1]
    moves = [
        pltpu.make_async_copy(r.from_sums, r.sums, r.load_sems.at[0]),
        pltpu.make_async_copy(r.from_heads, r.heads, r.load_sems.at[1]),
        pltpu.make_async_copy(r.from_vectors, r.vectors, r.load_sems.at[2]),
        pltpu.make_async_copy(r.from_result, r.result, r.load_sems.at[3]),
        pltpu.make_async_copy(r.from_grad, r.grad, r.load_sems.at[4]),
    ]
    for move in moves:
        move.start()
    stores = []

    def put(name, value):
        if value is not None:
            getattr(r, name)[...] = value
        stores.append(
            pltpu.make_async_copy(
                getattr(r, name), getattr(r, "to_" + name), r.store_sems.at[outs.index(name)]
            )
        )
        stores[-1].start()

    moves[0].wait()
    for k, name in enumerate(("gw1", "gw2", "ow")):
        put(name, r.sums[k * width : (k + 1) * width].astype(f32))
    r.f1[:, 0:width] = r.sums[3 * width : 4 * width].astype(f32)
    r.f1[:, width:] = r.sums[4 * width : 5 * width].astype(f32)
    put("f1", None)
    last = 5 * width + r.f2.shape[0]
    put("f2", r.sums[5 * width : last].astype(f32))
    rows_left = r.sums[last : last + 16].astype(f32)
    put("gb1", rows_left[0:1])
    put("fb", jnp.concatenate([rows_left[1:2], rows_left[2:3]], axis=1))
    moves[3].wait()
    put("result", None)
    moves[4].wait()
    put("grad", None)
    moves[1].wait()
    for s, name in enumerate(("qw", "kw", "vw")):
        cols = slice(HDIM * s, HDIM * (s + 1))
        spots = [h % 2 * (HEADS // 2) + h // 2 for h in range(HEADS)]
        total = jnp.concatenate([r.heads[spot, cols] for spot in spots], axis=0)
        put(name, total.T.astype(f32))
    moves[2].wait()
    for k, name in enumerate(("gain1", "gain2", "bias2", "gain3", "bias3")):
        put(name, r.vectors[k : k + 1])
    for store in stores:
        store.wait()


def on_device(
    count,
    cores,
    node_feat,
    edge_feat,
    edge_step,
    degree,
    graph_len,
    gine_w1,
    gine_b1,
    gine_w2,
    query_w,
    key_w,
    value_w,
    out_w,
    ffn_w1,
    ffn_b1,
    ffn_w2,
    norm1_gain,
    norm2_gain,
    norm2_bias,
    norm3_gain,
    norm3_bias,
    out_grad,
):
    rows, width = node_feat.shape
    ffn = ffn_w1.shape[1]
    planes = count // HEADS
    plane_rows = HEADS * rows
    vmem = pl.BlockSpec(memory_space=pltpu.VMEM)
    dma = pltpu.SemaphoreType.DMA
    shape = jax.ShapeDtypeStruct
    share_unit = 16 * HEADS * planes
    needed = 3 * width + 2 * ffn + 16
    part_rows = -(-needed // share_unit) * share_unit
    share = part_rows // HEADS

    def row(v):
        return v.reshape(1, -1)

    args = dict(
        x=node_feat,
        wk=key_w,
        wv=value_w,
        wq=query_w,
        step=edge_step.T,
        degree=row(degree),
        edge=edge_feat,
        w1=gine_w1,
        b1=row(gine_b1),
        w2=gine_w2,
        up=out_grad,
        out_w=out_w,
        f1=ffn_w1,
        fb=row(ffn_b1),
        f2=ffn_w2,
        g1=row(norm1_gain),
        g2=row(norm2_gain),
        b2=row(norm2_bias),
        g3=row(norm3_gain),
        b3=row(norm3_bias),
    )
    outs = dict(
        result=shape((rows, width), bf16),
        grad=shape((rows, width), f32),
        vectors=shape((8, width), f32),
        heads=shape((HEADS, 3 * HDIM, width), bf16),
        sums=shape((HEADS, share, width), bf16),
    )
    scratch = dict(
        ext=pltpu.VMEM((3 * rows, width), bf16),
        kv_send=pltpu.VMEM((HEADS, 2 * HDIM, rows), bf16),
        q_send=pltpu.VMEM((HEADS, HDIM, rows), bf16),
        kv=pltpu.VMEM((count, 2 * HDIM, rows), bf16),
        q=pltpu.VMEM((HEADS, HDIM, rows), bf16),
        columns=pltpu.VMEM((rows, 128), f32),
        slopes=pltpu.VMEM((EDGES, rows, width), f32),
        selects=pltpu.VMEM((EDGES, 3 * rows, rows), bf16),
        mixed=pltpu.VMEM((rows, width), bf16),
        active=pltpu.VMEM((rows, width), bf16),
        hidden_slope=pltpu.VMEM((rows, width), f32),
        res_one=pltpu.VMEM((rows, width), f32),
        grad_mixed=pltpu.VMEM((rows, width), f32),
        keys=pltpu.VMEM((plane_rows, 128), bf16),
        value_rows=pltpu.VMEM((HDIM + 16, plane_rows), bf16),
        values=pltpu.VMEM((plane_rows, 128), bf16),
        queries=pltpu.VMEM((128, plane_rows), bf16),
        grads=pltpu.VMEM((128, plane_rows), bf16),
        query_rows=pltpu.VMEM((HDIM, plane_rows), bf16),
        grad_rows=pltpu.VMEM((HDIM, plane_rows), bf16),
        factors=pltpu.VMEM((8, plane_rows), f32),
        kept=pltpu.VMEM((2, plane_rows, plane_rows), bf16),
        tops=pltpu.VMEM((planes, 8, plane_rows), f32),
        total=pltpu.VMEM((HDIM + 16, plane_rows), f32),
        top=pltpu.VMEM((8, plane_rows), f32),
        logs=pltpu.VMEM((8, plane_rows), f32),
        attended=pltpu.VMEM((HDIM, plane_rows), f32),
        att_send=pltpu.VMEM((HEADS, HDIM, rows), bf16),
        att_got=pltpu.VMEM((HEADS, HDIM, rows), bf16),
        do_send=pltpu.VMEM((HEADS, HDIM, rows), bf16),
        do=pltpu.VMEM((HEADS, HDIM, rows), bf16),
        stat0=pltpu.VMEM((count, 8, width // 2), f32),
        stat1=pltpu.VMEM((count, 8, width // 2), f32),
        stat2=pltpu.VMEM((count, 8, width // 2), f32),
        edge_send=pltpu.VMEM((2, rows, width), bf16),
        edge_got=pltpu.VMEM((2, rows, width), bf16),
        x_all=pltpu.VMEM((HEADS, rows, width), bf16),
        parts=pltpu.VMEM((part_rows, width), bf16),
        pair_got=pltpu.VMEM((part_rows // 2, width), bf16),
        pair_sum=pltpu.VMEM((part_rows // 2, width), bf16),
        chips_got=pltpu.VMEM((HEADS // 2, share, width), bf16),
        plane_sum=pltpu.VMEM((share, width), bf16),
        line_got=pltpu.VMEM((planes, share // planes, width), bf16),
        line_sum=pltpu.VMEM((planes, share // planes, width), bf16),
        dq_total=pltpu.VMEM((HDIM, plane_rows), f32),
        dkv_part=pltpu.VMEM((count, 2 * HDIM, rows), bf16),
        dkv_got=pltpu.VMEM((planes, HEADS, 2 * HDIM, rows), bf16),
        back_send=pltpu.VMEM((HEADS, 3 * HDIM, rows), bf16),
        back=pltpu.VMEM((HEADS, 3 * HDIM, rows), bf16),
        heads_part=pltpu.VMEM((3 * HDIM, width), bf16),
        heads_got=pltpu.VMEM((planes, 3 * HDIM, width), bf16),
        kv_sems=dma((planes, 2, 2)),
        halo_sems=dma((2, 4)),
        stat_sems=dma((3, 2)),
        line_sems=dma((2, 2)),
        dkv_sems=dma((planes, 2)),
        far_sems=dma((2, 2)),
        whole_sems=dma((2, 2)),
        last_sems=dma((2, 2)),
        **{
            name + "_sems": dma((2,))
            for name in ("q", "att", "do", "x", "pair", "parts", "back", "heads")
        },
    )
    scratch = dict(
        **{name: pltpu.VMEM(v.shape, v.dtype) for name, v in (args | outs).items()},
        **scratch,
        load_sems=dma((len(args),)),
        store_sems=dma((len(outs),)),
    )
    names = (
        "graph_len",
        *("from_" + name for name in args),
        *("to_" + name for name in outs),
        "far",
        *scratch,
    )
    anywhere = pl.BlockSpec(memory_space=pl.ANY)
    far = shape((planes - 2, plane_rows, plane_rows), bf16)
    result, grad, vectors, heads, sums, _ = pl.pallas_call(
        functools.partial(layer_kernel, count, cores, names, tuple(args), tuple(outs)),
        out_shape=(*outs.values(), far),
        in_specs=[pl.BlockSpec(memory_space=pltpu.SMEM)] + [anywhere] * len(args),
        out_specs=(anywhere,) * (len(outs) + 1),
        scratch_shapes=list(scratch.values()),
        compiler_params=pltpu.CompilerParams(
            vmem_limit_bytes=62 << 20, collective_id=1, has_side_effects=True
        ),
    )(graph_len, *args.values())

    square = shape((width, width), f32)
    line = shape((1, width), f32)
    ends = dict(
        result=shape((rows, width), bf16),
        grad=shape((rows, width), f32),
        gw1=square,
        gb1=line,
        gw2=square,
        qw=square,
        kw=square,
        vw=square,
        ow=square,
        f1=shape((width, ffn), f32),
        fb=shape((1, ffn), f32),
        f2=shape((ffn, width), f32),
        gain1=line,
        gain2=line,
        bias2=line,
        gain3=line,
        bias3=line,
    )
    parts = dict(
        sums=sums.reshape(part_rows, width),
        heads=heads,
        vectors=vectors,
        result=result,
        grad=grad,
    )
    scratch = dict(
        **{name: pltpu.VMEM(v.shape, v.dtype) for name, v in (parts | ends).items()},
        load_sems=dma((len(parts),)),
        store_sems=dma((len(ends),)),
    )
    names = (
        *("from_" + name for name in parts),
        *("to_" + name for name in ends),
        *scratch,
    )
    done = pl.pallas_call(
        functools.partial(finish_kernel, names, tuple(ends)),
        out_shape=tuple(ends.values()),
        in_specs=[anywhere] * len(parts),
        out_specs=(anywhere,) * len(ends),
        scratch_shapes=list(scratch.values()),
        compiler_params=pltpu.CompilerParams(vmem_limit_bytes=60 << 20),
    )(*parts.values())
    return tuple(v.reshape(-1) if v.shape[0] == 1 else v for v in done)


def solution(mesh):
    count = mesh.shape["blk"] * mesh.shape["rep"]
    rows = P(AXES, None)
    whole = P()
    return jax.shard_map(
        functools.partial(on_device, count, mesh.shape["rep"]),
        mesh=mesh,
        in_specs=(rows, P(AXES, None, None), rows, P(AXES)) + (whole,) * 16 + (rows,),
        out_specs=(rows, rows) + (whole,) * 15,
        check_vma=False,
    )
```

```python
import functools
import jax
import jax.numpy as jnp
from jax import lax
from jax.experimental import pallas as pl
from jax.experimental.pallas import tpu as pltpu
from jax.sharding import PartitionSpec as P

HEADS = 8
HDIM = 32
EDGES = 8
GRAPHS = 9
AXES = ("blk", "rep")
MESH = pl.DeviceIdType.MESH
bf16 = jnp.bfloat16
f32 = jnp.float32

norm_eps = 1e-05
far_score = -1e30
log2_e = 1.4426950408889634
score_scale = HDIM ** (-0.5)
gelu_c = 0.7978845608028654
gelu_a = 0.044715


def dot(left, right, left_dim=1, right_dim=0):
    return lax.dot_general(
        left, right, (((left_dim,), (right_dim,)), ((), ())), preferred_element_type=f32
    )


def gelu(v):
    return 0.5 * v * (1.0 + jnp.tanh(gelu_c * (v + gelu_a * (v * v * v))))


def gelu_slope(v):
    squared = v * v
    bend = jnp.tanh(gelu_c * v * (1.0 + gelu_a * squared))
    return 0.5 * (1.0 + bend) + 0.5 * v * (1.0 - bend * bend) * (
        gelu_c * (1.0 + 3.0 * gelu_a * squared)
    )


def three_parts(v):
    first = v.astype(bf16)
    rest = v - first.astype(f32)
    second = rest.astype(bf16)
    third = (rest - second.astype(f32)).astype(bf16)
    return first, second, third


class Place:
    def __init__(self, count, cores):
        self.count = count
        self.cores = cores
        self.planes = count // HEADS
        self.blk = lax.axis_index("blk")
        self.rep = lax.axis_index("rep")
        self.me = self.blk * cores + self.rep
        self.z = lax.div(self.me, HEADS)
        self.p = self.me - self.z * HEADS
        self.chip = lax.div(self.p, 2)
        self.core = self.p - 2 * self.chip
        self.share = self.core * (HEADS // 2) + self.chip
        self.steps = []
        bit, rest = 1, self.me
        while bit < count:
            half = lax.div(rest, 2)
            self.steps.append(bit * (1 - 2 * (rest - 2 * half)))
            bit, rest = 2 * bit, half

    def move(self, k, first=0, last=None):
        total = 0
        for j, step in enumerate(self.steps[first:last]):
            bit = 1 << (first + j)
            if isinstance(k, int):
                if k & bit:
                    total = total + step
            else:
                total = total + lax.rem(lax.div(k, bit), 2) * step
        return total

    def device(self, k):
        low = self.cores.bit_length() - 1
        return {
            "blk": self.blk + lax.div(self.move(k, low), self.cores),
            "rep": self.rep + self.move(k, 0, low),
        }

    def peer(self, k):
        return self.me + self.move(k)

    def spot(self, k):
        return self.p + self.move(k, 0, 3)

    def plane(self, k):
        return self.z + lax.div(self.move(k * HEADS, 3), HEADS)

    def loop(self, first, last, body):
        if last - first <= 32:
            for k in range(first, last):
                body(k)
        else:

            def step(k, _):
                body(k)
                return 0

            lax.fori_loop(first, last, step, 0)

    def greet(self):
        def hello(k):
            pl.semaphore_signal(
                pltpu.get_barrier_semaphore(),
                inc=1,
                device_id=self.device(self.count - k),
                device_id_type=MESH,
            )

        self.loop(1, self.count, hello)

    def greeted(self):
        pl.semaphore_wait(pltpu.get_barrier_semaphore(), self.count - 1)

    def copy(self, src, dst, sems, k):
        return self.copy_to(src, dst, sems.at[0], sems.at[1], self.device(k))

    def copy_to(self, src, dst, send_sem, recv_sem, device):
        return pltpu.make_async_remote_copy(
            src_ref=src,
            dst_ref=dst,
            send_sem=send_sem,
            recv_sem=recv_sem,
            device_id=device,
            device_id_type=MESH,
        )

    def to_plane(self, src_of, dst, sems):
        for k in reversed(range(1, HEADS)):
            self.copy(src_of(self.spot(k)), dst, sems, k).start()

    def to_line(self, src_of, dst_of, sems):
        for k in range(1, self.planes):
            self.copy(src_of(self.plane(k)), dst_of(k), sems, k * HEADS).start()

    def to_chips(self, src_of, dst_of, sems):
        for k in range(1, HEADS // 2):
            there = self.chip + lax.div(self.move(2 * k, 1, 3), 2)
            self.copy(src_of(there), dst_of(k), sems, 2 * k).start()

    def wait(self, like, sems):
        self.copy(like, like, sems, 1).wait()


def part_of(ref, spot, size):
    return ref.at[pl.ds(pl.multiple_of(spot * size, size), size)]


def total_of(ref, start=0):
    total = ref[start].astype(f32)
    for k in range(start + 1, ref.shape[0]):
        total = total + ref[k].astype(f32)
    return total


def col_sum(v):
    return jnp.sum(v, axis=0, keepdims=True)


def stack_rows(rows, width):
    four = jnp.concatenate(rows + [jnp.zeros((1, width), f32)] * (4 - len(rows)), axis=0)
    return jnp.concatenate([four[:, : width // 2], four[:, width // 2 :]], axis=0)


def graph_bounds(len_ref, positions):
    last = 0
    graph = jnp.zeros(positions.shape, jnp.int32)
    start = jnp.zeros(positions.shape, jnp.int32)
    ends = []
    for g in range(GRAPHS):
        last = last + len_ref[g]
        ends.append(last)
        passed = positions >= last
        graph = graph + passed.astype(jnp.int32)
        start = jnp.where(passed, last, start)
    stop = jnp.full(positions.shape, ends[-1], jnp.int32)
    for end in reversed(ends):
        stop = jnp.where(positions < end, end, stop)
    return graph, start, stop


def own_graph(len_ref, first, width):
    positions = first + lax.broadcasted_iota(jnp.int32, (1, width), 1)
    graph, _, _ = graph_bounds(len_ref, positions)
    rows = lax.broadcasted_iota(jnp.int32, (16, width), 0)
    return rows == graph


def as_columns(rows, width):
    return jnp.concatenate([rows, jnp.zeros((128 - rows.shape[0], width), f32)], axis=0).T


def gelu_and_slope(v):
    squared = v * v
    bend = jnp.tanh(gelu_c * v * (1.0 + gelu_a * squared))
    half = 0.5 * (1.0 + bend)
    slope = half + 0.5 * v * (1.0 - bend * bend) * (gelu_c * (1.0 + 3.0 * gelu_a * squared))
    return v * half, slope


class Refs:
    def __init__(self, names, refs):
        for name, ref in zip(names, refs, strict=True):
            setattr(self, name, ref)

    def need(self, *names):
        for name in names:
            self.loads[name].wait()


def share_stats(place, stats, buffer, sems, between):
    buffer[place.me] = stats

    def begin(k):
        place.copy(buffer.at[place.me], buffer.at[place.me], sems, place.count - k).start()

    place.loop(1, place.count, begin)
    between()
    place.wait(buffer.at[pl.ds(0, place.count - 1)], sems)
    return jnp.concatenate([buffer[:, 0:4, :], buffer[:, 4:8, :]], axis=2)


def project(r, place):
    rows, width = r.x.shape
    count = place.count
    r.edge_got[...] = jnp.zeros_like(r.edge_got)
    r.need("x")
    x = r.x[...]
    r.ext[0:rows, :] = jnp.zeros_like(x)
    r.ext[rows : 2 * rows, :] = x
    r.ext[2 * rows :, :] = jnp.zeros_like(x)
    place.greet()
    xt = x.T
    r.need("wk", "wv", "wq")
    kt = dot(r.wk[...].T, xt).astype(bf16)
    vt = dot(r.wv[...].T, xt).astype(bf16)
    for h in range(HEADS):
        cols = slice(HDIM * h, HDIM * (h + 1))
        r.kv_send[h, 0:HDIM] = kt[cols]
        r.kv_send[h, HDIM : 2 * HDIM] = vt[cols]
    qt = dot(r.wq[...].T, xt).astype(bf16)
    for h in range(HEADS):
        r.q_send[h] = qt[HDIM * h : HDIM * (h + 1)]
    r.need("step", "degree")
    edge_sources(r, place)
    place.greeted()

    place.to_plane(lambda spot: r.kv_send.at[spot], r.kv.at[place.me], r.kv_sems.at[0, 0])
    place.to_plane(lambda spot: r.q_send.at[spot], r.q.at[place.p], r.q_sems)
    half = lax.div(place.p, HEADS // 2)
    for k in reversed(range(HEADS)):
        place.copy_to(
            r.kv_send.at[place.spot(k)],
            r.kv.at[place.me],
            r.kv_sems.at[0, 1, 0],
            r.kv_sems.at[place.planes // 2, half, 1],
            place.device(count // 2 + k),
        ).start()
    up, down = halo(r, place, r.x, r.x, r.ext.at[pl.ds(0, rows)], r.ext.at[pl.ds(2 * rows, rows)])
    r.kv[place.me] = r.kv_send[place.p]
    r.q[place.p] = r.q_send[place.p]
    return up, down


def pass_on(r, place, dz, bit, half):
    rows = part_of(r.kv, 2 * place.plane(dz) + half, HEADS // 2)
    place.copy(rows, rows, r.kv_sems.at[dz + bit, half], bit * HEADS).start()


def pass_down(r, place, dz, half):
    bit = 1
    while bit < place.planes // 2:
        pl.when(lax.rem(dz, 2 * bit) == 0)(functools.partial(pass_on, r, place, dz, bit, half))
        bit *= 2


def kv_arrived(r, place, dz, half):
    like = r.kv.at[pl.ds(0, HEADS // 2)]
    place.copy(like, like, r.kv_sems.at[dz, half], 1).wait_recv()


def kv_sent(r, place):
    like = r.kv.at[pl.ds(0, HEADS // 2)]
    for dz in range(1, place.planes):
        if dz != place.planes // 2:
            for half in range(2):
                place.copy(like, like, r.kv_sems.at[dz, half], 1).wait_send()
    like = r.kv.at[pl.ds(0, HEADS)]
    place.copy(like, like, r.kv_sems.at[0, 1], 1).wait_send()


def halo(r, place, up_src, down_src, up_dst, down_dst, which=0):
    def neighbour(index):
        blk = lax.div(index, place.cores)
        return {"blk": blk, "rep": index - blk * place.cores}

    sems = r.halo_sems.at[which]
    last = place.count - 1
    after = neighbour(jnp.minimum(place.me + 1, last))
    before = neighbour(jnp.maximum(place.me - 1, 0))
    up = place.copy_to(up_src, up_dst, sems.at[0], sems.at[1], after)
    down = place.copy_to(down_src, down_dst, sems.at[2], sems.at[3], before)
    return up, down


def start_halo(place, up, down):
    @pl.when(place.me < place.count - 1)
    def send_up():
        up.start()

    @pl.when(place.me > 0)
    def send_down():
        down.start()


def wait_halo(place, up, down):
    @pl.when(place.me < place.count - 1)
    def with_after():
        up.wait_send()
        down.wait_recv()

    @pl.when(place.me > 0)
    def with_before():
        down.wait_send()
        up.wait_recv()


def edge_sources(r, place):
    rows = r.x.shape[0]
    positions = place.me * rows + lax.broadcasted_iota(jnp.int32, (1, rows), 1)
    _, start, stop = graph_bounds(r.graph_len, positions)
    source = jnp.minimum(jnp.maximum(positions + r.step[...], start), stop - 1)
    source = source - place.me * rows + rows
    r.columns[...] = as_columns(
        jnp.concatenate([source.astype(f32), r.degree[...].astype(f32)], axis=0), rows
    )
    cells = lax.broadcasted_iota(jnp.int32, (3 * rows, rows), 0)
    for k in range(EDGES):
        r.selects[k] = (source[k : k + 1, :] == cells).astype(f32).astype(bf16)


def gine_forward(r, place):
    rows, width = r.x.shape
    columns = r.columns[...]
    cells = lax.broadcasted_iota(jnp.int32, (rows, 3 * rows), 1).astype(f32)
    x = r.x[...].astype(f32)
    message = jnp.zeros_like(x)
    around = r.ext[...]
    for k in range(EDGES):
        select = (columns[:, k : k + 1] == cells).astype(f32).astype(bf16)
        v = dot(select, around) + r.edge[:, k, :].astype(f32)
        present = columns[:, EDGES : EDGES + 1] > k
        value, slope = gelu_and_slope(v)
        message = message + jnp.where(present, value, 0.0)
        r.slopes[k] = jnp.where(present, slope, 0.0)
    mixed = (x + message).astype(bf16)
    r.mixed[...] = mixed
    hidden = dot(mixed, r.w1[...]) + r.b1[...]
    value, slope = gelu_and_slope(hidden)
    active = value.astype(bf16)
    r.active[...] = active
    r.hidden_slope[...] = slope
    r.res_one[...] = x + dot(active, r.w2[...])


def build_keys(r, plane, a):
    cols = r.q.shape[2]
    block = plane * HEADS + a
    kt = r.kv[block, 0:HDIM]
    same = own_graph(r.graph_len, block * cols, cols).astype(f32).astype(bf16)
    ones = jnp.ones((16, cols), bf16)
    r.keys[a * cols : (a + 1) * cols, :] = jnp.concatenate([kt, kt, kt, same, ones], axis=0).T
    r.value_rows[0:HDIM, a * cols : (a + 1) * cols] = r.kv[block, HDIM : 2 * HDIM]


def build_queries(r, place, last_rows):
    cols = r.q.shape[2]
    for b in range(HEADS):
        parts = three_parts(r.q[b].astype(f32) * (score_scale * log2_e))
        same = own_graph(r.graph_len, (place.z * HEADS + b) * cols, cols)
        known = lax.broadcasted_iota(jnp.int32, (16, cols), 0) < GRAPHS
        mask = jnp.where(jnp.logical_or(same, jnp.logical_not(known)), 0.0, far_score).astype(bf16)
        r.queries[:, b * cols : (b + 1) * cols] = jnp.concatenate(
            list(parts) + [mask, last_rows(b)], axis=0
        )


def store_weights(r, dz):
    slot = lax.rem(dz, 2)
    return pltpu.make_async_copy(r.kept.at[slot], r.far.at[dz], r.far_sems.at[0, slot])


def load_weights(r, dz):
    slot = lax.rem(dz, 2)
    return pltpu.make_async_copy(r.far.at[dz], r.kept.at[slot], r.far_sems.at[1, slot])


def pipelined(ahead, behind, depth, between=None, at=None):
    pairs = [(a, b) for a in range(HEADS) for b in range(HEADS)]
    waiting = [ahead(*pair) for pair in pairs[:depth]]
    for i, pair in enumerate(pairs):
        if i + depth < len(pairs):
            waiting.append(ahead(*pairs[i + depth]))
        behind(*pair, waiting.pop(0))
        if i == at:
            between()


def attend(r, place, depth, halo_copies):
    cols = r.q.shape[2]
    width = HEADS * cols
    place.wait(r.kv.at[pl.ds(0, HEADS - 1)], r.kv_sems.at[0, 0])
    for half in range(2):
        bit = 1
        while bit < place.planes // 2:
            pass_on(r, place, 0, bit, half)
            bit *= 2
    start_halo(place, *halo_copies)
    place.to_plane(lambda spot: r.x, r.x_all.at[place.p], r.x_sems)
    r.x_all[place.p] = r.x[...]
    place.wait(r.q.at[pl.ds(0, HEADS - 1)], r.q_sems)
    build_queries(r, place, lambda b: jnp.zeros((16, cols), bf16))
    r.total[...] = jnp.zeros_like(r.total)
    r.value_rows[HDIM:, :] = jnp.ones((16, width), bf16)
    r.top[...] = jnp.full(r.top.shape, 2.0 * far_score, f32)
    farthest = place.planes // 2

    def plane_step(dz, _):
        plane = place.plane(dz)

        @pl.when(jnp.logical_and(dz > 0, dz != farthest))
        def arrived():
            for half in range(2):
                kv_arrived(r, place, dz, half)
                pass_down(r, place, dz, half)

        slot = lax.rem(dz, 2)

        @pl.when(dz >= 2)
        def slot_free():
            store_weights(r, dz - 2).wait()

        def ahead(a, b):
            ks, qs = slice(a * cols, (a + 1) * cols), slice(b * cols, (b + 1) * cols)
            if b == 0:
                build_keys(r, plane, a)
            return dot(r.keys[ks, :], r.queries[:, qs])

        def behind(a, b, scores):
            ks, qs = slice(a * cols, (a + 1) * cols), slice(b * cols, (b + 1) * cols)
            before = r.top[0:1, qs]
            now = jnp.maximum(before, jnp.max(scores, axis=0, keepdims=True))
            weights = jnp.exp2(scores - now).astype(bf16)
            r.kept[slot, ks, qs] = weights
            r.total[:, qs] = r.total[:, qs] * jnp.exp2(before - now) + dot(
                r.value_rows[:, ks], weights
            )
            r.top[0:1, qs] = now
            r.tops[dz, a : a + 1, qs] = now

        pipelined(ahead, behind, depth)

        @pl.when(dz < place.planes - 2)
        def away():
            store_weights(r, dz).start()

        @pl.when(dz == 0)
        def after_own():
            for half in range(2):
                kv_arrived(r, place, farthest, half)
                pass_down(r, place, farthest, half)

        return 0

    lax.fori_loop(0, place.planes, plane_step, 0)
    kv_sent(r, place)
    sums = r.total[HDIM : HDIM + 1, :]
    r.logs[0:1, :] = r.top[0:1, :] + jnp.log2(sums)
    attended = r.total[0:HDIM, :] / sums
    r.attended[...] = attended
    for b in range(HEADS):
        r.att_send[b] = attended[:, b * cols : (b + 1) * cols].astype(bf16)


def norms(r, place, halo_copies):
    rows, width = r.x.shape
    count = place.count
    total_rows = rows * count
    place.to_plane(lambda spot: r.att_send.at[spot], r.att_got.at[place.p], r.att_sems)
    r.att_got[place.p] = r.att_send[place.p]
    wait_halo(place, *halo_copies)
    gine_forward(r, place)
    x = r.x[...].astype(f32)
    res_one = r.res_one[...]

    def centre(v):
        mean = col_sum(v) / rows
        off = v - mean
        return mean, col_sum(off * off)

    def combine(means, squares):
        mean = jnp.sum(means, axis=0, keepdims=True) / count
        off = means - mean
        var = (
            jnp.sum(squares, axis=0, keepdims=True)
            + rows * jnp.sum(off * off, axis=0, keepdims=True)
        ) / total_rows
        return mean, lax.rsqrt(var + norm_eps)

    first_stats = centre(res_one)
    place.wait(r.att_got.at[pl.ds(0, HEADS - 1)], r.att_sems)
    att_half = jnp.concatenate([r.att_got[h] for h in range(HEADS)], axis=0)
    res_two = x + dot(att_half.T, r.out_w[...])

    def nothing():
        pass

    stats = share_stats(
        place,
        stack_rows([*first_stats, *centre(res_two)], width),
        r.stat0,
        r.stat_sems.at[0],
        nothing,
    )
    mean_one, inv_one = combine(stats[:, 0, :], stats[:, 1, :])
    mean_two, inv_two = combine(stats[:, 2, :], stats[:, 3, :])
    normed_one = (res_one - mean_one) * inv_one
    normed_two = (res_two - mean_two) * inv_two
    summed = r.g1[...] * normed_one + (r.g2[...] * normed_two + r.b2[...])
    summed_half = summed.astype(bf16)
    ffn_hidden = dot(summed_half, r.f1[...]) + r.fb[...]
    value, ffn_slope = gelu_and_slope(ffn_hidden)
    ffn_active = value.astype(bf16)
    res_three = summed + dot(ffn_active, r.f2[...])
    upstream = r.up[...].astype(f32)
    mean_here, squares_here = centre(res_three)
    stats = share_stats(
        place,
        stack_rows(
            [
                mean_here,
                squares_here,
                col_sum(upstream),
                col_sum(upstream * (res_three - mean_here)),
            ],
            width,
        ),
        r.stat1,
        r.stat_sems.at[1],
        nothing,
    )
    mean_three, inv_three = combine(stats[:, 0, :], stats[:, 1, :])
    normed_three = (res_three - mean_three) * inv_three
    bias_three = jnp.sum(stats[:, 2, :], axis=0, keepdims=True)
    gain_three = inv_three * jnp.sum(
        stats[:, 3, :] + (stats[:, 0, :] - mean_three) * stats[:, 2, :], axis=0, keepdims=True
    )
    g3 = r.g3[...]

    def norm_back(up, normed, inv, gain, bias_sum, gain_sum):
        return inv * (
            gain * up - gain * bias_sum / total_rows - normed * (gain * gain_sum / total_rows)
        )

    grad_three = norm_back(upstream, normed_three, inv_three, g3, bias_three, gain_three)
    grad_ffn = grad_three.astype(bf16)
    grad_hidden = (ffn_slope * dot(grad_ffn, r.f2[...], 1, 1)).astype(bf16)
    grad_summed = grad_three + dot(grad_hidden, r.f1[...], 1, 1)
    fb_part = col_sum(grad_hidden.astype(f32))

    def ffn_parts():
        r.result[...] = (g3 * normed_three + r.b3[...]).astype(bf16)
        r.stores["result"].start()
        f1_part = dot(summed_half.T, grad_hidden).astype(bf16)
        r.parts[3 * width : 4 * width, :] = f1_part[:, :width]
        r.parts[4 * width : 5 * width, :] = f1_part[:, width:]
        f2_part = dot(ffn_active.T, grad_ffn).astype(bf16)
        r.parts[5 * width : 5 * width + f2_part.shape[0], :] = f2_part

    stats = share_stats(
        place,
        stack_rows(
            [
                col_sum(grad_summed),
                col_sum(grad_summed * normed_one),
                col_sum(grad_summed * normed_two),
            ],
            width,
        ),
        r.stat2,
        r.stat_sems.at[2],
        ffn_parts,
    )
    sums = jnp.sum(stats, axis=0)
    bias_sum, gain_one, gain_two = sums[0:1], sums[1:2], sums[2:3]
    grad_second = norm_back(grad_summed, normed_two, inv_two, r.g2[...], bias_sum, gain_two)
    grad_global = grad_second.astype(bf16)
    grad_att = dot(r.out_w[...], grad_global, 1, 1).astype(bf16)
    for h in range(HEADS):
        r.do_send[h] = grad_att[HDIM * h : HDIM * (h + 1)]
    place.to_plane(lambda spot: r.do_send.at[spot], r.do.at[place.p], r.do_sems)
    r.do[place.p] = r.do_send[place.p]

    grad_first = norm_back(grad_summed, normed_one, inv_one, r.g1[...], bias_sum, gain_one)
    grad_local = grad_first.astype(bf16)
    grad_one = (r.hidden_slope[...] * dot(grad_local, r.w2[...], 1, 1)).astype(bf16)
    grad_mixed = dot(grad_one, r.w1[...], 1, 1)
    r.parts[2 * width : 3 * width, :] = dot(att_half, grad_global).astype(bf16)
    r.parts[width : 2 * width, :] = dot(r.active[...].T, grad_local).astype(bf16)
    r.parts[0:width, :] = dot(r.mixed[...].T, grad_one).astype(bf16)
    at = 5 * width + r.f2.shape[0]
    rows_left = [col_sum(grad_one.astype(f32)), fb_part[:, :width], fb_part[:, width:]]
    r.parts[at : at + 16, :] = jnp.concatenate(
        rows_left + [jnp.zeros((13, width), f32)], axis=0
    ).astype(bf16)
    r.parts[at + 16 :, :] = jnp.zeros((r.parts.shape[0] - at - 16, width), bf16)
    half = r.parts.shape[0] // 2
    place.copy(
        part_of(r.parts, 1 - place.core, half), r.pair_got, r.pair_sems, 1
    ).start()
    r.vectors[...] = jnp.concatenate(
        [gain_one, gain_two, bias_sum, gain_three, bias_three, jnp.zeros((3, width), f32)], axis=0
    )
    r.stores["vectors"].start()
    r.grad_mixed[...] = grad_mixed
    r.grad[...] = grad_first + grad_second + grad_mixed


def edges_back(r, place):
    rows, width = r.x.shape
    grad_mixed = r.grad_mixed[...]
    back = jnp.zeros((3 * rows, width), f32)
    for k in range(EDGES):
        back = back + dot(r.selects[k], (r.slopes[k] * grad_mixed).astype(bf16))
    r.edge_send[0] = back[2 * rows :].astype(bf16)
    r.edge_send[1] = back[:rows].astype(bf16)
    up, down = halo(
        r, place, r.edge_send.at[0], r.edge_send.at[1], r.edge_got.at[0], r.edge_got.at[1], 1
    )
    start_halo(place, up, down)
    r.grad[...] += back[rows : 2 * rows]
    return up, down


def spread(v):
    cols = v.shape[1]
    parts = [part.astype(f32) for part in three_parts(v)]
    row = lax.broadcasted_iota(jnp.int32, (16, cols), 0)
    out = jnp.where(row == 0, parts[0], 0.0)
    out = jnp.where(row == 1, parts[1], out)
    return jnp.where(row == 2, parts[2], out).astype(bf16)


def attend_back(r, place, depth):
    planes = place.planes
    cols = r.q.shape[2]
    width = HEADS * cols
    share = r.parts.shape[0] // HEADS
    slice_rows = share // planes
    place.wait(r.do.at[pl.ds(0, HEADS - 1)], r.do_sems)
    for b in range(HEADS):
        qs = slice(b * cols, (b + 1) * cols)
        grad = r.do[b].astype(f32)
        inner = jnp.sum(grad * r.attended[:, qs], axis=0, keepdims=True)
        r.grad_rows[:, qs] = r.do[b]
        r.grads[:, qs] = jnp.concatenate(
            list(three_parts(grad * score_scale))
            + [spread(inner * -score_scale), jnp.zeros((16, cols), bf16)],
            axis=0,
        )
    place.wait(r.pair_got, r.pair_sems)
    pair = part_of(r.parts, place.core, 4 * share)[...].astype(f32) + r.pair_got[...].astype(f32)
    r.pair_sum[...] = pair.astype(bf16)
    place.to_chips(
        lambda spot: part_of(r.pair_sum, spot, share), lambda k: r.chips_got.at[k], r.parts_sems
    )
    query_rows = jnp.concatenate([r.q[b] for b in range(HEADS)], axis=1)
    r.query_rows[...] = query_rows
    r.dq_total[...] = jnp.zeros_like(r.dq_total)

    def sum_parts(step):
        @pl.when(step == 0)
        def sum_plane():
            place.wait(r.chips_got.at[pl.ds(1, HEADS // 2 - 1)], r.parts_sems)
            total = part_of(r.pair_sum, place.chip, share)[...].astype(f32) + total_of(
                r.chips_got, 1
            )
            r.plane_sum[...] = total.astype(bf16)
            place.to_line(
                lambda spot: part_of(r.plane_sum, spot, slice_rows),
                lambda k: r.line_got.at[k],
                r.line_sems.at[0],
            )

        @pl.when(step == 1)
        def sum_line():
            place.wait(r.line_got.at[pl.ds(1, planes - 1)], r.line_sems.at[0])
            total = part_of(r.plane_sum, place.z, slice_rows)[...].astype(f32) + total_of(
                r.line_got, 1
            )
            r.line_sum[place.z] = total.astype(bf16)
            place.to_line(
                lambda spot: r.line_sum.at[place.z],
                lambda k: r.line_sum.at[place.z],
                r.line_sems.at[1],
            )

        @pl.when(step == 2)
        def spread_line():
            place.wait(r.line_sum.at[pl.ds(1, planes - 1)], r.line_sems.at[1])
            r.sums[place.share] = r.line_sum[...].reshape(share, cols)
            place.to_chips(
                lambda spot: r.sums.at[place.share],
                lambda k: r.sums.at[place.share],
                r.whole_sems.at[0],
            )

        @pl.when(step == 3)
        def spread_chip():
            place.wait(r.sums.at[pl.ds(0, HEADS // 2 - 1)], r.whole_sems.at[0])
            own_half = part_of(r.sums, place.core, HEADS // 2)
            place.copy(own_half, own_half, r.whole_sems.at[1], 1).start()

    def plane_of_keys(k):
        plane = place.plane(k)
        slot = lax.rem(k, 2)

        @pl.when(k < planes - 2)
        def weights_back():
            load_weights(r, k).wait()

        r.factors[...] = jnp.exp2(r.tops[k] - r.logs[0:1, :])

        def ahead(a, b):
            ks, qs = slice(a * cols, (a + 1) * cols), slice(b * cols, (b + 1) * cols)
            if b == 0:
                vt = r.kv[plane * HEADS + a, HDIM : 2 * HDIM]
                r.values[ks, :] = jnp.concatenate(
                    [vt, vt, vt, jnp.ones((HDIM, cols), bf16)], axis=0
                ).T
            return dot(r.values[ks, :], r.grads[:, qs])

        sums = [None, None]

        def behind(a, b, product):
            ks, qs = slice(a * cols, (a + 1) * cols), slice(b * cols, (b + 1) * cols)
            probs = r.kept[slot, ks, qs].astype(f32) * r.factors[a : a + 1, qs]
            grad_scores = (probs * product).astype(bf16)
            r.dq_total[:, qs] += dot(r.kv[plane * HEADS + a, 0:HDIM], grad_scores)
            dk = dot(r.query_rows[:, qs], grad_scores, 1, 1)
            dv = dot(r.grad_rows[:, qs], probs.astype(bf16), 1, 1)
            sums[:] = (dk, dv) if b == 0 else (sums[0] + dk, sums[1] + dv)
            if b == HEADS - 1:
                r.dkv_part[plane * HEADS + a] = jnp.concatenate(sums, axis=0).astype(bf16)

        pipelined(ahead, behind, depth, lambda: sum_parts(planes - 1 - k), 52)

    def plane_step(step, _):
        k = planes - 1 - step
        plane_of_keys(k)

        @pl.when(k >= 2)
        def next_weights():
            load_weights(r, k - 2).start()

        bit = 1
        while bit < planes:
            if 2 * bit < planes:

                @pl.when(jnp.logical_and(k > 0, lax.rem(k, 2 * bit) == 0))
                def add_part(bit=bit):
                    place.wait(r.dkv_got.at[0], r.dkv_sems.at[k + bit])
                    mine = part_of(r.dkv_part, place.plane(k), HEADS)
                    mine[...] = (
                        mine[...].astype(f32) + r.dkv_got[k + bit].astype(f32)
                    ).astype(bf16)

            @pl.when(lax.rem(k, 2 * bit) == bit)
            def send_part(bit=bit):
                place.copy(
                    part_of(r.dkv_part, place.plane(k), HEADS),
                    r.dkv_got.at[k],
                    r.dkv_sems.at[k],
                    bit * HEADS,
                ).start()

            bit *= 2

        return 0

    lax.fori_loop(0, planes, plane_step, 0)
    place.wait(r.x_all.at[pl.ds(0, HEADS - 1)], r.x_sems)
    dkv = part_of(r.dkv_part, place.z, HEADS)[...].astype(f32)
    bit = 1
    while bit < planes:
        place.wait(r.dkv_got.at[0], r.dkv_sems.at[bit])
        dkv = dkv + r.dkv_got[bit].astype(f32)
        bit *= 2
    for b in range(HEADS):
        r.back_send[b, 0:HDIM] = r.dq_total[:, b * cols : (b + 1) * cols].astype(bf16)
        r.back_send[b, HDIM : 3 * HDIM] = dkv[b].astype(bf16)
    place.to_plane(
        lambda spot: r.back_send.at[spot], r.back.at[place.p], r.back_sems
    )
    r.back[place.p] = r.back_send[place.p]
    total = dot(r.back_send[0], r.x_all[0])
    for b in range(1, HEADS):
        total = total + dot(r.back_send[b], r.x_all[b])
    r.heads_part[...] = total.astype(bf16)
    place.to_line(lambda spot: r.heads_part, lambda k: r.heads_got.at[k], r.heads_sems)
    halo_copies = edges_back(r, place)
    place.wait(r.heads_got.at[pl.ds(1, planes - 1)], r.heads_sems)
    total = r.heads_part[...].astype(f32) + total_of(r.heads_got, 1)
    r.heads[place.share] = total.astype(bf16)
    place.to_chips(
        lambda spot: r.heads.at[place.share],
        lambda k: r.heads.at[place.share],
        r.last_sems.at[0],
    )
    place.wait(r.back.at[pl.ds(0, HEADS - 1)], r.back_sems)
    grad = r.grad[...]
    for s, w in enumerate((r.wq, r.wk, r.wv)):
        part = jnp.concatenate(
            [r.back[h, HDIM * s : HDIM * (s + 1)] for h in range(HEADS)], axis=0
        )
        grad = grad + dot(part.T, w[...], 1, 1)
    place.wait(r.heads.at[pl.ds(0, HEADS // 2 - 1)], r.last_sems.at[0])
    own_half = part_of(r.heads, place.core, HEADS // 2)
    place.copy(own_half, own_half, r.last_sems.at[1], 1).start()
    wait_halo(place, *halo_copies)
    r.grad[...] = grad + r.edge_got[0].astype(f32) + r.edge_got[1].astype(f32)
    r.stores["grad"].start()
    place.wait(r.sums.at[pl.ds(0, HEADS // 2)], r.whole_sems.at[1])
    r.stores["sums"].start()
    place.wait(r.heads.at[pl.ds(0, HEADS // 2)], r.last_sems.at[1])
    r.stores["heads"].start()


def layer_kernel(count, cores, names, args, outs, *refs):
    r = Refs(names, refs)
    place = Place(count, cores)
    r.loads = {
        name: pltpu.make_async_copy(
            getattr(r, "from_" + name), getattr(r, name), r.load_sems.at[i]
        )
        for i, name in enumerate(args)
    }
    r.stores = {
        name: pltpu.make_async_copy(getattr(r, name), getattr(r, "to_" + name), r.store_sems.at[i])
        for i, name in enumerate(outs)
    }
    for load in r.loads.values():
        load.start()
    halo_copies = project(r, place)
    attend(r, place, 6, halo_copies)
    r.need("edge", "w1", "b1", "w2")
    r.need("up", "out_w", "f1", "fb", "f2", "g1", "g2", "b2", "g3", "b3")
    norms(r, place, halo_copies)
    attend_back(r, place, 6)
    for store in r.stores.values():
        store.wait()


def finish_kernel(names, outs, *refs):
    r = Refs(names, refs)
    width = r.grad.shape[1]
    moves = [
        pltpu.make_async_copy(r.from_sums, r.sums, r.load_sems.at[0]),
        pltpu.make_async_copy(r.from_heads, r.heads, r.load_sems.at[1]),
        pltpu.make_async_copy(r.from_vectors, r.vectors, r.load_sems.at[2]),
        pltpu.make_async_copy(r.from_result, r.result, r.load_sems.at[3]),
        pltpu.make_async_copy(r.from_grad, r.grad, r.load_sems.at[4]),
    ]
    for move in moves:
        move.start()
    stores = []

    def put(name, value):
        if value is not None:
            getattr(r, name)[...] = value
        stores.append(
            pltpu.make_async_copy(
                getattr(r, name), getattr(r, "to_" + name), r.store_sems.at[outs.index(name)]
            )
        )
        stores[-1].start()

    moves[0].wait()
    for k, name in enumerate(("gw1", "gw2", "ow")):
        put(name, r.sums[k * width : (k + 1) * width].astype(f32))
    r.f1[:, 0:width] = r.sums[3 * width : 4 * width].astype(f32)
    r.f1[:, width:] = r.sums[4 * width : 5 * width].astype(f32)
    put("f1", None)
    last = 5 * width + r.f2.shape[0]
    put("f2", r.sums[5 * width : last].astype(f32))
    rows_left = r.sums[last : last + 16].astype(f32)
    put("gb1", rows_left[0:1])
    put("fb", jnp.concatenate([rows_left[1:2], rows_left[2:3]], axis=1))
    moves[3].wait()
    put("result", None)
    moves[4].wait()
    put("grad", None)
    moves[1].wait()
    for s, name in enumerate(("qw", "kw", "vw")):
        cols = slice(HDIM * s, HDIM * (s + 1))
        spots = [h % 2 * (HEADS // 2) + h // 2 for h in range(HEADS)]
        total = jnp.concatenate([r.heads[spot, cols] for spot in spots], axis=0)
        put(name, total.T.astype(f32))
    moves[2].wait()
    for k, name in enumerate(("gain1", "gain2", "bias2", "gain3", "bias3")):
        put(name, r.vectors[k : k + 1])
    for store in stores:
        store.wait()


def on_device(
    count,
    cores,
    node_feat,
    edge_feat,
    edge_step,
    degree,
    graph_len,
    gine_w1,
    gine_b1,
    gine_w2,
    query_w,
    key_w,
    value_w,
    out_w,
    ffn_w1,
    ffn_b1,
    ffn_w2,
    norm1_gain,
    norm2_gain,
    norm2_bias,
    norm3_gain,
    norm3_bias,
    out_grad,
):
    rows, width = node_feat.shape
    ffn = ffn_w1.shape[1]
    planes = count // HEADS
    plane_rows = HEADS * rows
    vmem = pl.BlockSpec(memory_space=pltpu.VMEM)
    dma = pltpu.SemaphoreType.DMA
    shape = jax.ShapeDtypeStruct
    share_unit = 16 * HEADS * planes
    needed = 3 * width + 2 * ffn + 16
    part_rows = -(-needed // share_unit) * share_unit
    share = part_rows // HEADS

    def row(v):
        return v.reshape(1, -1)

    args = dict(
        x=node_feat,
        wk=key_w,
        wv=value_w,
        wq=query_w,
        step=edge_step.T,
        degree=row(degree),
        edge=edge_feat,
        w1=gine_w1,
        b1=row(gine_b1),
        w2=gine_w2,
        up=out_grad,
        out_w=out_w,
        f1=ffn_w1,
        fb=row(ffn_b1),
        f2=ffn_w2,
        g1=row(norm1_gain),
        g2=row(norm2_gain),
        b2=row(norm2_bias),
        g3=row(norm3_gain),
        b3=row(norm3_bias),
    )
    outs = dict(
        result=shape((rows, width), bf16),
        grad=shape((rows, width), f32),
        vectors=shape((8, width), f32),
        heads=shape((HEADS, 3 * HDIM, width), bf16),
        sums=shape((HEADS, share, width), bf16),
    )
    scratch = dict(
        ext=pltpu.VMEM((3 * rows, width), bf16),
        kv_send=pltpu.VMEM((HEADS, 2 * HDIM, rows), bf16),
        q_send=pltpu.VMEM((HEADS, HDIM, rows), bf16),
        kv=pltpu.VMEM((count, 2 * HDIM, rows), bf16),
        q=pltpu.VMEM((HEADS, HDIM, rows), bf16),
        columns=pltpu.VMEM((rows, 128), f32),
        slopes=pltpu.VMEM((EDGES, rows, width), f32),
        selects=pltpu.VMEM((EDGES, 3 * rows, rows), bf16),
        mixed=pltpu.VMEM((rows, width), bf16),
        active=pltpu.VMEM((rows, width), bf16),
        hidden_slope=pltpu.VMEM((rows, width), f32),
        res_one=pltpu.VMEM((rows, width), f32),
        grad_mixed=pltpu.VMEM((rows, width), f32),
        keys=pltpu.VMEM((plane_rows, 128), bf16),
        value_rows=pltpu.VMEM((HDIM + 16, plane_rows), bf16),
        values=pltpu.VMEM((plane_rows, 128), bf16),
        queries=pltpu.VMEM((128, plane_rows), bf16),
        grads=pltpu.VMEM((128, plane_rows), bf16),
        query_rows=pltpu.VMEM((HDIM, plane_rows), bf16),
        grad_rows=pltpu.VMEM((HDIM, plane_rows), bf16),
        factors=pltpu.VMEM((8, plane_rows), f32),
        kept=pltpu.VMEM((2, plane_rows, plane_rows), bf16),
        tops=pltpu.VMEM((planes, 8, plane_rows), f32),
        total=pltpu.VMEM((HDIM + 16, plane_rows), f32),
        top=pltpu.VMEM((8, plane_rows), f32),
        logs=pltpu.VMEM((8, plane_rows), f32),
        attended=pltpu.VMEM((HDIM, plane_rows), f32),
        att_send=pltpu.VMEM((HEADS, HDIM, rows), bf16),
        att_got=pltpu.VMEM((HEADS, HDIM, rows), bf16),
        do_send=pltpu.VMEM((HEADS, HDIM, rows), bf16),
        do=pltpu.VMEM((HEADS, HDIM, rows), bf16),
        stat0=pltpu.VMEM((count, 8, width // 2), f32),
        stat1=pltpu.VMEM((count, 8, width // 2), f32),
        stat2=pltpu.VMEM((count, 8, width // 2), f32),
        edge_send=pltpu.VMEM((2, rows, width), bf16),
        edge_got=pltpu.VMEM((2, rows, width), bf16),
        x_all=pltpu.VMEM((HEADS, rows, width), bf16),
        parts=pltpu.VMEM((part_rows, width), bf16),
        pair_got=pltpu.VMEM((part_rows // 2, width), bf16),
        pair_sum=pltpu.VMEM((part_rows // 2, width), bf16),
        chips_got=pltpu.VMEM((HEADS // 2, share, width), bf16),
        plane_sum=pltpu.VMEM((share, width), bf16),
        line_got=pltpu.VMEM((planes, share // planes, width), bf16),
        line_sum=pltpu.VMEM((planes, share // planes, width), bf16),
        dq_total=pltpu.VMEM((HDIM, plane_rows), f32),
        dkv_part=pltpu.VMEM((count, 2 * HDIM, rows), bf16),
        dkv_got=pltpu.VMEM((planes, HEADS, 2 * HDIM, rows), bf16),
        back_send=pltpu.VMEM((HEADS, 3 * HDIM, rows), bf16),
        back=pltpu.VMEM((HEADS, 3 * HDIM, rows), bf16),
        heads_part=pltpu.VMEM((3 * HDIM, width), bf16),
        heads_got=pltpu.VMEM((planes, 3 * HDIM, width), bf16),
        kv_sems=dma((planes, 2, 2)),
        halo_sems=dma((2, 4)),
        stat_sems=dma((3, 2)),
        line_sems=dma((2, 2)),
        dkv_sems=dma((planes, 2)),
        far_sems=dma((2, 2)),
        whole_sems=dma((2, 2)),
        last_sems=dma((2, 2)),
        **{
            name + "_sems": dma((2,))
            for name in ("q", "att", "do", "x", "pair", "parts", "back", "heads")
        },
    )
    scratch = dict(
        **{name: pltpu.VMEM(v.shape, v.dtype) for name, v in (args | outs).items()},
        **scratch,
        load_sems=dma((len(args),)),
        store_sems=dma((len(outs),)),
    )
    names = (
        "graph_len",
        *("from_" + name for name in args),
        *("to_" + name for name in outs),
        "far",
        *scratch,
    )
    anywhere = pl.BlockSpec(memory_space=pl.ANY)
    far = shape((planes - 2, plane_rows, plane_rows), bf16)
    result, grad, vectors, heads, sums, _ = pl.pallas_call(
        functools.partial(layer_kernel, count, cores, names, tuple(args), tuple(outs)),
        out_shape=(*outs.values(), far),
        in_specs=[pl.BlockSpec(memory_space=pltpu.SMEM)] + [anywhere] * len(args),
        out_specs=(anywhere,) * (len(outs) + 1),
        scratch_shapes=list(scratch.values()),
        compiler_params=pltpu.CompilerParams(
            vmem_limit_bytes=62 << 20, collective_id=1, has_side_effects=True
        ),
    )(graph_len, *args.values())

    square = shape((width, width), f32)
    line = shape((1, width), f32)
    ends = dict(
        result=shape((rows, width), bf16),
        grad=shape((rows, width), f32),
        gw1=square,
        gb1=line,
        gw2=square,
        qw=square,
        kw=square,
        vw=square,
        ow=square,
        f1=shape((width, ffn), f32),
        fb=shape((1, ffn), f32),
        f2=shape((ffn, width), f32),
        gain1=line,
        gain2=line,
        bias2=line,
        gain3=line,
        bias3=line,
    )
    parts = dict(
        sums=sums.reshape(part_rows, width),
        heads=heads,
        vectors=vectors,
        result=result,
        grad=grad,
    )
    scratch = dict(
        **{name: pltpu.VMEM(v.shape, v.dtype) for name, v in (parts | ends).items()},
        load_sems=dma((len(parts),)),
        store_sems=dma((len(ends),)),
    )
    names = (
        *("from_" + name for name in parts),
        *("to_" + name for name in ends),
        *scratch,
    )
    done = pl.pallas_call(
        functools.partial(finish_kernel, names, tuple(ends)),
        out_shape=tuple(ends.values()),
        in_specs=[anywhere] * len(parts),
        out_specs=(anywhere,) * len(ends),
        scratch_shapes=list(scratch.values()),
        compiler_params=pltpu.CompilerParams(vmem_limit_bytes=60 << 20),
    )(*parts.values())
    return tuple(v.reshape(-1) if v.shape[0] == 1 else v for v in done)


def solution(mesh):
    count = mesh.shape["blk"] * mesh.shape["rep"]
    rows = P(AXES, None)
    whole = P()
    return jax.shard_map(
        functools.partial(on_device, count, mesh.shape["rep"]),
        mesh=mesh,
        in_specs=(rows, P(AXES, None, None), rows, P(AXES)) + (whole,) * 16 + (rows,),
        out_specs=(rows, rows) + (whole,) * 15,
        check_vma=False,
    )
```
